32 devices in a mesh: groups: 2 (over x), ctx: 16 (over z, y, core).
Axes of the slice: x: 2, y: 2, z: 4, core: 2. Of those that a mesh axis runs over, the one named last changes fastest.
Arguments:
- queries: bfloat16 [2048, 2048], P('ctx', 'groups'), parts along dimension 1, may hold values from -25 to 25
- keys: bfloat16 [2048, 256], P('ctx', 'groups'), parts along dimension 1, may hold values from -6 to 6
- values: bfloat16 [2048, 256], P('ctx', 'groups'), parts along dimension 1, may hold values from -6 to 6
- d_out: bfloat16 [2048, 2048], P('ctx', 'groups'), parts along dimension 1, may hold values from -96 to 96
- mixer_input: bfloat16 [2048, 4096], P('ctx', 'groups'), parts along dimension 1, may hold values from -54 to 54
- gate_input: bfloat16 [2048, 4096], P('ctx', 'groups'), parts along dimension 1, may hold values from -6 to 6
- state_write: bfloat16 [2048, 512], P('ctx', 'groups'), parts along dimension 1, may hold values from -0.375 to 0.375
- state_read: bfloat16 [2048, 512], P('ctx', 'groups'), parts along dimension 1, may hold values from -0.375 to 0.375
- log_decay: float32 [2048, 64], P('ctx', 'groups'), parts along dimension 1, may hold values from -1 to 0
- norm_gain: float32 [4096], P('groups'), parts along dimension 0, may hold values from 0.25 to 1.75
- project_weight: bfloat16 [2048, 2560], P(None, 'groups'), parts along dimension 1, may hold values from -0.125 to 0.125
Outputs:
- input_gradient: float32 [2048, 4096], P('ctx', 'groups'), parts along dimension 1
- gate_gradient: float32 [2048, 4096], P('ctx', 'groups'), parts along dimension 1
- write_gradient: float32 [2048, 512], P('ctx', 'groups'), parts along dimension 1
- read_gradient: float32 [2048, 512], P('ctx', 'groups'), parts along dimension 1
The draws below stay inside these ranges and needn't reach their ends.
There are 2 independent parts, one for each index of `groups`. The reference program is written for one: setup_inputs(seed, part) draws one part's arguments, and reference() takes and returns one part's arrays. A program takes and returns all parts, laid end to end along the dimension named above; each array names one. Nothing has to cross between parts.
All inputs are finite; a program needn't handle non-finite values.
Results may differ from the reference program's by a relative error of at most 0.011.
Values may be sent and summed in bfloat16 or wider, within the bound.
No kernel may reach another device: no remote copies, remote signals or barrier semaphores. Data moves between devices by JAX's collectives and lax.ppermute only.
A program may use at most 192 MiB of HBM per device.

```python
import math
import jax
import jax.numpy as jnp
from jax import lax

TOK_DEV = 128
HEADS = 8
HEAD_DIM = 128
MHEADS = 32
MDIM = 64
NSTATE = 256
STRIDE = 16
WINDOW_TOKENS = 2048
CHANNELS = 2048
PROJECT = 1280


def draw_queries(key, part):
    value_key = jax.random.fold_in(key, 7002)
    base = jnp.clip(jax.random.normal(value_key, (WINDOW_TOKENS, HEADS * HEAD_DIM), jnp.float32), -6.0, 6.0)
    return base.astype(jnp.bfloat16)


def draw_keys(key, part):
    value_key = jax.random.fold_in(key, 7003)
    base = jnp.clip(jax.random.normal(value_key, (WINDOW_TOKENS, HEAD_DIM), jnp.float32), -6.0, 6.0)
    return base.astype(jnp.bfloat16)


def draw_mixer_input(key, part):
    row_key = jax.random.fold_in(key, 7101)
    column_key = jax.random.fold_in(key, 7102)
    value_key = jax.random.fold_in(key, 7103)
    row_scale = jnp.exp(jax.random.uniform(row_key, (WINDOW_TOKENS,), jnp.float32, minval=math.log(0.3), maxval=math.log(3.0)))
    base = jnp.clip(jax.random.normal(value_key, (WINDOW_TOKENS, CHANNELS), jnp.float32), -6.0, 6.0)
    column_scale = jnp.exp(jax.random.uniform(column_key, (CHANNELS,), jnp.float32, minval=math.log(0.3), maxval=math.log(3.0)))
    return (base * row_scale[:, None] * column_scale[None, :]).astype(jnp.bfloat16)


def draw_log_decay(key, part):
    pick_key = jax.random.fold_in(key, 7201)
    forgetful = jax.random.randint(pick_key, (MHEADS,), 0, 2) == 1
    fast_rate = jnp.exp(jax.random.uniform(jax.random.fold_in(key, 7202), (MHEADS,), jnp.float32, minval=math.log(1.0 / 50.0), maxval=math.log(1.0 / 30.0)))
    slow_rate = jnp.exp(jax.random.uniform(jax.random.fold_in(key, 7203), (MHEADS,), jnp.float32, minval=math.log(0.1), maxval=math.log(0.5))) / WINDOW_TOKENS
    head_rate = jnp.where(forgetful, fast_rate, slow_rate)
    device_factor = jnp.exp(jax.random.uniform(jax.random.fold_in(key, 7204), (STRIDE,), jnp.float32, minval=math.log(0.5), maxval=math.log(2.0)))
    every_row = jnp.arange(WINDOW_TOKENS)
    row_factor = device_factor[every_row // TOK_DEV]
    token_factor = jax.random.uniform(jax.random.fold_in(key, 7205), (WINDOW_TOKENS, MHEADS), jnp.float32, minval=0.5, maxval=1.5)
    decay_factor = -head_rate[None, :] * row_factor[:, None] * token_factor
    group_rows = jax.random.randint(jax.random.fold_in(key, 7206), (2,), 0, WINDOW_TOKENS)
    group_depth = jax.random.uniform(jax.random.fold_in(key, 7207), (2,), jnp.float32, minval=math.log(0.5), maxval=math.log(0.8))
    row_groups = jnp.sum(jnp.where(every_row[:, None] == group_rows[None, :], group_depth[None, :], 0.0), axis=1)
    return decay_factor + row_groups[:, None]


def shard_levels(stream_key, dims, pieces, smallest, top_value):
    def one(dim, parts):
        draws = jax.random.uniform(jax.random.fold_in(jax.random.fold_in(stream_key, 6), dim), (parts,), jnp.float32, smallest / len(pieces), top_value / len(pieces))
        return jnp.repeat(jnp.exp(draws), dims[dim] // parts).reshape((-1,) + (1,) * (len(dims) - dim - 1))

    factor_of = one(*pieces[0])
    for cut in pieces[1:]:
        factor_of = factor_of * one(*cut)
    return factor_of


def scatter_about(rng, shape, scale, bound, pieces=(), held_as=jnp.bfloat16):
    level = shard_levels(rng, shape, pieces, -0.22, 0.18) if pieces else 1.0
    array = jax.random.normal(rng, shape, jnp.float32) * scale * level
    return jnp.minimum(jnp.maximum(array, -bound), bound).astype(held_as)


def setup_inputs(seed: int = 0, part: int = 0) -> dict:
    seeds = jax.random.split(jax.random.key(seed), 12)
    own_keys = jax.random.split(jax.random.fold_in(seeds[11], part), 12)
    return {
        "queries": draw_queries(jax.random.fold_in(jax.random.fold_in(seeds[11], part), 71), part),
        "keys": draw_keys(jax.random.fold_in(jax.random.fold_in(seeds[11], part), 71), part),
        "values": scatter_about(own_keys[2], (WINDOW_TOKENS, HEAD_DIM), 1.0, 6.0, ((0, 16),)),
        "d_out": scatter_about(own_keys[3], (WINDOW_TOKENS, HEADS * HEAD_DIM), 16.0, 96.0, ((0, 16),)),
        "mixer_input": draw_mixer_input(jax.random.fold_in(jax.random.fold_in(seeds[11], part), 71), part),
        "gate_input": scatter_about(own_keys[5], (WINDOW_TOKENS, CHANNELS), 1.0, 6.0, ((0, 16),)),
        "state_write": scatter_about(own_keys[6], (WINDOW_TOKENS, NSTATE), NSTATE ** -0.5, 0.375, ((0, 16),)),
        "state_read": scatter_about(own_keys[7], (WINDOW_TOKENS, NSTATE), NSTATE ** -0.5, 0.375, ((0, 16),)),
        "log_decay": draw_log_decay(jax.random.fold_in(jax.random.fold_in(seeds[11], part), 71), part),
        "norm_gain": jnp.clip(1.0 + 0.15 * jax.random.normal(own_keys[9], (CHANNELS,), jnp.float32), 0.25, 1.75),
        "project_weight": scatter_about(own_keys[10], (CHANNELS, PROJECT), CHANNELS ** -0.5, 0.125),
    }


EPSILON = 1e-05
HIGHEST = lax.Precision.HIGHEST

def decay_parts(log_decay):
    cumulated = jnp.cumsum(log_decay, axis=0)
    length = cumulated.shape[0]
    causal_mask = (jnp.arange(length)[:, None] >= jnp.arange(length)[None, :])[None, :, :]
    spread = cumulated.T[:, :, None] - cumulated.T[:, None, :]
    decays = jnp.where(causal_mask, jnp.exp(jnp.where(causal_mask, spread, 0.0)), 0.0)
    remaining = jnp.exp(cumulated[-1][None, :] - cumulated)
    return (cumulated, decays, remaining)

def local_state(values_f, write_f, remaining):
    return jnp.einsum('shp,sn->hpn', values_f * remaining[:, :, None], write_f, precision=HIGHEST)

def block_output(weights, values_f, read_f, cumulated, incoming):
    within = jnp.einsum('hts,shp->thp', weights, values_f, precision=HIGHEST)
    carried = jnp.einsum('hpn,tn->thp', incoming, read_f, precision=HIGHEST)
    return within + jnp.exp(cumulated)[:, :, None] * carried

def local_adjoint(grads_f, read_f, cumulated):
    return jnp.einsum('thp,tn->hpn', grads_f * jnp.exp(cumulated)[:, :, None], read_f, precision=HIGHEST)

def block_grads(weights, decays, values_f, grads_f, write_f, read_f, cumulated, remaining, incoming, adjoint):
    value_grad = jnp.einsum('hts,thp->shp', weights, grads_f, precision=HIGHEST)
    value_grad = value_grad + remaining[:, :, None] * jnp.einsum('hpn,sn->shp', adjoint, write_f, precision=HIGHEST)
    pairs = jnp.einsum('thp,shp->hts', grads_f, values_f, precision=HIGHEST)
    pair_sum = lax.optimization_barrier(jnp.sum(decays * pairs, axis=0))
    read_grad = jnp.dot(pair_sum, write_f, precision=HIGHEST) + jnp.einsum('thp,hpn->tn', grads_f * jnp.exp(cumulated)[:, :, None], incoming, precision=HIGHEST)
    write_grad = jnp.dot(pair_sum.T, read_f, precision=HIGHEST) + jnp.einsum('shp,hpn->sn', values_f * remaining[:, :, None], adjoint, precision=HIGHEST)
    return (value_grad, write_grad, read_grad)

def gate_grads(mixer_out, gate_input, norm_gain, mixer_grad):
    gate_f = gate_input.astype(jnp.float32)
    sigmoid = jax.nn.sigmoid(gate_f)
    active = gate_f * sigmoid
    gated = mixer_out * active
    root_mean = jnp.sqrt(lax.optimization_barrier(jnp.mean(gated * gated, axis=-1, keepdims=True)) + EPSILON)
    scaled = norm_gain[None, :] * mixer_grad.astype(jnp.float32)
    gated_grad = scaled / root_mean - gated * lax.optimization_barrier(jnp.mean(scaled * gated, axis=-1, keepdims=True)) / root_mean ** 3
    gate_gradient = gated_grad * mixer_out * sigmoid * (1.0 + gate_f * (1.0 - sigmoid))
    out_grad = (gated_grad * active).astype(jnp.bfloat16)
    return (out_grad, gate_gradient)

def reference(queries, keys, values, d_out, mixer_input, gate_input, state_write, state_read, log_decay, norm_gain, project_weight):
    scale = 1.0 / math.sqrt(HEAD_DIM)
    every_row = jnp.arange(WINDOW_TOKENS, dtype=jnp.int32)
    position = every_row % TOK_DEV * STRIDE + every_row // TOK_DEV
    query_f = queries.astype(jnp.float32).reshape(WINDOW_TOKENS, HEADS, HEAD_DIM)
    grad_f = d_out.astype(jnp.float32).reshape(WINDOW_TOKENS, HEADS, HEAD_DIM)
    keys_f = keys.astype(jnp.float32)
    values_f = values.astype(jnp.float32)
    width = math.gcd(WINDOW_TOKENS, 512)
    count = WINDOW_TOKENS // width

    def query_block(carry, block_index):
        key_acc, value_acc = carry
        start = (block_index * width).astype(jnp.int32)
        query_part = lax.dynamic_slice_in_dim(query_f, start, width, 0)
        grad_part = lax.dynamic_slice_in_dim(grad_f, start, width, 0)
        place_part = lax.dynamic_slice_in_dim(position, start, width, 0)
        raw_scores = jnp.einsum('qhe,ke->qhk', query_part, keys_f) * scale
        visible = place_part[:, None, None] >= position[None, None, :]
        masked = jnp.where(visible, raw_scores, -jnp.inf)
        highest_score = lax.optimization_barrier(jnp.max(masked, axis=-1, keepdims=True))
        log_total = highest_score + jnp.log(lax.optimization_barrier(jnp.sum(jnp.exp(masked - highest_score), axis=-1, keepdims=True)))
        probs_f = jnp.exp(masked - log_total)
        probs_low = lax.optimization_barrier(probs_f.astype(jnp.bfloat16)).astype(jnp.float32)
        attention_out = jnp.einsum('qhk,kd->qhd', probs_low, values_f)
        delta = lax.optimization_barrier(jnp.sum(grad_part * attention_out, axis=-1, keepdims=True))
        prob_grad = jnp.einsum('qhd,kd->qhk', grad_part, values_f)
        score_grad = lax.optimization_barrier((probs_f * (prob_grad - delta)).astype(jnp.bfloat16)).astype(jnp.float32)
        query_grad = (jnp.einsum('qhk,ke->qhe', score_grad, keys_f) * scale).astype(jnp.bfloat16)
        key_acc = key_acc + jnp.einsum('qhk,qhe->ke', score_grad, query_part) * scale
        value_acc = value_acc + jnp.einsum('qhk,qhd->kd', probs_low, grad_part)
        return ((key_acc, value_acc), query_grad)
    empty_rows = jnp.zeros((WINDOW_TOKENS, HEAD_DIM), jnp.float32)
    (key_acc, value_acc), query_grads = lax.scan(query_block, (empty_rows, empty_rows), jnp.arange(count, dtype=jnp.int32))
    query_grads = query_grads.reshape(WINDOW_TOKENS, HEADS * HEAD_DIM)
    all_grads = jnp.concatenate([query_grads, key_acc.astype(jnp.bfloat16), value_acc.astype(jnp.bfloat16)], axis=1)
    attention_grad = jnp.dot(all_grads, project_weight.T, preferred_element_type=jnp.float32).astype(jnp.bfloat16)
    mixer_grad = attention_grad.reshape(STRIDE, TOK_DEV, CHANNELS).transpose(1, 0, 2).reshape(WINDOW_TOKENS, CHANNELS)
    input_blocks = mixer_input.reshape(STRIDE, TOK_DEV, CHANNELS)
    write_blocks = state_write.reshape(STRIDE, TOK_DEV, NSTATE)
    read_blocks = state_read.reshape(STRIDE, TOK_DEV, NSTATE)
    decay_blocks = log_decay.reshape(STRIDE, TOK_DEV, MHEADS)

    def forward_block(incoming, block):
        inputs_part, write_part, read_part, decay_part = block
        values_part = inputs_part.astype(jnp.float32).reshape(TOK_DEV, MHEADS, MDIM)
        write_f = write_part.astype(jnp.float32)
        read_f = read_part.astype(jnp.float32)
        cumulated, decays, remaining = decay_parts(decay_part)
        products = jnp.dot(read_part, write_part.T, preferred_element_type=jnp.float32)
        weights = decays * products[None, :, :]
        output = block_output(weights, values_part, read_f, cumulated, incoming)
        outgoing = jnp.exp(cumulated[-1])[:, None, None] * incoming + local_state(values_part, write_f, remaining)
        return (outgoing, (output.reshape(TOK_DEV, CHANNELS), incoming))
    start_state = jnp.zeros((MHEADS, MDIM, NSTATE), jnp.float32)
    _, (outputs, incomings) = lax.scan(forward_block, start_state, (input_blocks, write_blocks, read_blocks, decay_blocks))
    mixer_out = outputs.reshape(WINDOW_TOKENS, CHANNELS)
    out_grad, gate_gradient = gate_grads(mixer_out, gate_input, norm_gain, mixer_grad)

    def backward_block(adjoint, block):
        inputs_part, write_part, read_part, decay_part, grad_part, incoming = block
        values_part = inputs_part.astype(jnp.float32).reshape(TOK_DEV, MHEADS, MDIM)
        grads_part = grad_part.astype(jnp.float32).reshape(TOK_DEV, MHEADS, MDIM)
        write_f = write_part.astype(jnp.float32)
        read_f = read_part.astype(jnp.float32)
        cumulated, decays, remaining = decay_parts(decay_part)
        products = jnp.dot(read_part, write_part.T, preferred_element_type=jnp.float32)
        weights = decays * products[None, :, :]
        value_grad, write_grad, read_grad = block_grads(weights, decays, values_part, grads_part, write_f, read_f, cumulated, remaining, incoming, adjoint)
        outgoing = jnp.exp(cumulated[-1])[:, None, None] * adjoint + local_adjoint(grads_part, read_f, cumulated)
        return (outgoing, (value_grad.reshape(TOK_DEV, CHANNELS), write_grad, read_grad))
    grad_blocks = out_grad.reshape(STRIDE, TOK_DEV, CHANNELS)
    _, (value_grads, write_grads, read_grads) = lax.scan(backward_block, start_state, (input_blocks, write_blocks, read_blocks, decay_blocks, grad_blocks, incomings), reverse=True)
    return (value_grads.reshape(WINDOW_TOKENS, CHANNELS), gate_gradient, write_grads.reshape(WINDOW_TOKENS, NSTATE), read_grads.reshape(WINDOW_TOKENS, NSTATE))
```

```python
import functools
import math

import jax
import jax.numpy as jnp
from jax import lax
from jax.experimental import pallas as pl
from jax.experimental.pallas import tpu as pltpu
from jax.sharding import PartitionSpec as P

EPSILON = 1e-05
HIGHEST = lax.Precision.HIGHEST
F32 = jnp.float32
BF16 = jnp.bfloat16
EXTRA = 16
VMEM_LIMIT = 56 * 1024 * 1024


def nn(a, b, **kw):
    return lax.dot_general(a, b, (((1,), (0,)), ((), ())), preferred_element_type=F32, **kw)


def nt(a, b, **kw):
    return lax.dot_general(a, b, (((1,), (1,)), ((), ())), preferred_element_type=F32, **kw)


def tn(a, b, **kw):
    return lax.dot_general(a, b, (((0,), (0,)), ((), ())), preferred_element_type=F32, **kw)


def iota(shape, dim):
    return lax.broadcasted_iota(jnp.int32, shape, dim)


def call(kernel, outs, args, flops, smem=(), scratch=()):
    specs = [
        pl.BlockSpec(memory_space=pltpu.SMEM if i in smem else pltpu.VMEM) for i in range(len(args))
    ]
    moved = sum(a.size * a.dtype.itemsize for a in args) + sum(
        math.prod(o.shape) * o.dtype.itemsize for o in outs
    )
    return pl.pallas_call(
        kernel,
        out_shape=tuple(outs),
        in_specs=specs,
        out_specs=tuple(pl.BlockSpec(memory_space=pltpu.VMEM) for _ in outs),
        scratch_shapes=list(scratch),
        compiler_params=pltpu.CompilerParams(vmem_limit_bytes=VMEM_LIMIT),
        cost_estimate=pl.CostEstimate(flops=flops, bytes_accessed=moved, transcendentals=0),
    )(*args)


def struct(shape, dtype):
    return jax.ShapeDtypeStruct(shape, dtype)


def running_sums(log_decay):
    rows = log_decay.shape[0]
    lower = (iota((rows, rows), 0) >= iota((rows, rows), 1)).astype(F32)
    upper = (iota((rows, rows), 0) <= iota((rows, rows), 1)).astype(F32)
    return nn(lower, log_decay, precision=HIGHEST), tn(log_decay, upper, precision=HIGHEST)


def spread_heads(per_head, channels):
    heads = per_head.shape[1]
    mdim = channels // heads
    head, lane = iota((heads, channels), 0), iota((heads, channels), 1)
    pick = ((lane >= head * mdim) & (lane < (head + 1) * mdim)).astype(F32)
    return nn(per_head, pick, precision=HIGHEST)


def split_pair(block, mdim):
    first = iota(block.shape, 1) < mdim
    zero = jnp.zeros_like(block)
    return jnp.concatenate([jnp.where(first, block, zero), jnp.where(first, zero, block)], axis=0)


def pack_kernel(key_ref, value_ref, decay_ref, out_ref):
    rows, head_dim = key_ref.shape
    total = jnp.sum(decay_ref[...], axis=0, keepdims=True)
    heads = total.shape[1]
    high = total.astype(BF16).astype(F32)
    middle = (total - high).astype(BF16).astype(F32)
    low = (total - high - middle).astype(BF16).astype(F32)
    place = iota((EXTRA, heads), 0)
    split = jnp.where(place == 0, high, jnp.where(place == 1, middle, low))
    out_ref[0:rows, 0:head_dim] = key_ref[...]
    out_ref[0:rows, head_dim:] = value_ref[...]
    wide = jnp.concatenate([split, jnp.zeros((EXTRA, 2 * head_dim - heads), F32)], axis=1)
    out_ref[rows:, :] = wide.astype(BF16)


def state_kernel(input_ref, write_ref, decay_ref, state_ref):
    channels = input_ref.shape[1]
    cumulated, _ = running_sums(decay_ref[...])
    remaining = jnp.exp(cumulated[-1:, :] - cumulated)
    scaled = (input_ref[...].astype(F32) * spread_heads(remaining, channels)).astype(BF16)
    state_ref[...] = tn(scaled, write_ref[...]).astype(BF16)


def scan_kernel(reverse, mheads, factor_ref, part_ref, out_ref):
    count, here, nstate = part_ref.shape
    heads = factor_ref.shape[1]
    state = jnp.zeros((heads, here // heads, nstate), F32)
    order = range(count - 1, -1, -1) if reverse else range(count)
    for source in order:
        out_ref[source] = state.reshape(here, nstate).astype(BF16)
        factor = jnp.exp(factor_ref[source])[:, None, 0:1]
        part = part_ref[source].astype(F32).reshape(heads, here // heads, nstate)
        state = factor * state + part


def mixer_kernel(input_ref, write_ref, read_ref, decay_ref, incoming_ref, out_ref):
    rows, channels = input_ref.shape
    mheads = decay_ref.shape[1]
    mdim = channels // mheads
    cumulated, turned = running_sums(decay_ref[...])
    carried = nt(read_ref[...], incoming_ref[...])
    out_ref[...] = spread_heads(jnp.exp(cumulated), channels) * carried
    products = nt(read_ref[...], write_ref[...])
    causal = iota((rows, rows), 0) >= iota((rows, rows), 1)

    def weights_of(head):
        spread = cumulated[:, head : head + 1] - turned[head : head + 1, :]
        return (jnp.exp(jnp.where(causal, spread, -jnp.inf)) * products).astype(BF16)

    for pair in range(mheads // 2):
        lanes = slice(pair * 2 * mdim, (pair + 1) * 2 * mdim)
        weights = jnp.concatenate([weights_of(2 * pair), weights_of(2 * pair + 1)], axis=1)
        out_ref[:, lanes] += nn(weights, split_pair(input_ref[:, lanes], mdim))


def attention_kernel(
    in_kernel, me_ref, query_ref, grad_ref, gathered_ref, *rest
):
    if in_kernel:
        pack_ref, acc_ref, raw_ref, back_ref = rest
    else:
        query_out_ref, pack_ref, acc_ref, raw_ref, back_ref = rest
    rows = query_ref.shape[0]
    ctx_size = gathered_ref.shape[0]
    head_dim = gathered_ref.shape[2] // 2
    heads = query_ref.shape[1] // head_dim
    me = me_ref[0]
    scale = 1.0 / math.sqrt(head_dim)
    base2 = scale * math.log2(math.e)
    tile = min(32, rows)
    tiles = rows // tile
    wide = heads * tile
    per = rows // ctx_size

    def keys_of(b):
        return gathered_ref[:, b * tile : (b + 1) * tile, 0:head_dim].reshape(
            ctx_size * tile, head_dim
        )

    def values_of(b):
        return gathered_ref[:, b * tile : (b + 1) * tile, head_dim : 2 * head_dim].reshape(
            ctx_size * tile, head_dim
        )

    def stacked(ref, t):
        parts = [
            ref[t * tile : (t + 1) * tile, h * head_dim : (h + 1) * head_dim] for h in range(heads)
        ]
        return jnp.concatenate(parts, axis=0)

    key_row = iota((ctx_size * tile, wide), 0)
    key_place = (key_row % tile) * ctx_size + key_row // tile
    query_place = (iota((ctx_size * tile, wide), 1) % tile) * ctx_size + me
    visible = key_place <= query_place

    for t in range(tiles - 1, -1, -1):
        query = stacked(query_ref, t)
        grad = stacked(grad_ref, t)
        highest = None
        for b in range(t, -1, -1):
            raw = nt(keys_of(b), query)
            if b == t:
                raw = jnp.where(visible, raw, -jnp.inf)
            raw_ref[b] = raw
            block_high = jnp.max(raw, axis=0, keepdims=True)
            highest = block_high if highest is None else jnp.maximum(highest, block_high)
        total = jnp.zeros((1, wide), F32)
        delta = jnp.zeros((1, wide), F32)
        for b in range(t + 1):
            probs = jnp.exp2((raw_ref[b] - highest) * base2)
            back = nt(values_of(b), grad)
            raw_ref[b] = probs
            back_ref[b] = back
            total = total + jnp.sum(probs, axis=0, keepdims=True)
            delta = delta + jnp.sum(probs * back, axis=0, keepdims=True)
        inverse = 1.0 / total
        delta = delta * inverse
        query_grad = jnp.zeros((head_dim, wide), F32)
        for b in range(t + 1):
            weights = raw_ref[b] * inverse
            score_grad = (weights * (back_ref[b] - delta)).astype(BF16)
            value_part = nn(weights.astype(BF16), grad).reshape(ctx_size, tile, head_dim)
            key_part = nn(score_grad, query).reshape(ctx_size, tile, head_dim)
            here = slice(b * tile, (b + 1) * tile)
            if t == tiles - 1:
                acc_ref[:, here, 0:head_dim] = key_part
                acc_ref[:, here, head_dim:] = value_part
            else:
                acc_ref[:, here, 0:head_dim] += key_part
                acc_ref[:, here, head_dim:] += value_part
            query_grad = query_grad + tn(keys_of(b), score_grad)
        turned = (query_grad * scale).T
        by_head = [turned[h * tile : (h + 1) * tile, :] for h in range(heads)]
        if in_kernel:
            pairs = [
                jnp.concatenate(by_head[h : h + 2], axis=1) for h in range(0, heads, 2)
            ]
            for k in range(tile // per):
                rows_here = [p[k * per : (k + 1) * per, :] for p in pairs]
                pack_ref[t * (tile // per) + k, rows:, :] = jnp.concatenate(
                    rows_here, axis=0
                ).astype(BF16)
        else:
            for h in range(heads):
                query_out_ref[t * tile : (t + 1) * tile, h * head_dim : (h + 1) * head_dim] = (
                    by_head[h].astype(BF16)
                )

    both = jnp.where(iota((1, 1, 2 * head_dim), 2) < head_dim, scale, 1.0)
    if in_kernel:
        for target in range(ctx_size):
            block = acc_ref[:, target * per : (target + 1) * per, :] * both
            pack_ref[target, 0:rows, :] = block.reshape(rows, 2 * head_dim).astype(BF16)
    else:
        pack_ref[...] = (acc_ref[...] * both).astype(BF16)


def gate_kernel(
    received_ref,
    weight_ref,
    mixer_ref,
    gate_ref,
    gain_ref,
    read_ref,
    decay_ref,
    gate_out_ref,
    grad_out_ref,
    adjoint_ref,
):
    ctx_size = received_ref.shape[0]
    rows, channels = mixer_ref.shape
    wide = received_ref.shape[2]
    per = rows // ctx_size
    sums = received_ref[0, 0:rows, :].astype(F32)
    for source in range(1, ctx_size):
        sums = sums + received_ref[source, 0:rows, :].astype(F32)
    extra = received_ref.shape[1] - rows
    query_rows = received_ref[:, rows:, :].astype(F32)
    columns = []
    for part in range(extra // per):
        block = query_rows[:, part * per : (part + 1) * per, :]
        columns.append(block.reshape(rows, wide))
    columns.append(sums)
    grads = jnp.concatenate(columns, axis=1).astype(BF16)
    token = iota((rows, rows), 0)
    came = iota((rows, rows), 1)
    order = (token == (came % per) * ctx_size + came // per).astype(BF16)
    grads = nn(order, grads).astype(BF16)
    mixer_grad = nt(grads, weight_ref[...]).astype(BF16).astype(F32)

    mixer_out = mixer_ref[...]
    gate = gate_ref[...].astype(F32)
    sigmoid = jax.nn.sigmoid(gate)
    active = gate * sigmoid
    gated = mixer_out * active
    inverse = lax.rsqrt(jnp.mean(gated * gated, axis=-1, keepdims=True) + EPSILON)
    scaled = gain_ref[...] * mixer_grad
    mean = jnp.mean(scaled * gated, axis=-1, keepdims=True)
    gated_grad = scaled * inverse - gated * (mean * inverse * inverse * inverse)
    gate_out_ref[...] = gated_grad * mixer_out * sigmoid * (1.0 + gate * (1.0 - sigmoid))
    out_grad = (gated_grad * active).astype(BF16)
    grad_out_ref[...] = out_grad
    cumulated, _ = running_sums(decay_ref[...])
    grown = (out_grad.astype(F32) * spread_heads(jnp.exp(cumulated), channels)).astype(BF16)
    adjoint_ref[...] = tn(grown, read_ref[...]).astype(BF16)


def local_kernel(
    grad_ref, input_ref, write_ref, read_ref, decay_ref, incoming_ref, value_ref, write_out_ref, read_out_ref
):
    rows, channels = input_ref.shape
    mheads = decay_ref.shape[1]
    mdim = channels // mheads
    cumulated, turned = running_sums(decay_ref[...])
    turned_products = nt(write_ref[...], read_ref[...])
    causal = iota((rows, rows), 0) >= iota((rows, rows), 1)
    later = iota((rows, rows), 0) <= iota((rows, rows), 1)
    pair_sum = jnp.zeros((rows, rows), F32)

    def decays_of(head):
        spread = cumulated[:, head : head + 1] - turned[head : head + 1, :]
        return jnp.exp(jnp.where(causal, spread, -jnp.inf))

    def turned_weights_of(head):
        spread = turned[head : head + 1, :] - cumulated[:, head : head + 1]
        return (jnp.exp(jnp.where(later, spread, -jnp.inf)) * turned_products).astype(BF16)

    for pair in range(mheads // 2):
        lanes = slice(pair * 2 * mdim, (pair + 1) * 2 * mdim)
        grads = split_pair(grad_ref[:, lanes], mdim)
        weights = jnp.concatenate(
            [turned_weights_of(2 * pair), turned_weights_of(2 * pair + 1)], axis=1
        )
        value_ref[:, lanes] = nn(weights, grads)
        pairs = nt(grads, input_ref[:, lanes])
        pair_sum = (
            pair_sum + decays_of(2 * pair) * pairs[:rows] + decays_of(2 * pair + 1) * pairs[rows:]
        )
    pair_low = pair_sum.astype(BF16)
    grown = (grad_ref[...].astype(F32) * spread_heads(jnp.exp(cumulated), channels)).astype(BF16)
    read_out_ref[...] = nn(pair_low, write_ref[...]) + nn(grown, incoming_ref[...])
    write_out_ref[...] = tn(pair_low, read_ref[...])


def final_kernel(
    value_ref, write_part_ref, adjoint_ref, input_ref, write_ref, decay_ref, out_ref, write_out_ref
):
    channels = input_ref.shape[1]
    cumulated, _ = running_sums(decay_ref[...])
    remaining = spread_heads(jnp.exp(cumulated[-1:, :] - cumulated), channels)
    out_ref[...] = value_ref[...] + remaining * nt(write_ref[...], adjoint_ref[...])
    scaled = (input_ref[...].astype(F32) * remaining).astype(BF16)
    write_out_ref[...] = write_part_ref[...] + nn(scaled, adjoint_ref[...])


def scanned(part, factors, reverse):
    ctx_size = lax.axis_size("ctx")
    channels, nstate = part.shape
    here = channels // ctx_size
    mine = lax.all_to_all(
        part.reshape(ctx_size, here, nstate), "ctx", split_axis=0, concat_axis=0, tiled=True
    )
    (out,) = call(
        functools.partial(scan_kernel, reverse, factors.shape[1]),
        [struct((ctx_size, here, nstate), BF16)],
        [factors, mine],
        ctx_size * here * nstate * 2,
    )
    back = lax.all_to_all(out, "ctx", split_axis=0, concat_axis=0, tiled=True)
    return back.reshape(channels, nstate)


def body(
    queries,
    keys,
    values,
    d_out,
    mixer_input,
    gate_input,
    state_write,
    state_read,
    log_decay,
    norm_gain,
    project_weight,
):
    ctx_size = lax.axis_size("ctx")
    ctx_index = lax.axis_index("ctx")
    rows, head_dim = keys.shape
    wide = queries.shape[1]
    channels = mixer_input.shape[1]
    nstate = state_write.shape[1]
    mheads = log_decay.shape[1]
    per = rows // ctx_size

    (packed,) = call(
        pack_kernel,
        [struct((rows + EXTRA, 2 * head_dim), BF16)],
        [keys, values, log_decay],
        rows * mheads,
    )
    gathered = lax.all_gather(packed, "ctx", axis=0, tiled=False)
    (own_state,) = call(
        state_kernel,
        [struct((channels, nstate), BF16)],
        [mixer_input, state_write, log_decay],
        2 * rows * channels * nstate,
    )

    splits = gathered[:, rows : rows + 3, 0:mheads].astype(F32)
    totals = splits[:, 0] + splits[:, 1] + splits[:, 2]
    own_heads = mheads // ctx_size
    factors = lax.dynamic_slice_in_dim(totals, ctx_index * own_heads, own_heads, 1)
    factors = jnp.broadcast_to(factors[:, :, None], (ctx_size, own_heads, 128))
    incoming = scanned(own_state, factors, False)

    in_kernel = per % 8 == 0
    extra = per * wide // (2 * head_dim)
    me = ctx_index.astype(jnp.int32).reshape(1)
    flops = 10 * rows * wide * ctx_size * rows
    tile = min(32, rows)
    columns = tile * wide // head_dim
    scratch = [
        pltpu.VMEM((ctx_size, rows, 2 * head_dim), F32),
        pltpu.VMEM((rows // tile, ctx_size * tile, columns), F32),
        pltpu.VMEM((rows // tile, ctx_size * tile, columns), F32),
    ]
    if in_kernel:
        (sent,) = call(
            functools.partial(attention_kernel, True),
            [struct((ctx_size, rows + extra, 2 * head_dim), BF16)],
            [me, queries, d_out, gathered],
            flops,
            smem=(0,),
            scratch=scratch,
        )
    else:
        query_grad, kv_grad = call(
            functools.partial(attention_kernel, False),
            [struct((rows, wide), BF16), struct((ctx_size, rows, 2 * head_dim), BF16)],
            [me, queries, d_out, gathered],
            flops,
            smem=(0,),
            scratch=scratch,
        )
        by_target = kv_grad.reshape(ctx_size, ctx_size, per, 2 * head_dim).transpose(1, 0, 2, 3)
        by_pair = query_grad.reshape(ctx_size, per, -1, 2 * head_dim).transpose(0, 2, 1, 3)
        sent = jnp.concatenate(
            [
                by_target.reshape(ctx_size, rows, 2 * head_dim),
                by_pair.reshape(ctx_size, extra, 2 * head_dim),
            ],
            axis=1,
        )
    received = lax.all_to_all(sent, "ctx", split_axis=0, concat_axis=0, tiled=True)

    (mixer_out,) = call(
        mixer_kernel,
        [struct((rows, channels), F32)],
        [mixer_input, state_write, state_read, log_decay, incoming],
        2 * rows * channels * (nstate + rows),
    )
    gate_gradient, out_grad, own_adjoint = call(
        gate_kernel,
        [
            struct((rows, channels), F32),
            struct((rows, channels), BF16),
            struct((channels, nstate), BF16),
        ],
        [
            received,
            project_weight,
            mixer_out,
            gate_input,
            norm_gain.reshape(1, channels),
            state_read,
            log_decay,
        ],
        2 * rows * channels * (nstate + project_weight.shape[1]),
    )
    adjoint = scanned(own_adjoint, factors, True)
    value_part, write_part, read_gradient = call(
        local_kernel,
        [
            struct((rows, channels), F32),
            struct((rows, nstate), F32),
            struct((rows, nstate), F32),
        ],
        [out_grad, mixer_input, state_write, state_read, log_decay, incoming],
        2 * rows * channels * (nstate + 2 * rows),
    )
    input_gradient, write_gradient = call(
        final_kernel,
        [struct((rows, channels), F32), struct((rows, nstate), F32)],
        [value_part, write_part, adjoint, mixer_input, state_write, log_decay],
        4 * rows * channels * nstate,
    )
    return (input_gradient, gate_gradient, write_gradient, read_gradient)


def solution(mesh):
    both = P("ctx", "groups")
    return jax.shard_map(
        body,
        mesh=mesh,
        in_specs=(both,) * 9 + (P("groups"), P(None, "groups")),
        out_specs=(both,) * 4,
        check_vma=False,
    )
```

```python
import functools
import math

import jax
import jax.numpy as jnp
from jax import lax
from jax.experimental import pallas as pl
from jax.experimental.pallas import tpu as pltpu
from jax.sharding import PartitionSpec as P

EPSILON = 1e-05
HIGHEST = lax.Precision.HIGHEST
F32 = jnp.float32
BF16 = jnp.bfloat16
EXTRA = 16
MIB = 1024 * 1024


def nn(a, b, **kw):
    return lax.dot_general(a, b, (((1,), (0,)), ((), ())), preferred_element_type=F32, **kw)


def nt(a, b, **kw):
    return lax.dot_general(a, b, (((1,), (1,)), ((), ())), preferred_element_type=F32, **kw)


def tn(a, b, **kw):
    return lax.dot_general(a, b, (((0,), (0,)), ((), ())), preferred_element_type=F32, **kw)


def iota(shape, dim):
    return lax.broadcasted_iota(jnp.int32, shape, dim)


def call(kernel, outs, args, flops, smem=(), scratch=(), spare=4 * MIB):
    specs = [
        pl.BlockSpec(memory_space=pltpu.SMEM if i in smem else pltpu.VMEM) for i in range(len(args))
    ]
    moved = sum(a.size * a.dtype.itemsize for a in args) + sum(
        math.prod(o.shape) * o.dtype.itemsize for o in outs
    )
    held = moved + sum(math.prod(s.shape) * jnp.dtype(s.dtype).itemsize for s in scratch)
    return pl.pallas_call(
        kernel,
        out_shape=tuple(outs),
        in_specs=specs,
        out_specs=tuple(pl.BlockSpec(memory_space=pltpu.VMEM) for _ in outs),
        scratch_shapes=list(scratch),
        compiler_params=pltpu.CompilerParams(vmem_limit_bytes=held + spare),
        cost_estimate=pl.CostEstimate(flops=flops, bytes_accessed=moved, transcendentals=0),
    )(*args)


def struct(shape, dtype):
    return jax.ShapeDtypeStruct(shape, dtype)


def running_sums(log_decay):
    rows = log_decay.shape[1]
    lower = (iota((rows, rows), 0) >= iota((rows, rows), 1)).astype(F32)
    upper = (iota((rows, rows), 0) <= iota((rows, rows), 1)).astype(F32)
    return nt(lower, log_decay, precision=HIGHEST), nn(log_decay, upper, precision=HIGHEST)


def spread_heads(per_head, mdim):
    rows, heads = per_head.shape
    first = iota((rows, 2 * mdim), 1) < mdim
    pairs = [
        jnp.where(first, per_head[:, h : h + 1], per_head[:, h + 1 : h + 2])
        for h in range(0, heads, 2)
    ]
    return jnp.concatenate(pairs, axis=1)


def split_pair(block, mdim):
    first = iota(block.shape, 1) < mdim
    zero = jnp.zeros_like(block)
    return jnp.concatenate([jnp.where(first, block, zero), jnp.where(first, zero, block)], axis=0)


def pack_kernel(key_ref, value_ref, out_ref):
    head_dim = key_ref.shape[1]
    out_ref[:, 0:head_dim] = key_ref[...]
    out_ref[:, head_dim:] = value_ref[...]


def tile_of(rows):
    return min(32, rows)


def stack_heads(ref, out_ref):
    tiles, wide, head_dim = out_ref.shape
    tile = ref.shape[0] // tiles
    for t in range(tiles):
        for h in range(wide // tile):
            out_ref[t, h * tile : (h + 1) * tile, :] = ref[
                t * tile : (t + 1) * tile, h * head_dim : (h + 1) * head_dim
            ]


def put_logs(ref, logs):
    heads = logs.shape[1]
    high = logs.astype(BF16).astype(F32)
    middle = (logs - high).astype(BF16).astype(F32)
    low = (logs - high - middle).astype(BF16).astype(F32)
    place = iota((EXTRA, heads), 0)
    split = jnp.where(place == 0, high, jnp.where(place == 1, middle, low))
    wide = jnp.concatenate([split, jnp.zeros((EXTRA, ref.shape[1] - heads), F32)], axis=1)
    ref[ref.shape[0] - EXTRA :, :] = wide.astype(BF16)


def get_logs(ref, heads):
    parts = ref[ref.shape[0] - EXTRA :, 0:heads].astype(F32)
    return parts[0:1, :] + parts[1:2, :] + parts[2:3, :]


def times(logs, start, mdim, state):
    head = iota(logs.shape, 1)
    blocks = []
    for i in range(state.shape[0] // mdim):
        log = jnp.sum(jnp.where(head == start + i, logs, 0.0), axis=1, keepdims=True)
        blocks.append(jnp.exp(log) * state[i * mdim : (i + 1) * mdim, :])
    return jnp.concatenate(blocks, axis=0)


def write_halves(core, logs, scaled_ref, other_ref, keep_ref, give_ref):
    half = keep_ref.shape[0]
    for out_ref, which in ((keep_ref, core), (give_ref, 1 - core)):
        lanes = pl.ds(pl.multiple_of(which * half, half), half)
        out_ref[0:half, :] = tn(scaled_ref[:, lanes], other_ref[...]).astype(BF16)
    put_logs(give_ref, logs)


def state_kernel(
    me_ref,
    input_ref,
    write_ref,
    decay_ref,
    query_ref,
    grad_ref,
    keep_ref,
    give_ref,
    scaled_ref,
    remain_ref,
    grow_ref,
    sum_ref,
    turned_ref,
    query_out_ref,
    grad_out_ref,
):
    cumulated, turned = running_sums(decay_ref[...])
    sum_ref[...], turned_ref[...] = cumulated, turned
    mdim = input_ref.shape[1] // cumulated.shape[1]
    last = cumulated[-1:, :]
    remain_ref[...] = spread_heads(jnp.exp(last - cumulated), mdim)
    grow_ref[...] = spread_heads(jnp.exp(cumulated), mdim)
    scaled_ref[...] = (input_ref[...].astype(F32) * remain_ref[...]).astype(BF16)
    write_halves(me_ref[0] % 2, last, scaled_ref, write_ref, keep_ref, give_ref)
    stack_heads(query_ref, query_out_ref)
    stack_heads(grad_ref, grad_out_ref)


def chip_kernel(reverse, me_ref, sum_ref, keep_ref, got_ref, *rest):
    *out_refs, total_ref = rest
    heads = sum_ref.shape[1]
    half = keep_ref.shape[0]
    mdim = 2 * half // heads
    core = me_ref[0] % 2
    chip = me_ref[0] // 2 % len(out_refs)
    slice_rows = out_refs[0].shape[0] - EXTRA
    own_logs = sum_ref[sum_ref.shape[0] - 1 :, :]
    got_logs = get_logs(got_ref, heads)
    keep, got = keep_ref[...].astype(F32), got_ref[0:half, :].astype(F32)
    first = core == (1 if reverse else 0)
    decayed = times(jnp.where(first, got_logs, own_logs), core * heads // 2, mdim, jnp.where(first, keep, got))
    total_ref[...] = decayed + jnp.where(first, got, keep)
    for k, out_ref in enumerate(out_refs):
        start = pl.multiple_of((chip ^ k) * slice_rows, slice_rows)
        out_ref[0:slice_rows, :] = total_ref[pl.ds(start, slice_rows), :].astype(BF16)
        put_logs(out_ref, own_logs + got_logs)


def steps(count, reverse):
    return range(count - 1, -1, -1) if reverse else range(count)


def ordered(chip, part_refs, order_ref):
    for k, part_ref in enumerate(part_refs):
        order_ref[chip ^ k] = part_ref[...]


def advance(order_ref, source, start, heads, mdim, state):
    part_ref = order_ref.at[source]
    rows = state.shape[0]
    return times(get_logs(part_ref, heads), start, mdim, state) + part_ref[0:rows, :].astype(F32)


def total_kernel(reverse, heads, mdim, me_ref, *rest):
    *part_refs, out_ref, order_ref = rest
    count = len(part_refs)
    chip = me_ref[0] // 2 % count
    ordered(chip, part_refs, order_ref)
    start = me_ref[0] % 2 * (heads // 2) + chip * (heads // 2 // count)
    state = jnp.zeros(out_ref.shape, F32)
    for source in steps(count, reverse):
        state = advance(order_ref, source, start, heads, mdim, state)
    out_ref[...] = state.astype(BF16)


def scan_kernel(reverse, heads, mdim, me_ref, carry_ref, *rest):
    *refs, order_ref, result_ref = rest
    count = len(refs) // 2
    chip = me_ref[0] // 2 % count
    ordered(chip, refs[:count], order_ref)
    start = me_ref[0] % 2 * (heads // 2) + chip * (heads // 2 // count)
    state = carry_ref[...].astype(F32)
    for source in steps(count, reverse):
        result_ref[source] = state.astype(BF16)
        state = advance(order_ref, source, start, heads, mdim, state)
    for k, out_ref in enumerate(refs[count:]):
        out_ref[...] = result_ref[chip ^ k]


def core_kernel(reverse, me_ref, sum_ref, keep_ref, got_ref, *rest):
    *part_refs, mine_ref, send_ref, order_ref = rest
    count = len(part_refs)
    heads = sum_ref.shape[1]
    half = keep_ref.shape[0]
    core = me_ref[0] % 2
    chip = me_ref[0] // 2 % count
    slice_rows = part_refs[0].shape[0]
    for k, part_ref in enumerate(part_refs):
        start = pl.multiple_of((chip ^ k) * slice_rows, slice_rows)
        order_ref[pl.ds(start, slice_rows), :] = part_ref[...]
    first = core == (1 if reverse else 0)
    logs = jnp.where(first, sum_ref[sum_ref.shape[0] - 1 :, :], get_logs(got_ref, heads))
    own = jnp.where(first, keep_ref[...].astype(F32), got_ref[0:half, :].astype(F32))
    incoming = order_ref[...].astype(F32)
    passed = times(logs, core * heads // 2, 2 * half // heads, incoming) + own
    mine_ref[...] = jnp.where(first, incoming, passed).astype(BF16)
    send_ref[...] = jnp.where(first, passed, incoming).astype(BF16)


def whole_state(me_ref, mine_ref, other_ref, both_ref):
    core = me_ref[0] % 2
    both_ref[core] = mine_ref[...]
    both_ref[1 - core] = other_ref[...]
    _, half, nstate = both_ref.shape
    return both_ref[...].reshape(2 * half, nstate)


def mixer_kernel(
    me_ref,
    input_ref,
    write_ref,
    read_ref,
    sum_ref,
    turned_ref,
    grow_ref,
    mine_ref,
    other_ref,
    out_ref,
    both_ref,
):
    rows, channels = input_ref.shape
    mheads = sum_ref.shape[1]
    mdim = channels // mheads
    cumulated, turned = sum_ref[...], turned_ref[...]
    carried = nt(read_ref[...], whole_state(me_ref, mine_ref, other_ref, both_ref))
    out_ref[...] = grow_ref[...] * carried
    products = nt(read_ref[...], write_ref[...])
    causal = iota((rows, rows), 0) >= iota((rows, rows), 1)

    def weights_of(head):
        spread = cumulated[:, head : head + 1] - turned[head : head + 1, :]
        return (jnp.exp(jnp.where(causal, spread, -jnp.inf)) * products).astype(BF16)

    for pair in range(mheads // 2):
        lanes = slice(pair * 2 * mdim, (pair + 1) * 2 * mdim)
        weights = jnp.concatenate([weights_of(2 * pair), weights_of(2 * pair + 1)], axis=1)
        out_ref[:, lanes] += nn(weights, split_pair(input_ref[:, lanes], mdim))


def attention_kernel(
    in_kernel, ctx_size, me_ref, query_ref, grad_ref, *rest
):
    piece_refs, rest = rest[:ctx_size], rest[ctx_size:]
    query_out_ref, *out_refs, gathered_ref, acc_ref, raw_ref, back_ref = rest
    tiles, wide, head_dim = query_ref.shape
    rows = gathered_ref.shape[1]
    tile = rows // tiles
    heads = wide // tile
    me = me_ref[0]
    scale = 1.0 / math.sqrt(head_dim)
    base2 = scale * math.log2(math.e)
    per = rows // ctx_size
    for offset, piece_ref in enumerate(piece_refs):
        gathered_ref[me ^ offset] = piece_ref[...]

    def keys_of(b):
        return gathered_ref[:, b * tile : (b + 1) * tile, 0:head_dim].reshape(
            ctx_size * tile, head_dim
        )

    def values_of(b):
        return gathered_ref[:, b * tile : (b + 1) * tile, head_dim : 2 * head_dim].reshape(
            ctx_size * tile, head_dim
        )

    key_row = iota((ctx_size * tile, wide), 0)
    key_place = (key_row % tile) * ctx_size + key_row // tile
    query_place = (iota((ctx_size * tile, wide), 1) % tile) * ctx_size + me
    visible = key_place <= query_place

    for t in range(tiles - 1, -1, -1):
        query = query_ref[t]
        grad = grad_ref[t]
        highest = None
        for b in range(t, -1, -1):
            raw = nt(keys_of(b), query)
            if b == t:
                raw = jnp.where(visible, raw, -jnp.inf)
            raw_ref[b] = raw
            block_high = jnp.max(raw, axis=0, keepdims=True)
            highest = block_high if highest is None else jnp.maximum(highest, block_high)
        total = jnp.zeros((1, wide), F32)
        delta = jnp.zeros((1, wide), F32)
        for b in range(t + 1):
            probs = jnp.exp2((raw_ref[b] - highest) * base2)
            back = nt(values_of(b), grad)
            raw_ref[b] = probs
            back_ref[b] = back
            total = total + jnp.sum(probs, axis=0, keepdims=True)
            delta = delta + jnp.sum(probs * back, axis=0, keepdims=True)
        inverse = 1.0 / total
        delta = delta * inverse
        query_grad = jnp.zeros((head_dim, wide), F32)
        for b in range(t + 1):
            weights = raw_ref[b] * inverse
            score_grad = (weights * (back_ref[b] - delta)).astype(BF16)
            value_part = nn(weights.astype(BF16), grad).reshape(ctx_size, tile, head_dim)
            key_part = nn(score_grad, query).reshape(ctx_size, tile, head_dim)
            here = slice(b * tile, (b + 1) * tile)
            if t == tiles - 1:
                acc_ref[:, here, 0:head_dim] = key_part
                acc_ref[:, here, head_dim:] = value_part
            else:
                acc_ref[:, here, 0:head_dim] += key_part
                acc_ref[:, here, head_dim:] += value_part
            query_grad = query_grad + tn(keys_of(b), score_grad)
        turned = (query_grad * scale).T
        by_head = [turned[h * tile : (h + 1) * tile, :] for h in range(heads)]
        for h in range(heads):
            query_out_ref[t * tile : (t + 1) * tile, h * head_dim : (h + 1) * head_dim] = (
                by_head[h].astype(BF16)
            )

    both = jnp.where(iota((1, 1, 2 * head_dim), 2) < head_dim, scale, 1.0)
    if in_kernel:
        keep_ref, give_ref = out_refs
        for chip in range(ctx_size // 2):
            for out_ref, core in ((keep_ref, me % 2), (give_ref, 1 - me % 2)):
                start = pl.multiple_of((2 * chip + core) * per, per)
                block = acc_ref[:, pl.ds(start, per), :] * both
                out_ref[chip] = block.reshape(rows, 2 * head_dim).astype(BF16)
    else:
        (pack_ref,) = out_refs
        pack_ref[...] = (acc_ref[...] * both).astype(BF16)


def join_kernel(me_ref, keep_ref, got_ref, near_ref, far_ref):
    chips = keep_ref.shape[0]
    chip = me_ref[0] // 2
    for z in range(chips // 2):
        for out_ref, y in ((near_ref, chip % 2), (far_ref, 1 - chip % 2)):
            target = 2 * z + y
            both = keep_ref[target].astype(F32) + got_ref[target].astype(F32)
            out_ref[z] = both.astype(out_ref.dtype)


def level_kernel(me_ref, near_ref, far_ref, *out_refs):
    level = me_ref[0] // 4
    for k, out_ref in enumerate(out_refs):
        out_ref[...] = (near_ref[level ^ k] + far_ref[level ^ k].astype(F32)).astype(BF16)


def token_rows(ctx_size, grads):
    rows = grads.shape[0]
    per = rows // ctx_size
    token, came = iota((rows, rows), 0), iota((rows, rows), 1)
    order = (token == (came % per) * ctx_size + came // per).astype(BF16)
    return nn(order, grads).astype(BF16)


def project_kernel(ctx_size, weight_ref, query_ref, out_ref):
    grads = token_rows(ctx_size, query_ref[...])
    out_ref[...] = nt(grads, weight_ref[:, 0 : grads.shape[1]])


def gate_kernel(
    ctx_size,
    me_ref,
    weight_ref,
    projected_ref,
    mixer_ref,
    gate_ref,
    gain_ref,
    read_ref,
    grow_ref,
    sum_ref,
    *rest,
):
    *part_refs, gate_out_ref, grad_out_ref, keep_ref, give_ref, grown_ref = rest
    rows, channels = mixer_ref.shape
    me = me_ref[0]
    sums = part_refs[0][...].astype(F32)
    for part_ref in part_refs[1:]:
        sums = sums + part_ref[...].astype(F32)
    grads = token_rows(ctx_size, sums.astype(BF16))
    columns = weight_ref.shape[1] - grads.shape[1]
    mixed = projected_ref[...] + nt(grads, weight_ref[:, columns:])
    mixer_grad = mixed.astype(BF16).astype(F32)

    mixer_out = mixer_ref[...]
    gate = gate_ref[...].astype(F32)
    sigmoid = jax.nn.sigmoid(gate)
    active = gate * sigmoid
    gated = mixer_out * active
    inverse = lax.rsqrt(jnp.mean(gated * gated, axis=-1, keepdims=True) + EPSILON)
    scaled = gain_ref[...] * mixer_grad
    mean = jnp.mean(scaled * gated, axis=-1, keepdims=True)
    gated_grad = scaled * inverse - gated * (mean * inverse * inverse * inverse)
    gate_out_ref[...] = gated_grad * mixer_out * sigmoid * (1.0 + gate * (1.0 - sigmoid))
    out_grad = (gated_grad * active).astype(BF16)
    grad_out_ref[...] = out_grad
    grown_ref[...] = (out_grad.astype(F32) * grow_ref[...]).astype(BF16)
    last = sum_ref[rows - 1 :, :]
    write_halves(me % 2, last, grown_ref, read_ref, keep_ref, give_ref)


def local_kernel(
    me_ref,
    grad_ref,
    grown_ref,
    input_ref,
    write_ref,
    read_ref,
    sum_ref,
    turned_ref,
    mine_ref,
    other_ref,
    value_ref,
    write_out_ref,
    read_out_ref,
    both_ref,
):
    rows, channels = input_ref.shape
    mheads = sum_ref.shape[1]
    mdim = channels // mheads
    cumulated, turned = sum_ref[...], turned_ref[...]
    turned_products = nt(write_ref[...], read_ref[...])
    causal = iota((rows, rows), 0) >= iota((rows, rows), 1)
    later = iota((rows, rows), 0) <= iota((rows, rows), 1)
    pair_sum = jnp.zeros((rows, rows), F32)

    def decays_of(head):
        spread = cumulated[:, head : head + 1] - turned[head : head + 1, :]
        return jnp.exp(jnp.where(causal, spread, -jnp.inf))

    def turned_weights_of(head):
        spread = turned[head : head + 1, :] - cumulated[:, head : head + 1]
        return (jnp.exp(jnp.where(later, spread, -jnp.inf)) * turned_products).astype(BF16)

    for pair in range(mheads // 2):
        lanes = slice(pair * 2 * mdim, (pair + 1) * 2 * mdim)
        grads = split_pair(grad_ref[:, lanes], mdim)
        weights = jnp.concatenate(
            [turned_weights_of(2 * pair), turned_weights_of(2 * pair + 1)], axis=1
        )
        value_ref[:, lanes] = nn(weights, grads)
        pairs = nt(grads, input_ref[:, lanes])
        pair_sum = (
            pair_sum + decays_of(2 * pair) * pairs[:rows] + decays_of(2 * pair + 1) * pairs[rows:]
        )
    pair_low = pair_sum.astype(BF16)
    incoming = whole_state(me_ref, mine_ref, other_ref, both_ref)
    read_out_ref[...] = nn(pair_low, write_ref[...]) + nn(grown_ref[...], incoming)
    write_out_ref[...] = tn(pair_low, read_ref[...])


def final_kernel(
    me_ref,
    value_ref,
    write_part_ref,
    scaled_ref,
    remain_ref,
    write_ref,
    mine_ref,
    other_ref,
    out_ref,
    write_out_ref,
    both_ref,
):
    adjoint = whole_state(me_ref, mine_ref, other_ref, both_ref)
    out_ref[...] = value_ref[...] + remain_ref[...] * nt(write_ref[...], adjoint)
    write_out_ref[...] = write_part_ref[...] + nn(scaled_ref[...], adjoint)


def crossed(array, bits):
    pairs = [(i, i ^ bits) for i in range(lax.axis_size("ctx"))]
    return lax.ppermute(array, "ctx", pairs)


def tied(arrays, after):
    return lax.optimization_barrier((arrays, after))[0]


def scan_slices(me, cumulated, keep, give, reverse):
    group = lax.axis_size("ctx") // 4
    half_rows, nstate = keep.shape
    got = crossed(give, 1)
    slices = call(
        functools.partial(chip_kernel, reverse),
        [struct((half_rows // group + EXTRA, nstate), BF16)] * group,
        [me, cumulated, keep, got],
        half_rows * nstate,
        smem=(0,),
        scratch=[pltpu.VMEM((half_rows, nstate), F32)],
    )
    return slices, got


def scan_parts(slices):
    return [slices[0]] + [crossed(slices[k], 2 * k) for k in range(1, len(slices))]


def scan_total(me, cumulated, keep, parts, reverse):
    group = len(parts)
    half_rows, nstate = keep.shape
    slice_rows = half_rows // group
    heads = cumulated.shape[1]
    (total,) = call(
        functools.partial(total_kernel, reverse, heads, 2 * half_rows // heads),
        [struct((slice_rows, nstate), BF16)],
        [me] + list(parts),
        half_rows * nstate,
        smem=(0,),
        scratch=[pltpu.VMEM((group, slice_rows + EXTRA, nstate), BF16)],
    )
    return total


def scan_carry(total, reverse):
    half = lax.axis_size("ctx") // 2
    if reverse:
        pairs = [(i + half, i) for i in range(half)]
    else:
        pairs = [(i, i + half) for i in range(half)]
    return lax.ppermute(total, "ctx", pairs)


def scan_back(me, cumulated, carry, keep, parts, reverse):
    group = len(parts)
    slice_rows, nstate = carry.shape
    heads = cumulated.shape[1]
    backs = call(
        functools.partial(scan_kernel, reverse, heads, 2 * keep.shape[0] // heads),
        [struct(carry.shape, BF16)] * group,
        [me, carry] + list(parts),
        group * slice_rows * nstate,
        smem=(0,),
        scratch=[
            pltpu.VMEM((group, slice_rows + EXTRA, nstate), BF16),
            pltpu.VMEM((group, slice_rows, nstate), BF16),
        ],
    )
    return backs


def scan_out(me, cumulated, returned, keep, got, reverse):
    mine, send = call(
        functools.partial(core_kernel, reverse),
        [struct(keep.shape, BF16)] * 2,
        [me, cumulated, keep, got] + list(returned),
        keep.size,
        smem=(0,),
        scratch=[pltpu.VMEM(keep.shape, BF16)],
    )
    return mine, crossed(send, 1)


def gather_near(packed):
    ctx_size = lax.axis_size("ctx")
    pieces = [None] * ctx_size
    pieces[0] = packed
    for k in range(4, ctx_size, 4):
        pieces[k] = crossed(packed, k)
    return pieces


def gather_far(pieces, y_after, core_after):
    ctx_size = len(pieces)
    pieces = list(pieces)
    for k in range(0, ctx_size, 4):
        last = k == ctx_size - 4
        pieces[k + 2] = crossed(tied(pieces[k], y_after) if last else pieces[k], 2)
    for k in range(0, ctx_size, 2):
        last = k == ctx_size - 2
        pieces[k + 1] = crossed(tied(pieces[k], core_after) if last else pieces[k], 1)
    return pieces


def body(
    queries,
    keys,
    values,
    d_out,
    mixer_input,
    gate_input,
    state_write,
    state_read,
    log_decay,
    norm_gain,
    project_weight,
):
    ctx_size = lax.axis_size("ctx")
    ctx_index = lax.axis_index("ctx")
    rows, head_dim = keys.shape
    wide = queries.shape[1]
    channels = mixer_input.shape[1]
    nstate = state_write.shape[1]
    mheads = log_decay.shape[1]
    per = rows // ctx_size
    me = ctx_index.astype(jnp.int32).reshape(1)
    (packed,) = call(
        pack_kernel, [struct((rows, 2 * head_dim), BF16)], [keys, values], rows * head_dim
    )
    pieces = gather_near(packed)
    half_states = [
        struct((channels // 2, nstate), BF16),
        struct((channels // 2 + EXTRA, nstate), BF16),
    ]
    tile = tile_of(rows)
    columns = tile * wide // head_dim
    stacked = struct((rows // tile, columns, head_dim), BF16)
    keep, give, scaled, remain, grow, cumulated, turned, query_tiles, grad_tiles = call(
        state_kernel,
        [
            *half_states,
            struct((rows, channels), BF16),
            struct((rows, channels), F32),
            struct((rows, channels), F32),
            struct((rows, mheads), F32),
            struct((mheads, rows), F32),
            stacked,
            stacked,
        ],
        [me, mixer_input, state_write, tied(log_decay.T, tuple(pieces[4::4])), queries, d_out],
        2 * rows * channels * nstate,
        smem=(0,),
    )

    slices, got = scan_slices(me, cumulated, keep, give, False)
    pieces = gather_far(pieces, scaled, slices[0])
    parts = scan_parts(slices)

    total = scan_total(me, cumulated, keep, parts, False)
    carry = scan_carry(total, False)
    query_tiles = tied(query_tiles, total)

    in_kernel = per % 8 == 0
    flops = 10 * rows * wide * ctx_size * rows
    scratch = [
        pltpu.VMEM((ctx_size, rows, 2 * head_dim), BF16),
        pltpu.VMEM((ctx_size, rows, 2 * head_dim), F32),
        pltpu.VMEM((rows // tile, ctx_size * tile, columns), F32),
        pltpu.VMEM((rows // tile, ctx_size * tile, columns), F32),
    ]
    attention_args = [me, query_tiles, grad_tiles] + list(pieces)
    chips = ctx_size // 2
    query_grad, *kv_grads = call(
        functools.partial(attention_kernel, in_kernel, ctx_size),
        [struct((rows, wide), BF16)]
        + (
            [struct((chips, rows, 2 * head_dim), BF16)] * 2
            if in_kernel
            else [struct((ctx_size, rows, 2 * head_dim), BF16)]
        ),
        attention_args,
        flops,
        smem=(0,),
        scratch=scratch,
    )
    if in_kernel:
        kv_keep, kv_give = kv_grads
    else:
        by_target = kv_grads[0].reshape(ctx_size, ctx_size, per, 2 * head_dim)
        by_target = by_target.transpose(1, 0, 2, 3).reshape(chips, 2, rows, 2 * head_dim)
        kv_keep = lax.dynamic_index_in_dim(by_target, ctx_index % 2, 1, False)
        kv_give = lax.dynamic_index_in_dim(by_target, 1 - ctx_index % 2, 1, False)

    carry, kv_keep, kv_give = lax.optimization_barrier((carry, kv_keep, kv_give))
    kv_got = crossed(kv_give, 1)
    backs = scan_back(me, cumulated, carry, keep, parts, False)
    near, far = call(
        join_kernel,
        [
            struct((chips // 2, rows, 2 * head_dim), F32),
            struct((chips // 2, rows, 2 * head_dim), BF16),
        ],
        [me, kv_keep, tied(kv_got, backs[0])],
        chips * rows * 2 * head_dim,
        smem=(0,),
    )
    far_got = crossed(far, 2)
    query_grad = tied(query_grad, far).reshape(ctx_size, per, wide)
    query_grad = lax.all_to_all(query_grad, "ctx", split_axis=0, concat_axis=0, tiled=True)
    part_sent = call(
        level_kernel,
        [struct((rows, 2 * head_dim), BF16)] * (chips // 2),
        [me, near, far_got],
        chips * rows * head_dim,
        smem=(0,),
    )
    part_received = [part_sent[0]] + [crossed(part_sent[k], 4 * k) for k in range(1, chips // 2)]
    (projected,) = call(
        functools.partial(project_kernel, ctx_size),
        [struct((rows, channels), F32)],
        [project_weight, query_grad.reshape(rows, wide)],
        2 * rows * channels * wide,
    )
    returned = tied(tuple(scan_parts(backs)), far)
    incoming, incoming_other = scan_out(me, cumulated, returned, keep, got, False)
    incoming = tied(incoming, (part_sent[0], projected))

    both_states = pltpu.VMEM((2, channels // 2, nstate), BF16)
    (mixer_out,) = call(
        mixer_kernel,
        [struct((rows, channels), F32)],
        [
            me,
            mixer_input,
            state_write,
            state_read,
            cumulated,
            turned,
            grow,
            incoming,
            incoming_other,
        ],
        2 * rows * channels * (nstate + rows),
        smem=(0,),
        scratch=[both_states],
    )
    gate_gradient, out_grad, adjoint_keep, adjoint_give, grown = call(
        functools.partial(gate_kernel, ctx_size),
        [
            struct((rows, channels), F32),
            struct((rows, channels), BF16),
            *half_states,
            struct((rows, channels), BF16),
        ],
        [
            me,
            project_weight,
            projected,
            mixer_out,
            gate_input,
            norm_gain.reshape(1, channels),
            state_read,
            grow,
            cumulated,
        ]
        + part_received,
        2 * rows * channels * (nstate + 2 * head_dim),
        smem=(0,),
    )
    value_part, write_part, read_gradient = call(
        local_kernel,
        [
            struct((rows, channels), F32),
            struct((rows, nstate), F32),
            struct((rows, nstate), F32),
        ],
        [
            me,
            out_grad,
            grown,
            mixer_input,
            state_write,
            state_read,
            cumulated,
            turned,
            incoming,
            incoming_other,
        ],
        2 * rows * channels * (nstate + 2 * rows),
        smem=(0,),
        scratch=[both_states],
    )
    slices, got = scan_slices(me, cumulated, adjoint_keep, adjoint_give, True)
    parts = scan_parts(slices)
    carry = scan_carry(scan_total(me, cumulated, adjoint_keep, parts, True), True)
    carry = tied(carry, write_part)
    backs = scan_back(me, cumulated, carry, adjoint_keep, parts, True)
    adjoint, adjoint_other = scan_out(
        me, cumulated, scan_parts(backs), adjoint_keep, got, True
    )
    input_gradient, write_gradient = call(
        final_kernel,
        [struct((rows, channels), F32), struct((rows, nstate), F32)],
        [
            me,
            value_part,
            write_part,
            scaled,
            remain,
            state_write,
            adjoint,
            adjoint_other,
        ],
        4 * rows * channels * nstate,
        smem=(0,),
        scratch=[both_states],
    )
    return (input_gradient, gate_gradient, write_gradient, read_gradient)


def solution(mesh):
    both = P("ctx", "groups")
    return jax.shard_map(
        body,
        mesh=mesh,
        in_specs=(both,) * 9 + (P("groups"), P(None, "groups")),
        out_specs=(both,) * 4,
        check_vma=False,
    )
```

```python
import functools
import math

import jax
import jax.numpy as jnp
import numpy as np
from jax import lax
from jax.experimental import pallas as pl
from jax.experimental.pallas import tpu as pltpu
from jax.sharding import PartitionSpec as P

EPSILON = 1e-05
HIGHEST = lax.Precision.HIGHEST
F32 = jnp.float32
BF16 = jnp.bfloat16
EXTRA = 16
MIB = 1024 * 1024


def nn(a, b, **kw):
    return lax.dot_general(a, b, (((1,), (0,)), ((), ())), preferred_element_type=F32, **kw)


def nt(a, b, **kw):
    return lax.dot_general(a, b, (((1,), (1,)), ((), ())), preferred_element_type=F32, **kw)


def tn(a, b, **kw):
    return lax.dot_general(a, b, (((0,), (0,)), ((), ())), preferred_element_type=F32, **kw)


def iota(shape, dim):
    return lax.broadcasted_iota(jnp.int32, shape, dim)


def call(kernel, outs, args, flops, smem=(), scratch=(), spare=4 * MIB, in_place=False):
    space = pl.ANY if in_place else pltpu.VMEM
    specs = [
        pl.BlockSpec(memory_space=pltpu.SMEM if i in smem else space) for i in range(len(args))
    ]
    moved = sum(a.size * a.dtype.itemsize for a in args) + sum(
        math.prod(o.shape) * o.dtype.itemsize for o in outs
    )
    held = moved + sum(
        math.prod(s.shape) * jnp.dtype(s.dtype).itemsize for s in scratch if isinstance(s.dtype, np.dtype)
    )
    return pl.pallas_call(
        kernel,
        out_shape=tuple(outs),
        in_specs=specs,
        out_specs=tuple(pl.BlockSpec(memory_space=space) for _ in outs),
        scratch_shapes=list(scratch),
        compiler_params=pltpu.CompilerParams(vmem_limit_bytes=held + spare),
        cost_estimate=pl.CostEstimate(flops=flops, bytes_accessed=moved, transcendentals=0),
    )(*args)


def struct(shape, dtype):
    return jax.ShapeDtypeStruct(shape, dtype)


def running_sums(log_decay):
    rows = log_decay.shape[1]
    lower = (iota((rows, rows), 0) >= iota((rows, rows), 1)).astype(F32)
    upper = (iota((rows, rows), 0) <= iota((rows, rows), 1)).astype(F32)
    return nt(lower, log_decay, precision=HIGHEST), nn(log_decay, upper, precision=HIGHEST)


def spread_heads(per_head, mdim):
    rows, heads = per_head.shape
    first = iota((rows, 2 * mdim), 1) < mdim
    pairs = [
        jnp.where(first, per_head[:, h : h + 1], per_head[:, h + 1 : h + 2])
        for h in range(0, heads, 2)
    ]
    return jnp.concatenate(pairs, axis=1)


def split_pair(block, mdim):
    first = iota(block.shape, 1) < mdim
    zero = jnp.zeros_like(block)
    return jnp.concatenate([jnp.where(first, block, zero), jnp.where(first, zero, block)], axis=0)


def pack_kernel(key_ref, value_ref, packed_ref, sem):
    head_dim = key_ref.shape[1]
    copies = [
        pltpu.make_async_copy(key_ref, packed_ref.at[:, 0:head_dim], sem.at[0]),
        pltpu.make_async_copy(value_ref, packed_ref.at[:, head_dim : 2 * head_dim], sem.at[1]),
    ]
    for copy in copies:
        copy.start()
    for copy in copies:
        copy.wait()


def tile_of(rows):
    return min(32, rows)


def stack_kernel(*refs):
    count = len(refs) // 2
    for ref, out_ref in zip(refs[:count], refs[count:]):
        tiles, wide, head_dim = out_ref.shape
        tile = ref.shape[0] // tiles
        for t in range(tiles):
            for h in range(wide // tile):
                out_ref[t, h * tile : (h + 1) * tile, :] = ref[
                    t * tile : (t + 1) * tile, h * head_dim : (h + 1) * head_dim
                ]


def put_logs(ref, logs):
    heads = logs.shape[1]
    high = logs.astype(BF16).astype(F32)
    middle = (logs - high).astype(BF16).astype(F32)
    low = (logs - high - middle).astype(BF16).astype(F32)
    place = iota((EXTRA, heads), 0)
    split = jnp.where(place == 0, high, jnp.where(place == 1, middle, low))
    wide = jnp.concatenate([split, jnp.zeros((EXTRA, ref.shape[1] - heads), F32)], axis=1)
    ref[ref.shape[0] - EXTRA :, :] = wide.astype(BF16)


def get_logs(ref, heads):
    parts = ref[ref.shape[0] - EXTRA :, 0:heads].astype(F32)
    return parts[0:1, :] + parts[1:2, :] + parts[2:3, :]


def times(logs, start, mdim, state):
    head = iota(logs.shape, 1)
    blocks = []
    for i in range(state.shape[0] // mdim):
        log = jnp.sum(jnp.where(head == start + i, logs, 0.0), axis=1, keepdims=True)
        blocks.append(jnp.exp(log) * state[i * mdim : (i + 1) * mdim, :])
    return jnp.concatenate(blocks, axis=0)


def write_halves(core, logs, scaled_ref, other_ref, keep_ref, give_ref):
    half = keep_ref.shape[0]
    for out_ref, which in ((keep_ref, core), (give_ref, 1 - core)):
        lanes = pl.ds(pl.multiple_of(which * half, half), half)
        out_ref[0:half, :] = tn(scaled_ref[:, lanes], other_ref[...]).astype(BF16)
    put_logs(give_ref, logs)


def state_kernel(
    me_ref,
    input_ref,
    write_ref,
    decay_ref,
    keep_ref,
    give_ref,
    scaled_ref,
    remain_ref,
    grow_ref,
    sum_ref,
    turned_ref,
):
    cumulated, turned = running_sums(decay_ref[...])
    sum_ref[...], turned_ref[...] = cumulated, turned
    mdim = input_ref.shape[1] // cumulated.shape[1]
    last = cumulated[-1:, :]
    remain_ref[...] = spread_heads(jnp.exp(last - cumulated), mdim)
    grow_ref[...] = spread_heads(jnp.exp(cumulated), mdim)
    scaled_ref[...] = (input_ref[...].astype(F32) * remain_ref[...]).astype(BF16)
    write_halves(me_ref[0] % 2, last, scaled_ref, write_ref, keep_ref, give_ref)


def chip_kernel(reverse, me_ref, sum_ref, keep_ref, got_ref, *rest):
    *out_refs, total_ref = rest
    heads = sum_ref.shape[1]
    half = keep_ref.shape[0]
    mdim = 2 * half // heads
    core = me_ref[0] % 2
    chip = me_ref[0] // 2 % len(out_refs)
    slice_rows = out_refs[0].shape[0] - EXTRA
    own_logs = sum_ref[sum_ref.shape[0] - 1 :, :]
    got_logs = get_logs(got_ref, heads)
    keep, got = keep_ref[...].astype(F32), got_ref[0:half, :].astype(F32)
    first = core == (1 if reverse else 0)
    decayed = times(jnp.where(first, got_logs, own_logs), core * heads // 2, mdim, jnp.where(first, keep, got))
    total_ref[...] = decayed + jnp.where(first, got, keep)
    for k, out_ref in enumerate(out_refs):
        start = pl.multiple_of((chip ^ k) * slice_rows, slice_rows)
        out_ref[0:slice_rows, :] = total_ref[pl.ds(start, slice_rows), :].astype(BF16)
        put_logs(out_ref, own_logs + got_logs)


def steps(count, reverse):
    return range(count - 1, -1, -1) if reverse else range(count)


def ordered(chip, part_refs, order_ref):
    for k, part_ref in enumerate(part_refs):
        order_ref[chip ^ k] = part_ref[...]


def advance(order_ref, source, start, heads, mdim, state):
    part_ref = order_ref.at[source]
    rows = state.shape[0]
    return times(get_logs(part_ref, heads), start, mdim, state) + part_ref[0:rows, :].astype(F32)


def total_kernel(reverse, heads, mdim, me_ref, *rest):
    *part_refs, out_ref, order_ref = rest
    count = len(part_refs)
    chip = me_ref[0] // 2 % count
    ordered(chip, part_refs, order_ref)
    start = me_ref[0] % 2 * (heads // 2) + chip * (heads // 2 // count)
    state = jnp.zeros(out_ref.shape, F32)
    for source in steps(count, reverse):
        state = advance(order_ref, source, start, heads, mdim, state)
    out_ref[...] = state.astype(BF16)


def scan_kernel(reverse, heads, mdim, me_ref, carry_ref, *rest):
    *refs, order_ref, result_ref = rest
    count = len(refs) // 2
    chip = me_ref[0] // 2 % count
    ordered(chip, refs[:count], order_ref)
    start = me_ref[0] % 2 * (heads // 2) + chip * (heads // 2 // count)
    state = carry_ref[...].astype(F32)
    for source in steps(count, reverse):
        result_ref[source] = state.astype(BF16)
        state = advance(order_ref, source, start, heads, mdim, state)
    for k, out_ref in enumerate(refs[count:]):
        out_ref[...] = result_ref[chip ^ k]


def core_kernel(reverse, me_ref, sum_ref, keep_ref, got_ref, *rest):
    *part_refs, mine_ref, send_ref, order_ref = rest
    count = len(part_refs)
    heads = sum_ref.shape[1]
    half = keep_ref.shape[0]
    core = me_ref[0] % 2
    chip = me_ref[0] // 2 % count
    slice_rows = part_refs[0].shape[0]
    for k, part_ref in enumerate(part_refs):
        start = pl.multiple_of((chip ^ k) * slice_rows, slice_rows)
        order_ref[pl.ds(start, slice_rows), :] = part_ref[...]
    first = core == (1 if reverse else 0)
    logs = jnp.where(first, sum_ref[sum_ref.shape[0] - 1 :, :], get_logs(got_ref, heads))
    own = jnp.where(first, keep_ref[...].astype(F32), got_ref[0:half, :].astype(F32))
    incoming = order_ref[...].astype(F32)
    passed = times(logs, core * heads // 2, 2 * half // heads, incoming) + own
    mine_ref[...] = jnp.where(first, incoming, passed).astype(BF16)
    send_ref[...] = jnp.where(first, passed, incoming).astype(BF16)


def whole_state(me_ref, mine_ref, other_ref, both_ref):
    core = me_ref[0] % 2
    both_ref[core] = mine_ref[...]
    both_ref[1 - core] = other_ref[...]
    _, half, nstate = both_ref.shape
    return both_ref[...].reshape(2 * half, nstate)


def mixer_kernel(
    me_ref,
    input_ref,
    write_ref,
    read_ref,
    sum_ref,
    turned_ref,
    grow_ref,
    mine_ref,
    other_ref,
    out_ref,
    both_ref,
):
    rows, channels = input_ref.shape
    mheads = sum_ref.shape[1]
    mdim = channels // mheads
    cumulated, turned = sum_ref[...], turned_ref[...]
    carried = nt(read_ref[...], whole_state(me_ref, mine_ref, other_ref, both_ref))
    out_ref[...] = grow_ref[...] * carried
    products = nt(read_ref[...], write_ref[...])
    causal = iota((rows, rows), 0) >= iota((rows, rows), 1)

    def weights_of(head):
        spread = cumulated[:, head : head + 1] - turned[head : head + 1, :]
        return (jnp.exp(jnp.where(causal, spread, -jnp.inf)) * products).astype(BF16)

    for pair in range(mheads // 2):
        lanes = slice(pair * 2 * mdim, (pair + 1) * 2 * mdim)
        weights = jnp.concatenate([weights_of(2 * pair), weights_of(2 * pair + 1)], axis=1)
        out_ref[:, lanes] += nn(weights, split_pair(input_ref[:, lanes], mdim))


def attention_kernel(
    in_kernel, ctx_size, me_ref, query_ref, grad_ref, *rest
):
    piece_refs, rest = rest[:ctx_size], rest[ctx_size:]
    if in_kernel:
        keep_ref, give_ref, gathered_ref, acc_ref, raw_ref, back_ref, query_acc_ref = rest
    else:
        query_out_ref, pack_ref, gathered_ref, acc_ref, raw_ref, back_ref = rest
    tiles, wide, head_dim = query_ref.shape
    rows = gathered_ref.shape[1]
    tile = rows // tiles
    heads = wide // tile
    me = me_ref[0]
    scale = 1.0 / math.sqrt(head_dim)
    base2 = scale * math.log2(math.e)
    per = rows // ctx_size
    for offset, piece_ref in enumerate(piece_refs):
        gathered_ref[me ^ offset] = piece_ref[...]

    def keys_of(b):
        return gathered_ref[:, b * tile : (b + 1) * tile, 0:head_dim].reshape(
            ctx_size * tile, head_dim
        )

    def values_of(b):
        return gathered_ref[:, b * tile : (b + 1) * tile, head_dim : 2 * head_dim].reshape(
            ctx_size * tile, head_dim
        )

    key_row = iota((ctx_size * tile, wide), 0)
    key_place = (key_row % tile) * ctx_size + key_row // tile
    query_place = (iota((ctx_size * tile, wide), 1) % tile) * ctx_size + me
    visible = key_place <= query_place

    for t in range(tiles - 1, -1, -1):
        query = query_ref[t]
        grad = grad_ref[t]
        highest = None
        for b in range(t, -1, -1):
            raw = nt(keys_of(b), query)
            if b == t:
                raw = jnp.where(visible, raw, -jnp.inf)
            raw_ref[b] = raw
            block_high = jnp.max(raw, axis=0, keepdims=True)
            highest = block_high if highest is None else jnp.maximum(highest, block_high)
        total = jnp.zeros((1, wide), F32)
        delta = jnp.zeros((1, wide), F32)
        for b in range(t + 1):
            probs = jnp.exp2((raw_ref[b] - highest) * base2)
            back = nt(values_of(b), grad)
            raw_ref[b] = probs
            back_ref[b] = back
            total = total + jnp.sum(probs, axis=0, keepdims=True)
            delta = delta + jnp.sum(probs * back, axis=0, keepdims=True)
        inverse = 1.0 / total
        delta = delta * inverse
        query_grad = jnp.zeros((head_dim, wide), F32)
        for b in range(t + 1):
            weights = raw_ref[b] * inverse
            score_grad = (weights * (back_ref[b] - delta)).astype(BF16)
            value_part = nn(weights.astype(BF16), grad).reshape(ctx_size, tile, head_dim)
            key_part = nn(score_grad, query).reshape(ctx_size, tile, head_dim)
            here = slice(b * tile, (b + 1) * tile)
            if t == tiles - 1:
                acc_ref[:, here, 0:head_dim] = key_part
                acc_ref[:, here, head_dim:] = value_part
            else:
                acc_ref[:, here, 0:head_dim] += key_part
                acc_ref[:, here, head_dim:] += value_part
            query_grad = query_grad + tn(keys_of(b), score_grad)
        turned = (query_grad * scale).T
        by_head = [turned[h * tile : (h + 1) * tile, :] for h in range(heads)]
        if in_kernel:
            pairs = [
                jnp.concatenate(by_head[h : h + 2], axis=1) for h in range(0, heads, 2)
            ]
            for k in range(tile // per):
                rows_here = [p[k * per : (k + 1) * per, :] for p in pairs]
                query_acc_ref[t * (tile // per) + k] = jnp.concatenate(rows_here, axis=0)
        else:
            for h in range(heads):
                query_out_ref[t * tile : (t + 1) * tile, h * head_dim : (h + 1) * head_dim] = (
                    by_head[h].astype(BF16)
                )

    both = jnp.where(iota((1, 1, 2 * head_dim), 2) < head_dim, scale, 1.0)
    if in_kernel:
        for chip in range(ctx_size // 2):
            for out_ref, core in ((keep_ref, me % 2), (give_ref, 1 - me % 2)):
                target = 2 * chip + core
                start = pl.multiple_of(target * per, per)
                block = acc_ref[:, pl.ds(start, per), :] * both
                out_ref[chip, 0:rows, :] = block.reshape(rows, 2 * head_dim).astype(BF16)
                out_ref[chip, rows:, :] = query_acc_ref[target].astype(BF16)
    else:
        pack_ref[...] = (acc_ref[...] * both).astype(BF16)


def join_kernel(me_ref, keep_ref, got_ref, near_ref, far_ref, *query_refs):
    chips = keep_ref.shape[0]
    rows = near_ref.shape[1]
    extra = keep_ref.shape[1] - rows
    chip = me_ref[0] // 2
    for z in range(chips // 2):
        for out_ref, y in ((near_ref, chip % 2), (far_ref, 1 - chip % 2)):
            target = 2 * z + y
            both = keep_ref[target, 0:rows, :].astype(F32) + got_ref[target, 0:rows, :].astype(F32)
            out_ref[z] = both.astype(out_ref.dtype)
    for k, query_ref in enumerate(query_refs):
        query_ref[0:extra, :] = keep_ref[chip ^ k, rows:, :]
        query_ref[extra:, :] = got_ref[chip ^ k, rows:, :]


def level_kernel(me_ref, near_ref, far_ref, *out_refs):
    level = me_ref[0] // 4
    for k, out_ref in enumerate(out_refs):
        out_ref[...] = (near_ref[level ^ k] + far_ref[level ^ k].astype(F32)).astype(BF16)


def in_token_order(ctx_size, devices, grads):
    rows = grads.shape[0]
    per = rows // ctx_size
    token, came = iota((rows, rows), 0), iota((rows, rows), 1)
    order = (token == (came % per) * ctx_size + devices(came // per)).astype(BF16)
    return nn(order, grads).astype(BF16)


def project_kernel(me_ref, weight_ref, *rest):
    *query_refs, out_ref = rest
    chips = len(query_refs)
    rows = out_ref.shape[0]
    per = rows // (2 * chips)
    extra = query_refs[0].shape[0] // 2
    query_rows = [query_ref[...].astype(F32) for query_ref in query_refs]
    columns = []
    for part in range(extra // per):
        blocks = [
            block[core * extra + part * per : core * extra + (part + 1) * per, :]
            for core in range(2)
            for block in query_rows
        ]
        columns.append(jnp.concatenate(blocks, axis=0))
    query_grads = jnp.concatenate(columns, axis=1).astype(BF16)
    grads = in_token_order(
        2 * chips, lambda place: (2 * (place % chips) + place // chips) ^ me_ref[0], query_grads
    )
    out_ref[...] = nt(grads, weight_ref[:, 0 : grads.shape[1]])


def gate_kernel(
    ctx_size,
    me_ref,
    weight_ref,
    projected_ref,
    mixer_ref,
    gate_ref,
    gain_ref,
    read_ref,
    grow_ref,
    sum_ref,
    *rest,
):
    *part_refs, gate_out_ref, grad_out_ref, keep_ref, give_ref, grown_ref = rest
    rows, channels = mixer_ref.shape
    me = me_ref[0]
    sums = part_refs[0][...].astype(F32)
    for part_ref in part_refs[1:]:
        sums = sums + part_ref[...].astype(F32)
    grads = in_token_order(ctx_size, lambda place: place, sums.astype(BF16))
    columns = weight_ref.shape[1] - grads.shape[1]
    mixed = projected_ref[...] + nt(grads, weight_ref[:, columns:])
    mixer_grad = mixed.astype(BF16).astype(F32)

    mixer_out = mixer_ref[...]
    gate = gate_ref[...].astype(F32)
    sigmoid = jax.nn.sigmoid(gate)
    active = gate * sigmoid
    gated = mixer_out * active
    inverse = lax.rsqrt(jnp.mean(gated * gated, axis=-1, keepdims=True) + EPSILON)
    scaled = gain_ref[...] * mixer_grad
    mean = jnp.mean(scaled * gated, axis=-1, keepdims=True)
    gated_grad = scaled * inverse - gated * (mean * inverse * inverse * inverse)
    gate_out_ref[...] = gated_grad * mixer_out * sigmoid * (1.0 + gate * (1.0 - sigmoid))
    out_grad = (gated_grad * active).astype(BF16)
    grad_out_ref[...] = out_grad
    grown_ref[...] = (out_grad.astype(F32) * grow_ref[...]).astype(BF16)
    last = sum_ref[rows - 1 :, :]
    write_halves(me % 2, last, grown_ref, read_ref, keep_ref, give_ref)


def local_kernel(
    me_ref,
    grad_ref,
    grown_ref,
    input_ref,
    write_ref,
    read_ref,
    sum_ref,
    turned_ref,
    mine_ref,
    other_ref,
    value_ref,
    write_out_ref,
    read_out_ref,
    both_ref,
):
    rows, channels = input_ref.shape
    mheads = sum_ref.shape[1]
    mdim = channels // mheads
    cumulated, turned = sum_ref[...], turned_ref[...]
    turned_products = nt(write_ref[...], read_ref[...])
    causal = iota((rows, rows), 0) >= iota((rows, rows), 1)
    later = iota((rows, rows), 0) <= iota((rows, rows), 1)
    pair_sum = jnp.zeros((rows, rows), F32)

    def decays_of(head):
        spread = cumulated[:, head : head + 1] - turned[head : head + 1, :]
        return jnp.exp(jnp.where(causal, spread, -jnp.inf))

    def turned_weights_of(head):
        spread = turned[head : head + 1, :] - cumulated[:, head : head + 1]
        return (jnp.exp(jnp.where(later, spread, -jnp.inf)) * turned_products).astype(BF16)

    for pair in range(mheads // 2):
        lanes = slice(pair * 2 * mdim, (pair + 1) * 2 * mdim)
        grads = split_pair(grad_ref[:, lanes], mdim)
        weights = jnp.concatenate(
            [turned_weights_of(2 * pair), turned_weights_of(2 * pair + 1)], axis=1
        )
        value_ref[:, lanes] = nn(weights, grads)
        pairs = nt(grads, input_ref[:, lanes])
        pair_sum = (
            pair_sum + decays_of(2 * pair) * pairs[:rows] + decays_of(2 * pair + 1) * pairs[rows:]
        )
    pair_low = pair_sum.astype(BF16)
    incoming = whole_state(me_ref, mine_ref, other_ref, both_ref)
    read_out_ref[...] = nn(pair_low, write_ref[...]) + nn(grown_ref[...], incoming)
    write_out_ref[...] = tn(pair_low, read_ref[...])


def final_kernel(
    me_ref,
    value_ref,
    write_part_ref,
    scaled_ref,
    remain_ref,
    write_ref,
    mine_ref,
    other_ref,
    out_ref,
    write_out_ref,
    both_ref,
):
    adjoint = whole_state(me_ref, mine_ref, other_ref, both_ref)
    out_ref[...] = value_ref[...] + remain_ref[...] * nt(write_ref[...], adjoint)
    write_out_ref[...] = write_part_ref[...] + nn(scaled_ref[...], adjoint)


def crossed(array, bits):
    pairs = [(i, i ^ bits) for i in range(lax.axis_size("ctx"))]
    return lax.ppermute(array, "ctx", pairs)


def tied(arrays, after):
    return lax.optimization_barrier((arrays, after))[0]


def scan_slices(me, cumulated, keep, give, reverse):
    group = lax.axis_size("ctx") // 4
    half_rows, nstate = keep.shape
    got = crossed(give, 1)
    slices = call(
        functools.partial(chip_kernel, reverse),
        [struct((half_rows // group + EXTRA, nstate), BF16)] * group,
        [me, cumulated, keep, got],
        half_rows * nstate,
        smem=(0,),
        scratch=[pltpu.VMEM((half_rows, nstate), F32)],
    )
    return slices, got


def scan_parts(slices):
    return [slices[0]] + [crossed(slices[k], 2 * k) for k in range(1, len(slices))]


def scan_total(me, cumulated, keep, parts, reverse):
    group = len(parts)
    half_rows, nstate = keep.shape
    slice_rows = half_rows // group
    heads = cumulated.shape[1]
    (total,) = call(
        functools.partial(total_kernel, reverse, heads, 2 * half_rows // heads),
        [struct((slice_rows, nstate), BF16)],
        [me] + list(parts),
        half_rows * nstate,
        smem=(0,),
        scratch=[pltpu.VMEM((group, slice_rows + EXTRA, nstate), BF16)],
    )
    return total


def scan_carry(total, reverse):
    half = lax.axis_size("ctx") // 2
    if reverse:
        pairs = [(i + half, i) for i in range(half)]
    else:
        pairs = [(i, i + half) for i in range(half)]
    return lax.ppermute(total, "ctx", pairs)


def scan_back(me, cumulated, carry, keep, parts, reverse):
    group = len(parts)
    slice_rows, nstate = carry.shape
    heads = cumulated.shape[1]
    backs = call(
        functools.partial(scan_kernel, reverse, heads, 2 * keep.shape[0] // heads),
        [struct(carry.shape, BF16)] * group,
        [me, carry] + list(parts),
        group * slice_rows * nstate,
        smem=(0,),
        scratch=[
            pltpu.VMEM((group, slice_rows + EXTRA, nstate), BF16),
            pltpu.VMEM((group, slice_rows, nstate), BF16),
        ],
    )
    return backs


def scan_out(me, cumulated, returned, keep, got, reverse):
    mine, send = call(
        functools.partial(core_kernel, reverse),
        [struct(keep.shape, BF16)] * 2,
        [me, cumulated, keep, got] + list(returned),
        keep.size,
        smem=(0,),
        scratch=[pltpu.VMEM(keep.shape, BF16)],
    )
    return mine, crossed(send, 1)


def gather_near(packed):
    ctx_size = lax.axis_size("ctx")
    pieces = [None] * ctx_size
    pieces[0] = packed
    for k in range(4, ctx_size, 4):
        pieces[k] = crossed(packed, k)
    return pieces


def gather_far(pieces, y_after, core_after):
    ctx_size = len(pieces)
    pieces = list(pieces)
    for k in range(0, ctx_size, 4):
        pieces[k + 2] = crossed(tied(pieces[k], y_after) if k else pieces[k], 2)
    for k in range(0, ctx_size, 2):
        last = k == ctx_size - 2
        pieces[k + 1] = crossed(tied(pieces[k], core_after) if last else pieces[k], 1)
    return pieces


def body(
    queries,
    keys,
    values,
    d_out,
    mixer_input,
    gate_input,
    state_write,
    state_read,
    log_decay,
    norm_gain,
    project_weight,
):
    ctx_size = lax.axis_size("ctx")
    ctx_index = lax.axis_index("ctx")
    rows, head_dim = keys.shape
    wide = queries.shape[1]
    channels = mixer_input.shape[1]
    nstate = state_write.shape[1]
    mheads = log_decay.shape[1]
    per = rows // ctx_size
    me = ctx_index.astype(jnp.int32).reshape(1)
    (packed,) = call(
        pack_kernel,
        [struct((rows, 2 * head_dim), BF16)],
        [keys, values],
        rows * head_dim,
        scratch=[pltpu.SemaphoreType.DMA((2,))],
        spare=56 * MIB,
        in_place=True,
    )
    pieces = gather_near(packed)
    half_states = [
        struct((channels // 2, nstate), BF16),
        struct((channels // 2 + EXTRA, nstate), BF16),
    ]
    tile = tile_of(rows)
    columns = tile * wide // head_dim
    stacked = struct((rows // tile, columns, head_dim), BF16)
    keep, give, scaled, remain, grow, cumulated, turned = call(
        state_kernel,
        [
            *half_states,
            struct((rows, channels), BF16),
            struct((rows, channels), F32),
            struct((rows, channels), F32),
            struct((rows, mheads), F32),
            struct((mheads, rows), F32),
        ],
        [me, mixer_input, state_write, log_decay.T],
        2 * rows * channels * nstate,
        smem=(0,),
    )

    query_tiles, grad_tiles = call(
        stack_kernel, [stacked, stacked], [queries, d_out], rows * wide
    )
    slices, got = scan_slices(me, cumulated, keep, give, False)
    pieces = gather_far(pieces, scaled, (slices[0], query_tiles))
    parts = scan_parts(slices)

    total = scan_total(me, cumulated, keep, parts, False)
    carry = scan_carry(total, False)
    query_tiles = tied(query_tiles, total)

    in_kernel = per % 8 == 0
    flops = 10 * rows * wide * ctx_size * rows
    scratch = [
        pltpu.VMEM((ctx_size, rows, 2 * head_dim), BF16),
        pltpu.VMEM((ctx_size, rows, 2 * head_dim), F32),
        pltpu.VMEM((rows // tile, ctx_size * tile, columns), F32),
        pltpu.VMEM((rows // tile, ctx_size * tile, columns), F32),
    ]
    attention_args = [me, query_tiles, grad_tiles] + list(pieces)
    chips = ctx_size // 2
    extra = per * wide // (2 * head_dim)
    if in_kernel:
        part = struct((chips, rows + extra, 2 * head_dim), BF16)
        kv_keep, kv_give = call(
            functools.partial(attention_kernel, True, ctx_size),
            [part, part],
            attention_args,
            flops,
            smem=(0,),
            scratch=scratch + [pltpu.VMEM((ctx_size, extra, 2 * head_dim), F32)],
        )
    else:
        query_grad, kv_grad = call(
            functools.partial(attention_kernel, False, ctx_size),
            [struct((rows, wide), BF16), struct((ctx_size, rows, 2 * head_dim), BF16)],
            attention_args,
            flops,
            smem=(0,),
            scratch=scratch,
        )
        by_target = kv_grad.reshape(ctx_size, ctx_size, per, 2 * head_dim).transpose(1, 0, 2, 3)
        by_pair = query_grad.reshape(ctx_size, per, -1, 2 * head_dim).transpose(0, 2, 1, 3)
        sent = jnp.concatenate(
            [
                by_target.reshape(ctx_size, rows, 2 * head_dim),
                by_pair.reshape(ctx_size, extra, 2 * head_dim),
            ],
            axis=1,
        ).reshape(chips, 2, rows + extra, 2 * head_dim)
        kv_keep = lax.dynamic_index_in_dim(sent, ctx_index % 2, 1, False)
        kv_give = lax.dynamic_index_in_dim(sent, 1 - ctx_index % 2, 1, False)

    carry, kv_keep, kv_give = lax.optimization_barrier((carry, kv_keep, kv_give))
    kv_got = crossed(kv_give, 1)
    backs = scan_back(me, cumulated, carry, keep, parts, False)
    near, far, *query_sent = call(
        join_kernel,
        [
            struct((chips // 2, rows, 2 * head_dim), F32),
            struct((chips // 2, rows, 2 * head_dim), BF16),
        ]
        + [struct((2 * extra, 2 * head_dim), BF16)] * chips,
        [me, kv_keep, tied(kv_got, backs[0])],
        chips * rows * 2 * head_dim,
        smem=(0,),
    )
    far_got = crossed(far, 2)
    query_received = [query_sent[0]] + [crossed(query_sent[k], 2 * k) for k in range(1, chips)]
    far_got, query_received = lax.optimization_barrier((far_got, tuple(query_received)))
    part_sent = call(
        level_kernel,
        [struct((rows, 2 * head_dim), BF16)] * (chips // 2),
        [me, near, far_got],
        chips * rows * head_dim,
        smem=(0,),
    )
    part_received = [part_sent[0]] + [crossed(part_sent[k], 4 * k) for k in range(1, chips // 2)]
    (projected,) = call(
        project_kernel,
        [struct((rows, channels), F32)],
        [me, project_weight] + list(query_received),
        2 * rows * channels * wide,
        smem=(0,),
    )
    returned = tied(tuple(scan_parts(backs)), part_sent[0])
    incoming, incoming_other = scan_out(me, cumulated, returned, keep, got, False)
    incoming = tied(incoming, projected)

    both_states = pltpu.VMEM((2, channels // 2, nstate), BF16)
    (mixer_out,) = call(
        mixer_kernel,
        [struct((rows, channels), F32)],
        [
            me,
            mixer_input,
            state_write,
            state_read,
            cumulated,
            turned,
            grow,
            incoming,
            incoming_other,
        ],
        2 * rows * channels * (nstate + rows),
        smem=(0,),
        scratch=[both_states],
    )
    gate_gradient, out_grad, adjoint_keep, adjoint_give, grown = call(
        functools.partial(gate_kernel, ctx_size),
        [
            struct((rows, channels), F32),
            struct((rows, channels), BF16),
            *half_states,
            struct((rows, channels), BF16),
        ],
        [
            me,
            project_weight,
            projected,
            mixer_out,
            gate_input,
            norm_gain.reshape(1, channels),
            state_read,
            grow,
            cumulated,
        ]
        + part_received,
        2 * rows * channels * (nstate + 2 * head_dim),
        smem=(0,),
    )
    value_part, write_part, read_gradient = call(
        local_kernel,
        [
            struct((rows, channels), F32),
            struct((rows, nstate), F32),
            struct((rows, nstate), F32),
        ],
        [
            me,
            out_grad,
            grown,
            mixer_input,
            state_write,
            state_read,
            cumulated,
            turned,
            incoming,
            incoming_other,
        ],
        2 * rows * channels * (nstate + 2 * rows),
        smem=(0,),
        scratch=[both_states],
    )
    slices, got = scan_slices(me, cumulated, adjoint_keep, adjoint_give, True)
    parts = scan_parts(slices)
    carry = scan_carry(scan_total(me, cumulated, adjoint_keep, parts, True), True)
    carry = tied(carry, write_part)
    backs = scan_back(me, cumulated, carry, adjoint_keep, parts, True)
    adjoint, adjoint_other = scan_out(
        me, cumulated, scan_parts(backs), adjoint_keep, got, True
    )
    input_gradient, write_gradient = call(
        final_kernel,
        [struct((rows, channels), F32), struct((rows, nstate), F32)],
        [
            me,
            value_part,
            write_part,
            scaled,
            remain,
            state_write,
            adjoint,
            adjoint_other,
        ],
        4 * rows * channels * nstate,
        smem=(0,),
        scratch=[both_states],
    )
    return (input_gradient, gate_gradient, write_gradient, read_gradient)


def solution(mesh):
    both = P("ctx", "groups")
    return jax.shard_map(
        body,
        mesh=mesh,
        in_specs=(both,) * 9 + (P("groups"), P(None, "groups")),
        out_specs=(both,) * 4,
        check_vma=False,
    )
```

```python
import functools
import math

import jax
import jax.numpy as jnp
from jax import lax
from jax.experimental import pallas as pl
from jax.experimental.pallas import tpu as pltpu
from jax.sharding import PartitionSpec as P

EPSILON = 1e-05
HIGHEST = lax.Precision.HIGHEST
F32 = jnp.float32
BF16 = jnp.bfloat16
EXTRA = 16
MIB = 1024 * 1024


def nn(a, b, **kw):
    return lax.dot_general(a, b, (((1,), (0,)), ((), ())), preferred_element_type=F32, **kw)


def nt(a, b, **kw):
    return lax.dot_general(a, b, (((1,), (1,)), ((), ())), preferred_element_type=F32, **kw)


def tn(a, b, **kw):
    return lax.dot_general(a, b, (((0,), (0,)), ((), ())), preferred_element_type=F32, **kw)


def iota(shape, dim):
    return lax.broadcasted_iota(jnp.int32, shape, dim)


def call(kernel, outs, args, flops, smem=(), scratch=(), spare=4 * MIB):
    specs = [
        pl.BlockSpec(memory_space=pltpu.SMEM if i in smem else pltpu.VMEM) for i in range(len(args))
    ]
    moved = sum(a.size * a.dtype.itemsize for a in args) + sum(
        math.prod(o.shape) * o.dtype.itemsize for o in outs
    )
    held = moved + sum(
        math.prod(s.shape) * jnp.dtype(s.dtype).itemsize for s in scratch
    )
    return pl.pallas_call(
        kernel,
        out_shape=tuple(outs),
        in_specs=specs,
        out_specs=tuple(pl.BlockSpec(memory_space=pltpu.VMEM) for _ in outs),
        scratch_shapes=list(scratch),
        compiler_params=pltpu.CompilerParams(vmem_limit_bytes=held + spare),
        cost_estimate=pl.CostEstimate(flops=flops, bytes_accessed=moved, transcendentals=0),
    )(*args)


def struct(shape, dtype):
    return jax.ShapeDtypeStruct(shape, dtype)


def running_sums(log_decay):
    rows = log_decay.shape[1]
    lower = (iota((rows, rows), 0) >= iota((rows, rows), 1)).astype(F32)
    upper = (iota((rows, rows), 0) <= iota((rows, rows), 1)).astype(F32)
    return nt(lower, log_decay, precision=HIGHEST), nn(log_decay, upper, precision=HIGHEST)


def spread_heads(per_head, mdim):
    rows, heads = per_head.shape
    first = iota((rows, 2 * mdim), 1) < mdim
    pairs = [
        jnp.where(first, per_head[:, h : h + 1], per_head[:, h + 1 : h + 2])
        for h in range(0, heads, 2)
    ]
    return jnp.concatenate(pairs, axis=1)


def split_pair(block, mdim):
    first = iota(block.shape, 1) < mdim
    zero = jnp.zeros_like(block)
    return jnp.concatenate([jnp.where(first, block, zero), jnp.where(first, zero, block)], axis=0)


def plane_kernel(*refs):
    *piece_refs, out_ref = refs
    for i, piece_ref in enumerate(piece_refs):
        out_ref[i] = piece_ref[...]


def tile_of(rows):
    return min(32, rows)


def stack_kernel(*refs):
    count = len(refs) // 2
    for ref, out_ref in zip(refs[:count], refs[count:]):
        tiles, wide, head_dim = out_ref.shape
        tile = ref.shape[0] // tiles
        for t in range(tiles):
            for h in range(wide // tile):
                out_ref[t, h * tile : (h + 1) * tile, :] = ref[
                    t * tile : (t + 1) * tile, h * head_dim : (h + 1) * head_dim
                ]


def put_logs(ref, logs):
    heads = logs.shape[1]
    high = logs.astype(BF16).astype(F32)
    middle = (logs - high).astype(BF16).astype(F32)
    low = (logs - high - middle).astype(BF16).astype(F32)
    place = iota((EXTRA, heads), 0)
    split = jnp.where(place == 0, high, jnp.where(place == 1, middle, low))
    wide = jnp.concatenate([split, jnp.zeros((EXTRA, ref.shape[1] - heads), F32)], axis=1)
    ref[ref.shape[0] - EXTRA :, :] = wide.astype(BF16)


def get_logs(ref, heads):
    parts = ref[ref.shape[0] - EXTRA :, 0:heads].astype(F32)
    return parts[0:1, :] + parts[1:2, :] + parts[2:3, :]


def times(logs, start, mdim, state):
    head = iota(logs.shape, 1)
    blocks = []
    for i in range(state.shape[0] // mdim):
        log = jnp.sum(jnp.where(head == start + i, logs, 0.0), axis=1, keepdims=True)
        blocks.append(jnp.exp(log) * state[i * mdim : (i + 1) * mdim, :])
    return jnp.concatenate(blocks, axis=0)


def write_halves(core, logs, scaled_ref, other_ref, keep_ref, give_ref):
    half = keep_ref.shape[0]
    for out_ref, which in ((keep_ref, core), (give_ref, 1 - core)):
        lanes = pl.ds(pl.multiple_of(which * half, half), half)
        out_ref[0:half, :] = tn(scaled_ref[:, lanes], other_ref[...]).astype(BF16)
    put_logs(give_ref, logs)


def state_kernel(
    me_ref,
    input_ref,
    write_ref,
    decay_ref,
    keep_ref,
    give_ref,
    scaled_ref,
    remain_ref,
    grow_ref,
    sum_ref,
    turned_ref,
):
    cumulated, turned = running_sums(decay_ref[...])
    sum_ref[...], turned_ref[...] = cumulated, turned
    mdim = input_ref.shape[1] // cumulated.shape[1]
    last = cumulated[-1:, :]
    remain_ref[...] = spread_heads(jnp.exp(last - cumulated), mdim)
    grow_ref[...] = spread_heads(jnp.exp(cumulated), mdim)
    scaled_ref[...] = (input_ref[...].astype(F32) * remain_ref[...]).astype(BF16)
    write_halves(me_ref[0] % 2, last, scaled_ref, write_ref, keep_ref, give_ref)


def chip_kernel(reverse, me_ref, sum_ref, keep_ref, got_ref, *rest):
    *out_refs, total_ref = rest
    heads = sum_ref.shape[1]
    half = keep_ref.shape[0]
    mdim = 2 * half // heads
    core = me_ref[0] % 2
    chip = me_ref[0] // 2 % len(out_refs)
    slice_rows = out_refs[0].shape[0] - EXTRA
    own_logs = sum_ref[sum_ref.shape[0] - 1 :, :]
    got_logs = get_logs(got_ref, heads)
    keep, got = keep_ref[...].astype(F32), got_ref[0:half, :].astype(F32)
    first = core == (1 if reverse else 0)
    decayed = times(jnp.where(first, got_logs, own_logs), core * heads // 2, mdim, jnp.where(first, keep, got))
    total_ref[...] = decayed + jnp.where(first, got, keep)
    for k, out_ref in enumerate(out_refs):
        start = pl.multiple_of((chip ^ k) * slice_rows, slice_rows)
        out_ref[0:slice_rows, :] = total_ref[pl.ds(start, slice_rows), :].astype(BF16)
        put_logs(out_ref, own_logs + got_logs)


def steps(count, reverse):
    return range(count - 1, -1, -1) if reverse else range(count)


def ordered(chip, part_refs, order_ref):
    for k, part_ref in enumerate(part_refs):
        order_ref[chip ^ k] = part_ref[...]


def advance(order_ref, source, start, heads, mdim, state):
    part_ref = order_ref.at[source]
    rows = state.shape[0]
    return times(get_logs(part_ref, heads), start, mdim, state) + part_ref[0:rows, :].astype(F32)


def total_kernel(reverse, heads, mdim, me_ref, *rest):
    *part_refs, out_ref, order_ref = rest
    count = len(part_refs)
    chip = me_ref[0] // 2 % count
    ordered(chip, part_refs, order_ref)
    start = me_ref[0] % 2 * (heads // 2) + chip * (heads // 2 // count)
    state = jnp.zeros(out_ref.shape, F32)
    for source in steps(count, reverse):
        state = advance(order_ref, source, start, heads, mdim, state)
    out_ref[...] = state.astype(BF16)


def scan_kernel(reverse, heads, mdim, me_ref, carry_ref, *rest):
    *refs, order_ref, result_ref = rest
    count = len(refs) // 2
    chip = me_ref[0] // 2 % count
    ordered(chip, refs[:count], order_ref)
    start = me_ref[0] % 2 * (heads // 2) + chip * (heads // 2 // count)
    state = carry_ref[...].astype(F32)
    for source in steps(count, reverse):
        result_ref[source] = state.astype(BF16)
        state = advance(order_ref, source, start, heads, mdim, state)
    for k, out_ref in enumerate(refs[count:]):
        out_ref[...] = result_ref[chip ^ k]


def core_kernel(reverse, me_ref, sum_ref, keep_ref, got_ref, *rest):
    *part_refs, mine_ref, send_ref, order_ref = rest
    count = len(part_refs)
    heads = sum_ref.shape[1]
    half = keep_ref.shape[0]
    core = me_ref[0] % 2
    chip = me_ref[0] // 2 % count
    slice_rows = part_refs[0].shape[0]
    for k, part_ref in enumerate(part_refs):
        start = pl.multiple_of((chip ^ k) * slice_rows, slice_rows)
        order_ref[pl.ds(start, slice_rows), :] = part_ref[...]
    first = core == (1 if reverse else 0)
    logs = jnp.where(first, sum_ref[sum_ref.shape[0] - 1 :, :], get_logs(got_ref, heads))
    own = jnp.where(first, keep_ref[...].astype(F32), got_ref[0:half, :].astype(F32))
    incoming = order_ref[...].astype(F32)
    passed = times(logs, core * heads // 2, 2 * half // heads, incoming) + own
    mine_ref[...] = jnp.where(first, incoming, passed).astype(BF16)
    send_ref[...] = jnp.where(first, passed, incoming).astype(BF16)


def whole_state(me_ref, mine_ref, other_ref, both_ref):
    core = me_ref[0] % 2
    both_ref[core] = mine_ref[...]
    both_ref[1 - core] = other_ref[...]
    _, half, nstate = both_ref.shape
    return both_ref[...].reshape(2 * half, nstate)


def mixer_kernel(
    me_ref,
    input_ref,
    write_ref,
    read_ref,
    sum_ref,
    turned_ref,
    grow_ref,
    gate_ref,
    mine_ref,
    other_ref,
    gated_ref,
    inverse_ref,
    active_ref,
    slope_ref,
    both_ref,
    out_ref,
):
    rows, channels = input_ref.shape
    mheads = sum_ref.shape[1]
    mdim = channels // mheads
    cumulated, turned = sum_ref[...], turned_ref[...]
    carried = nt(read_ref[...], whole_state(me_ref, mine_ref, other_ref, both_ref))
    out_ref[...] = grow_ref[...] * carried
    products = nt(read_ref[...], write_ref[...])
    causal = iota((rows, rows), 0) >= iota((rows, rows), 1)

    def weights_of(head):
        spread = cumulated[:, head : head + 1] - turned[head : head + 1, :]
        return (jnp.exp(jnp.where(causal, spread, -jnp.inf)) * products).astype(BF16)

    for pair in range(mheads // 2):
        lanes = slice(pair * 2 * mdim, (pair + 1) * 2 * mdim)
        weights = jnp.concatenate([weights_of(2 * pair), weights_of(2 * pair + 1)], axis=1)
        out_ref[:, lanes] += nn(weights, split_pair(input_ref[:, lanes], mdim))

    mixer_out = out_ref[...]
    gate = gate_ref[...].astype(F32)
    sigmoid = jax.nn.sigmoid(gate)
    active = gate * sigmoid
    gated = mixer_out * active
    active_ref[...] = active
    gated_ref[...] = gated
    slope_ref[...] = mixer_out * sigmoid * (1.0 + gate * (1.0 - sigmoid))
    inverse = lax.rsqrt(jnp.mean(gated * gated, axis=-1, keepdims=True) + EPSILON)
    inverse_ref[...] = jnp.broadcast_to(inverse, inverse_ref.shape)


def attention_kernel(
    in_kernel, ctx_size, me_ref, query_ref, grad_ref, *rest
):
    plane_refs, rest = rest[:4], rest[4:]
    if in_kernel:
        keep_ref, give_ref, gathered_ref, acc_ref, raw_ref, back_ref, query_acc_ref = rest
    else:
        query_out_ref, pack_ref, gathered_ref, acc_ref, raw_ref, back_ref = rest
    tiles, wide, head_dim = query_ref.shape
    rows = gathered_ref.shape[1]
    tile = rows // tiles
    heads = wide // tile
    me = me_ref[0]
    scale = 1.0 / math.sqrt(head_dim)
    base2 = scale * math.log2(math.e)
    per = rows // ctx_size
    for offset, plane_ref in enumerate(plane_refs):
        for level in range(ctx_size // 4):
            gathered_ref[me ^ (4 * level + offset)] = plane_ref[level]

    def keys_of(b):
        return gathered_ref[:, b * tile : (b + 1) * tile, 0:head_dim].reshape(
            ctx_size * tile, head_dim
        )

    def values_of(b):
        return gathered_ref[:, b * tile : (b + 1) * tile, head_dim : 2 * head_dim].reshape(
            ctx_size * tile, head_dim
        )

    key_row = iota((ctx_size * tile, wide), 0)
    key_place = (key_row % tile) * ctx_size + key_row // tile
    query_place = (iota((ctx_size * tile, wide), 1) % tile) * ctx_size + me
    visible = key_place <= query_place

    for t in range(tiles - 1, -1, -1):
        query = query_ref[t]
        grad = grad_ref[t]
        highest = None
        for b in range(t, -1, -1):
            raw = nt(keys_of(b), query)
            if b == t:
                raw = jnp.where(visible, raw, -jnp.inf)
            raw_ref[b] = raw
            block_high = jnp.max(raw, axis=0, keepdims=True)
            highest = block_high if highest is None else jnp.maximum(highest, block_high)
        total = jnp.zeros((1, wide), F32)
        delta = jnp.zeros((1, wide), F32)
        for b in range(t + 1):
            probs = jnp.exp2((raw_ref[b] - highest) * base2)
            back = nt(values_of(b), grad)
            raw_ref[b] = probs
            back_ref[b] = back
            total = total + jnp.sum(probs, axis=0, keepdims=True)
            delta = delta + jnp.sum(probs * back, axis=0, keepdims=True)
        inverse = 1.0 / total
        delta = delta * inverse
        query_grad = jnp.zeros((head_dim, wide), F32)
        for b in range(t + 1):
            weights = raw_ref[b] * inverse
            score_grad = (weights * (back_ref[b] - delta)).astype(BF16)
            value_part = nn(weights.astype(BF16), grad).reshape(ctx_size, tile, head_dim)
            key_part = nn(score_grad, query).reshape(ctx_size, tile, head_dim)
            here = slice(b * tile, (b + 1) * tile)
            if t == tiles - 1:
                acc_ref[:, here, 0:head_dim] = key_part
                acc_ref[:, here, head_dim:] = value_part
            else:
                acc_ref[:, here, 0:head_dim] += key_part
                acc_ref[:, here, head_dim:] += value_part
            query_grad = query_grad + tn(keys_of(b), score_grad)
        turned = (query_grad * scale).T
        by_head = [turned[h * tile : (h + 1) * tile, :] for h in range(heads)]
        if in_kernel:
            pairs = [
                jnp.concatenate(by_head[h : h + 2], axis=1) for h in range(0, heads, 2)
            ]
            for k in range(tile // per):
                rows_here = [p[k * per : (k + 1) * per, :] for p in pairs]
                query_acc_ref[t * (tile // per) + k] = jnp.concatenate(rows_here, axis=0)
        else:
            for h in range(heads):
                query_out_ref[t * tile : (t + 1) * tile, h * head_dim : (h + 1) * head_dim] = (
                    by_head[h].astype(BF16)
                )

    both = jnp.where(iota((1, 1, 2 * head_dim), 2) < head_dim, scale, 1.0)
    if in_kernel:
        for chip in range(ctx_size // 2):
            for out_ref, core in ((keep_ref, me % 2), (give_ref, 1 - me % 2)):
                target = 2 * chip + core
                start = pl.multiple_of(target * per, per)
                block = acc_ref[:, pl.ds(start, per), :] * both
                out_ref[chip, 0:rows, :] = block.reshape(rows, 2 * head_dim).astype(BF16)
                out_ref[chip, rows:, :] = query_acc_ref[target].astype(BF16)
    else:
        pack_ref[...] = (acc_ref[...] * both).astype(BF16)


def join_kernel(me_ref, keep_ref, got_ref, *out_refs):
    mid = keep_ref.shape[1]
    rows = 2 * mid - out_refs[0].shape[0]
    chip = me_ref[0] // 2
    for k, out_ref in enumerate(out_refs):
        target = chip ^ k
        both = keep_ref[target, 0:rows, :].astype(F32) + got_ref[target, 0:rows, :].astype(F32)
        out_ref[0:rows, :] = both.astype(BF16)
        out_ref[rows:mid, :] = keep_ref[target, rows:, :]
        out_ref[mid:, :] = got_ref[target, rows:, :]


def in_token_order(ctx_size, devices, grads):
    rows = grads.shape[0]
    per = rows // ctx_size
    token, came = iota((rows, rows), 0), iota((rows, rows), 1)
    order = (token == (came % per) * ctx_size + devices(came // per)).astype(BF16)
    return nn(order, grads).astype(BF16)


def gate_kernel(
    order,
    me_ref,
    weight_ref,
    gated_ref,
    inverse_ref,
    active_ref,
    slope_ref,
    gain_ref,
    read_ref,
    grow_ref,
    sum_ref,
    *rest,
):
    *part_refs, gate_out_ref, grad_out_ref, keep_ref, give_ref, grown_ref = rest
    rows = gated_ref.shape[0]
    chips = len(part_refs)
    ctx_size = 2 * chips
    per = rows // ctx_size
    part_refs = [part_refs[order.index(k)] for k in range(chips)]
    me = me_ref[0]
    sums = part_refs[0][0:rows, :].astype(F32)
    for part_ref in part_refs[1:]:
        sums = sums + part_ref[0:rows, :].astype(F32)
    kv_grads = in_token_order(ctx_size, lambda place: place, sums.astype(BF16))
    extra = (part_refs[0].shape[0] - rows) // 2
    query_rows = [part_ref[rows:, :].astype(F32) for part_ref in part_refs]
    columns = []
    for part in range(extra // per):
        blocks = [
            block[core * extra + part * per : core * extra + (part + 1) * per, :]
            for core in range(2)
            for block in query_rows
        ]
        columns.append(jnp.concatenate(blocks, axis=0))
    query_grads = in_token_order(
        ctx_size,
        lambda place: (2 * (place % chips) + place // chips) ^ me,
        jnp.concatenate(columns, axis=1).astype(BF16),
    )
    grads = jnp.concatenate([query_grads, kv_grads], axis=1)
    mixer_grad = nt(grads, weight_ref[...]).astype(BF16).astype(F32)

    gated = gated_ref[...]
    inverse = inverse_ref[:, 0:1]
    scaled = gain_ref[...] * mixer_grad
    mean = jnp.mean(scaled * gated, axis=-1, keepdims=True)
    gated_grad = scaled * inverse - gated * (mean * inverse * inverse * inverse)
    gate_out_ref[...] = gated_grad * slope_ref[...]
    out_grad = (gated_grad * active_ref[...]).astype(BF16)
    grad_out_ref[...] = out_grad
    grown_ref[...] = (out_grad.astype(F32) * grow_ref[...]).astype(BF16)
    last = sum_ref[rows - 1 :, :]
    write_halves(me % 2, last, grown_ref, read_ref, keep_ref, give_ref)


def local_kernel(
    me_ref,
    grad_ref,
    grown_ref,
    input_ref,
    write_ref,
    read_ref,
    sum_ref,
    turned_ref,
    mine_ref,
    other_ref,
    value_ref,
    write_out_ref,
    read_out_ref,
    both_ref,
):
    rows, channels = input_ref.shape
    mheads = sum_ref.shape[1]
    mdim = channels // mheads
    cumulated, turned = sum_ref[...], turned_ref[...]
    turned_products = nt(write_ref[...], read_ref[...])
    causal = iota((rows, rows), 0) >= iota((rows, rows), 1)
    later = iota((rows, rows), 0) <= iota((rows, rows), 1)
    pair_sum = jnp.zeros((rows, rows), F32)

    def decays_of(head):
        spread = cumulated[:, head : head + 1] - turned[head : head + 1, :]
        return jnp.exp(jnp.where(causal, spread, -jnp.inf))

    def turned_weights_of(head):
        spread = turned[head : head + 1, :] - cumulated[:, head : head + 1]
        return (jnp.exp(jnp.where(later, spread, -jnp.inf)) * turned_products).astype(BF16)

    for pair in range(mheads // 2):
        lanes = slice(pair * 2 * mdim, (pair + 1) * 2 * mdim)
        grads = split_pair(grad_ref[:, lanes], mdim)
        weights = jnp.concatenate(
            [turned_weights_of(2 * pair), turned_weights_of(2 * pair + 1)], axis=1
        )
        value_ref[:, lanes] = nn(weights, grads)
        pairs = nt(grads, input_ref[:, lanes])
        pair_sum = (
            pair_sum + decays_of(2 * pair) * pairs[:rows] + decays_of(2 * pair + 1) * pairs[rows:]
        )
    pair_low = pair_sum.astype(BF16)
    incoming = whole_state(me_ref, mine_ref, other_ref, both_ref)
    read_out_ref[...] = nn(pair_low, write_ref[...]) + nn(grown_ref[...], incoming)
    write_out_ref[...] = tn(pair_low, read_ref[...])


def final_kernel(
    me_ref,
    value_ref,
    write_part_ref,
    scaled_ref,
    remain_ref,
    write_ref,
    mine_ref,
    other_ref,
    out_ref,
    write_out_ref,
    both_ref,
):
    adjoint = whole_state(me_ref, mine_ref, other_ref, both_ref)
    out_ref[...] = value_ref[...] + remain_ref[...] * nt(write_ref[...], adjoint)
    write_out_ref[...] = write_part_ref[...] + nn(scaled_ref[...], adjoint)


def crossed(array, bits):
    pairs = [(i, i ^ bits) for i in range(lax.axis_size("ctx"))]
    return lax.ppermute(array, "ctx", pairs)


def tied(arrays, after):
    return lax.optimization_barrier((arrays, after))[0]


def scan_slices(me, cumulated, keep, give, reverse):
    group = lax.axis_size("ctx") // 4
    half_rows, nstate = keep.shape
    got = crossed(give, 1)
    slices = call(
        functools.partial(chip_kernel, reverse),
        [struct((half_rows // group + EXTRA, nstate), BF16)] * group,
        [me, cumulated, keep, got],
        half_rows * nstate,
        smem=(0,),
        scratch=[pltpu.VMEM((half_rows, nstate), F32)],
    )
    return slices, got


def scan_parts(slices):
    return [slices[0]] + [crossed(slices[k], 2 * k) for k in range(1, len(slices))]


def scan_total(me, cumulated, keep, parts, reverse):
    group = len(parts)
    half_rows, nstate = keep.shape
    slice_rows = half_rows // group
    heads = cumulated.shape[1]
    (total,) = call(
        functools.partial(total_kernel, reverse, heads, 2 * half_rows // heads),
        [struct((slice_rows, nstate), BF16)],
        [me] + list(parts),
        half_rows * nstate,
        smem=(0,),
        scratch=[pltpu.VMEM((group, slice_rows + EXTRA, nstate), BF16)],
    )
    return total


def scan_carry(total, reverse):
    half = lax.axis_size("ctx") // 2
    if reverse:
        pairs = [(i + half, i) for i in range(half)]
    else:
        pairs = [(i, i + half) for i in range(half)]
    return lax.ppermute(total, "ctx", pairs)


def scan_back(me, cumulated, carry, keep, parts, reverse):
    group = len(parts)
    slice_rows, nstate = carry.shape
    heads = cumulated.shape[1]
    backs = call(
        functools.partial(scan_kernel, reverse, heads, 2 * keep.shape[0] // heads),
        [struct(carry.shape, BF16)] * group,
        [me, carry] + list(parts),
        group * slice_rows * nstate,
        smem=(0,),
        scratch=[
            pltpu.VMEM((group, slice_rows + EXTRA, nstate), BF16),
            pltpu.VMEM((group, slice_rows, nstate), BF16),
        ],
    )
    return backs


def scan_out(me, cumulated, returned, keep, got, reverse):
    mine, send = call(
        functools.partial(core_kernel, reverse),
        [struct(keep.shape, BF16)] * 2,
        [me, cumulated, keep, got] + list(returned),
        keep.size,
        smem=(0,),
        scratch=[pltpu.VMEM(keep.shape, BF16)],
    )
    return mine, crossed(send, 1)


def body(
    queries,
    keys,
    values,
    d_out,
    mixer_input,
    gate_input,
    state_write,
    state_read,
    log_decay,
    norm_gain,
    project_weight,
):
    ctx_size = lax.axis_size("ctx")
    ctx_index = lax.axis_index("ctx")
    rows, head_dim = keys.shape
    wide = queries.shape[1]
    channels = mixer_input.shape[1]
    nstate = state_write.shape[1]
    mheads = log_decay.shape[1]
    per = rows // ctx_size
    me = ctx_index.astype(jnp.int32).reshape(1)
    packed = jnp.pad(keys, ((0, 0), (0, head_dim))) + jnp.pad(values, ((0, 0), (head_dim, 0)))
    near_plane = [packed] + [crossed(packed, k) for k in range(4, ctx_size, 4)]
    (plane,) = call(
        plane_kernel,
        [struct((ctx_size // 4, rows, 2 * head_dim), BF16)],
        near_plane,
        rows * head_dim,
    )
    plane_other = crossed(plane, 1)
    half_states = [
        struct((channels // 2, nstate), BF16),
        struct((channels // 2 + EXTRA, nstate), BF16),
    ]
    tile = tile_of(rows)
    columns = tile * wide // head_dim
    stacked = struct((rows // tile, columns, head_dim), BF16)
    keep, give, scaled, remain, grow, cumulated, turned = call(
        state_kernel,
        [
            *half_states,
            struct((rows, channels), BF16),
            struct((rows, channels), F32),
            struct((rows, channels), F32),
            struct((rows, mheads), F32),
            struct((mheads, rows), F32),
        ],
        [me, mixer_input, state_write, tied(log_decay.T, packed)],
        2 * rows * channels * nstate,
        smem=(0,),
    )

    query_tiles, grad_tiles = call(
        stack_kernel, [stacked, stacked], [queries, d_out], rows * wide
    )
    slices, got = scan_slices(me, cumulated, keep, give, False)
    parts = scan_parts(slices)
    across = crossed(plane, 2)
    across_other = crossed(tied(across, (tuple(parts[1:]), query_tiles)), 1)

    total = scan_total(me, cumulated, keep, parts, False)
    carry = scan_carry(total, False)
    query_tiles = tied(query_tiles, total)

    in_kernel = per % 8 == 0
    flops = 10 * rows * wide * ctx_size * rows
    scratch = [
        pltpu.VMEM((ctx_size, rows, 2 * head_dim), BF16),
        pltpu.VMEM((ctx_size, rows, 2 * head_dim), F32),
        pltpu.VMEM((rows // tile, ctx_size * tile, columns), F32),
        pltpu.VMEM((rows // tile, ctx_size * tile, columns), F32),
    ]
    attention_args = [me, query_tiles, grad_tiles, plane, plane_other, across, across_other]
    chips = ctx_size // 2
    extra = per * wide // (2 * head_dim)
    if in_kernel:
        part = struct((chips, rows + extra, 2 * head_dim), BF16)
        kv_keep, kv_give = call(
            functools.partial(attention_kernel, True, ctx_size),
            [part, part],
            attention_args,
            flops,
            smem=(0,),
            scratch=scratch + [pltpu.VMEM((ctx_size, extra, 2 * head_dim), F32)],
        )
    else:
        query_grad, kv_grad = call(
            functools.partial(attention_kernel, False, ctx_size),
            [struct((rows, wide), BF16), struct((ctx_size, rows, 2 * head_dim), BF16)],
            attention_args,
            flops,
            smem=(0,),
            scratch=scratch,
        )
        by_target = kv_grad.reshape(ctx_size, ctx_size, per, 2 * head_dim).transpose(1, 0, 2, 3)
        by_pair = query_grad.reshape(ctx_size, per, -1, 2 * head_dim).transpose(0, 2, 1, 3)
        sent = jnp.concatenate(
            [
                by_target.reshape(ctx_size, rows, 2 * head_dim),
                by_pair.reshape(ctx_size, extra, 2 * head_dim),
            ],
            axis=1,
        ).reshape(chips, 2, rows + extra, 2 * head_dim)
        kv_keep = lax.dynamic_index_in_dim(sent, ctx_index % 2, 1, False)
        kv_give = lax.dynamic_index_in_dim(sent, 1 - ctx_index % 2, 1, False)

    carry, kv_keep, kv_give = lax.optimization_barrier((carry, kv_keep, kv_give))
    kv_got = crossed(kv_give, 1)
    backs = scan_back(me, cumulated, carry, keep, parts, False)
    sent = call(
        join_kernel,
        [struct((rows + 2 * extra, 2 * head_dim), BF16)] * chips,
        [me, kv_keep, tied(kv_got, backs[0])],
        chips * rows * 2 * head_dim,
        smem=(0,),
    )
    order = sorted(range(chips), key=lambda k: (-(k // 4), k % 2, -k))
    received = [crossed(sent[k], 2 * k) if k else sent[k] for k in order]
    returned = tied(tuple(scan_parts(backs)), tuple(received[:3]))
    incoming, incoming_other = scan_out(me, cumulated, returned, keep, got, False)

    both_states = pltpu.VMEM((2, channels // 2, nstate), BF16)
    whole = struct((rows, channels), F32)
    gated, inverse, active, slope = call(
        mixer_kernel,
        [whole, struct((rows, 128), F32), whole, whole],
        [
            me,
            mixer_input,
            state_write,
            state_read,
            cumulated,
            turned,
            grow,
            gate_input,
            incoming,
            incoming_other,
        ],
        2 * rows * channels * (nstate + rows),
        smem=(0,),
        scratch=[both_states, pltpu.VMEM((rows, channels), F32)],
    )
    gate_gradient, out_grad, adjoint_keep, adjoint_give, grown = call(
        functools.partial(gate_kernel, order),
        [
            struct((rows, channels), F32),
            struct((rows, channels), BF16),
            *half_states,
            struct((rows, channels), BF16),
        ],
        [
            me,
            project_weight,
            gated,
            inverse,
            active,
            slope,
            norm_gain.reshape(1, channels),
            state_read,
            grow,
            cumulated,
        ]
        + received,
        2 * rows * channels * (nstate + project_weight.shape[1]),
        smem=(0,),
    )
    value_part, write_part, read_gradient = call(
        local_kernel,
        [
            struct((rows, channels), F32),
            struct((rows, nstate), F32),
            struct((rows, nstate), F32),
        ],
        [
            me,
            out_grad,
            grown,
            mixer_input,
            state_write,
            state_read,
            cumulated,
            turned,
            incoming,
            incoming_other,
        ],
        2 * rows * channels * (nstate + 2 * rows),
        smem=(0,),
        scratch=[both_states],
    )
    slices, got = scan_slices(me, cumulated, adjoint_keep, adjoint_give, True)
    parts = scan_parts(slices)
    carry = scan_carry(scan_total(me, cumulated, adjoint_keep, parts, True), True)
    carry = tied(carry, write_part)
    backs = scan_back(me, cumulated, carry, adjoint_keep, parts, True)
    adjoint, adjoint_other = scan_out(
        me, cumulated, scan_parts(backs), adjoint_keep, got, True
    )
    input_gradient, write_gradient = call(
        final_kernel,
        [struct((rows, channels), F32), struct((rows, nstate), F32)],
        [
            me,
            value_part,
            write_part,
            scaled,
            remain,
            state_write,
            adjoint,
            adjoint_other,
        ],
        4 * rows * channels * nstate,
        smem=(0,),
        scratch=[both_states],
    )
    return (input_gradient, gate_gradient, write_gradient, read_gradient)


def solution(mesh):
    both = P("ctx", "groups")
    return jax.shard_map(
        body,
        mesh=mesh,
        in_specs=(both,) * 9 + (P("groups"), P(None, "groups")),
        out_specs=(both,) * 4,
        check_vma=False,
    )
```

```python
import functools
import math

import jax
import jax.numpy as jnp
from jax import lax
from jax.experimental import pallas as pl
from jax.experimental.pallas import tpu as pltpu
from jax.sharding import PartitionSpec as P

EPSILON = 1e-05
HIGHEST = lax.Precision.HIGHEST
F32 = jnp.float32
BF16 = jnp.bfloat16
EXTRA = 16
MIB = 1024 * 1024


def nn(a, b, **kw):
    return lax.dot_general(a, b, (((1,), (0,)), ((), ())), preferred_element_type=F32, **kw)


def nt(a, b, **kw):
    return lax.dot_general(a, b, (((1,), (1,)), ((), ())), preferred_element_type=F32, **kw)


def tn(a, b, **kw):
    return lax.dot_general(a, b, (((0,), (0,)), ((), ())), preferred_element_type=F32, **kw)


def iota(shape, dim):
    return lax.broadcasted_iota(jnp.int32, shape, dim)


def call(kernel, outs, args, flops, smem=(), scratch=(), spare=4 * MIB):
    specs = [
        pl.BlockSpec(memory_space=pltpu.SMEM if i in smem else pltpu.VMEM) for i in range(len(args))
    ]
    moved = sum(a.size * a.dtype.itemsize for a in args) + sum(
        math.prod(o.shape) * o.dtype.itemsize for o in outs
    )
    held = moved + sum(
        math.prod(s.shape) * jnp.dtype(s.dtype).itemsize for s in scratch
    )
    return pl.pallas_call(
        kernel,
        out_shape=tuple(outs),
        in_specs=specs,
        out_specs=tuple(pl.BlockSpec(memory_space=pltpu.VMEM) for _ in outs),
        scratch_shapes=list(scratch),
        compiler_params=pltpu.CompilerParams(vmem_limit_bytes=held + spare),
        cost_estimate=pl.CostEstimate(flops=flops, bytes_accessed=moved, transcendentals=0),
    )(*args)


def struct(shape, dtype):
    return jax.ShapeDtypeStruct(shape, dtype)


def running_sums(log_decay):
    rows = log_decay.shape[1]
    lower = (iota((rows, rows), 0) >= iota((rows, rows), 1)).astype(F32)
    upper = (iota((rows, rows), 0) <= iota((rows, rows), 1)).astype(F32)
    return nt(lower, log_decay, precision=HIGHEST), nn(log_decay, upper, precision=HIGHEST)


def spread_heads(per_head, mdim):
    rows, heads = per_head.shape
    first = iota((rows, 2 * mdim), 1) < mdim
    pairs = [
        jnp.where(first, per_head[:, h : h + 1], per_head[:, h + 1 : h + 2])
        for h in range(0, heads, 2)
    ]
    return jnp.concatenate(pairs, axis=1)


def split_pair(block, mdim):
    first = iota(block.shape, 1) < mdim
    zero = jnp.zeros_like(block)
    return jnp.concatenate([jnp.where(first, block, zero), jnp.where(first, zero, block)], axis=0)


def plane_kernel(*refs):
    *piece_refs, out_ref = refs
    for i, piece_ref in enumerate(piece_refs):
        out_ref[i] = piece_ref[...]


def tile_of(rows):
    return min(32, rows)


def stack_kernel(*refs):
    count = len(refs) // 2
    for ref, out_ref in zip(refs[:count], refs[count:]):
        tiles, wide, head_dim = out_ref.shape
        tile = ref.shape[0] // tiles
        for t in range(tiles):
            for h in range(wide // tile):
                out_ref[t, h * tile : (h + 1) * tile, :] = ref[
                    t * tile : (t + 1) * tile, h * head_dim : (h + 1) * head_dim
                ]


def put_logs(ref, logs):
    heads = logs.shape[1]
    high = logs.astype(BF16).astype(F32)
    middle = (logs - high).astype(BF16).astype(F32)
    low = (logs - high - middle).astype(BF16).astype(F32)
    place = iota((EXTRA, heads), 0)
    split = jnp.where(place == 0, high, jnp.where(place == 1, middle, low))
    wide = jnp.concatenate([split, jnp.zeros((EXTRA, ref.shape[1] - heads), F32)], axis=1)
    ref[ref.shape[0] - EXTRA :, :] = wide.astype(BF16)


def get_logs(ref, heads):
    parts = ref[ref.shape[0] - EXTRA :, 0:heads].astype(F32)
    return parts[0:1, :] + parts[1:2, :] + parts[2:3, :]


def times(logs, start, mdim, state):
    head = iota(logs.shape, 1)
    blocks = []
    for i in range(state.shape[0] // mdim):
        log = jnp.sum(jnp.where(head == start + i, logs, 0.0), axis=1, keepdims=True)
        blocks.append(jnp.exp(log) * state[i * mdim : (i + 1) * mdim, :])
    return jnp.concatenate(blocks, axis=0)


def write_halves(core, logs, scaled_ref, other_ref, keep_ref, give_ref):
    half = keep_ref.shape[0]
    for out_ref, which in ((keep_ref, core), (give_ref, 1 - core)):
        lanes = pl.ds(pl.multiple_of(which * half, half), half)
        out_ref[0:half, :] = tn(scaled_ref[:, lanes], other_ref[...]).astype(BF16)
    put_logs(give_ref, logs)


def state_kernel(
    me_ref,
    input_ref,
    write_ref,
    decay_ref,
    keep_ref,
    give_ref,
    scaled_ref,
    remain_ref,
    grow_ref,
    sum_ref,
    turned_ref,
):
    cumulated, turned = running_sums(decay_ref[...])
    sum_ref[...], turned_ref[...] = cumulated, turned
    mdim = input_ref.shape[1] // cumulated.shape[1]
    last = cumulated[-1:, :]
    remain_ref[...] = spread_heads(jnp.exp(last - cumulated), mdim)
    grow_ref[...] = spread_heads(jnp.exp(cumulated), mdim)
    scaled_ref[...] = (input_ref[...].astype(F32) * remain_ref[...]).astype(BF16)
    write_halves(me_ref[0] % 2, last, scaled_ref, write_ref, keep_ref, give_ref)


def chip_kernel(reverse, me_ref, sum_ref, keep_ref, got_ref, *rest):
    *out_refs, total_ref = rest
    heads = sum_ref.shape[1]
    half = keep_ref.shape[0]
    mdim = 2 * half // heads
    core = me_ref[0] % 2
    chip = me_ref[0] // 2 % len(out_refs)
    slice_rows = out_refs[0].shape[0] - EXTRA
    own_logs = sum_ref[sum_ref.shape[0] - 1 :, :]
    got_logs = get_logs(got_ref, heads)
    keep, got = keep_ref[...].astype(F32), got_ref[0:half, :].astype(F32)
    first = core == (1 if reverse else 0)
    decayed = times(jnp.where(first, got_logs, own_logs), core * heads // 2, mdim, jnp.where(first, keep, got))
    total_ref[...] = decayed + jnp.where(first, got, keep)
    for k, out_ref in enumerate(out_refs):
        start = pl.multiple_of((chip ^ k) * slice_rows, slice_rows)
        out_ref[0:slice_rows, :] = total_ref[pl.ds(start, slice_rows), :].astype(BF16)
        put_logs(out_ref, own_logs + got_logs)


def steps(count, reverse):
    return range(count - 1, -1, -1) if reverse else range(count)


def by_offset(part_refs):
    return [part_refs[0], *part_refs[:0:-1]]


def ordered(chip, part_refs, order_ref):
    for k, part_ref in enumerate(by_offset(part_refs)):
        order_ref[chip ^ k] = part_ref[...]


def advance(order_ref, source, start, heads, mdim, state):
    part_ref = order_ref.at[source]
    rows = state.shape[0]
    return times(get_logs(part_ref, heads), start, mdim, state) + part_ref[0:rows, :].astype(F32)


def total_kernel(reverse, heads, mdim, me_ref, *rest):
    *part_refs, out_ref, order_ref = rest
    count = len(part_refs)
    chip = me_ref[0] // 2 % count
    ordered(chip, part_refs, order_ref)
    start = me_ref[0] % 2 * (heads // 2) + chip * (heads // 2 // count)
    state = jnp.zeros(out_ref.shape, F32)
    for source in steps(count, reverse):
        state = advance(order_ref, source, start, heads, mdim, state)
    out_ref[...] = state.astype(BF16)


def scan_kernel(reverse, heads, mdim, me_ref, carry_ref, *rest):
    *refs, order_ref, result_ref = rest
    count = len(refs) // 2
    chip = me_ref[0] // 2 % count
    ordered(chip, refs[:count], order_ref)
    start = me_ref[0] % 2 * (heads // 2) + chip * (heads // 2 // count)
    state = carry_ref[...].astype(F32)
    for source in steps(count, reverse):
        result_ref[source] = state.astype(BF16)
        state = advance(order_ref, source, start, heads, mdim, state)
    for k, out_ref in enumerate(refs[count:]):
        out_ref[...] = result_ref[chip ^ k]


def core_kernel(reverse, me_ref, sum_ref, keep_ref, got_ref, *rest):
    *part_refs, mine_ref, send_ref, order_ref = rest
    count = len(part_refs)
    heads = sum_ref.shape[1]
    half = keep_ref.shape[0]
    core = me_ref[0] % 2
    chip = me_ref[0] // 2 % count
    slice_rows = part_refs[0].shape[0]
    for k, part_ref in enumerate(by_offset(part_refs)):
        start = pl.multiple_of((chip ^ k) * slice_rows, slice_rows)
        order_ref[pl.ds(start, slice_rows), :] = part_ref[...]
    first = core == (1 if reverse else 0)
    logs = jnp.where(first, sum_ref[sum_ref.shape[0] - 1 :, :], get_logs(got_ref, heads))
    own = jnp.where(first, keep_ref[...].astype(F32), got_ref[0:half, :].astype(F32))
    incoming = order_ref[...].astype(F32)
    passed = times(logs, core * heads // 2, 2 * half // heads, incoming) + own
    mine_ref[...] = jnp.where(first, incoming, passed).astype(BF16)
    send_ref[...] = jnp.where(first, passed, incoming).astype(BF16)


def whole_state(me_ref, mine_ref, other_ref, both_ref):
    core = me_ref[0] % 2
    both_ref[core] = mine_ref[...]
    both_ref[1 - core] = other_ref[...]
    _, half, nstate = both_ref.shape
    return both_ref[...].reshape(2 * half, nstate)


def mixer_kernel(
    me_ref,
    input_ref,
    write_ref,
    read_ref,
    sum_ref,
    turned_ref,
    grow_ref,
    gate_ref,
    mine_ref,
    other_ref,
    gated_ref,
    inverse_ref,
    active_ref,
    slope_ref,
    both_ref,
    out_ref,
):
    rows, channels = input_ref.shape
    mheads = sum_ref.shape[1]
    mdim = channels // mheads
    cumulated, turned = sum_ref[...], turned_ref[...]
    carried = nt(read_ref[...], whole_state(me_ref, mine_ref, other_ref, both_ref))
    out_ref[...] = grow_ref[...] * carried
    products = nt(read_ref[...], write_ref[...])
    causal = iota((rows, rows), 0) >= iota((rows, rows), 1)

    def weights_of(head):
        spread = cumulated[:, head : head + 1] - turned[head : head + 1, :]
        return (jnp.exp(jnp.where(causal, spread, -jnp.inf)) * products).astype(BF16)

    for pair in range(mheads // 2):
        lanes = slice(pair * 2 * mdim, (pair + 1) * 2 * mdim)
        weights = jnp.concatenate([weights_of(2 * pair), weights_of(2 * pair + 1)], axis=1)
        out_ref[:, lanes] += nn(weights, split_pair(input_ref[:, lanes], mdim))

    mixer_out = out_ref[...]
    gate = gate_ref[...].astype(F32)
    sigmoid = jax.nn.sigmoid(gate)
    active = gate * sigmoid
    gated = mixer_out * active
    active_ref[...] = active
    gated_ref[...] = gated
    slope_ref[...] = mixer_out * sigmoid * (1.0 + gate * (1.0 - sigmoid))
    inverse = lax.rsqrt(jnp.mean(gated * gated, axis=-1, keepdims=True) + EPSILON)
    inverse_ref[...] = jnp.broadcast_to(inverse, inverse_ref.shape)


def attention_kernel(
    in_kernel, ctx_size, me_ref, query_ref, grad_ref, *rest
):
    plane_refs, rest = rest[:4], rest[4:]
    if in_kernel:
        keep_ref, give_ref, gathered_ref, acc_ref, raw_ref, back_ref, query_acc_ref = rest
    else:
        query_out_ref, pack_ref, gathered_ref, acc_ref, raw_ref, back_ref = rest
    tiles, wide, head_dim = query_ref.shape
    rows = gathered_ref.shape[1]
    tile = rows // tiles
    heads = wide // tile
    me = me_ref[0]
    scale = 1.0 / math.sqrt(head_dim)
    base2 = scale * math.log2(math.e)
    per = rows // ctx_size
    for offset, plane_ref in enumerate(plane_refs):
        for level in range(ctx_size // 4):
            gathered_ref[me ^ (4 * level + offset)] = plane_ref[level]

    def keys_of(b):
        return gathered_ref[:, b * tile : (b + 1) * tile, 0:head_dim].reshape(
            ctx_size * tile, head_dim
        )

    def values_of(b):
        return gathered_ref[:, b * tile : (b + 1) * tile, head_dim : 2 * head_dim].reshape(
            ctx_size * tile, head_dim
        )

    key_row = iota((ctx_size * tile, wide), 0)
    key_place = (key_row % tile) * ctx_size + key_row // tile
    query_place = (iota((ctx_size * tile, wide), 1) % tile) * ctx_size + me
    visible = key_place <= query_place

    for t in range(tiles - 1, -1, -1):
        query = query_ref[t]
        grad = grad_ref[t]
        highest = None
        for b in range(t, -1, -1):
            raw = nt(keys_of(b), query)
            if b == t:
                raw = jnp.where(visible, raw, -jnp.inf)
            raw_ref[b] = raw
            block_high = jnp.max(raw, axis=0, keepdims=True)
            highest = block_high if highest is None else jnp.maximum(highest, block_high)
        total = jnp.zeros((1, wide), F32)
        delta = jnp.zeros((1, wide), F32)
        for b in range(t + 1):
            probs = jnp.exp2((raw_ref[b] - highest) * base2)
            back = nt(values_of(b), grad)
            raw_ref[b] = probs
            back_ref[b] = back
            total = total + jnp.sum(probs, axis=0, keepdims=True)
            delta = delta + jnp.sum(probs * back, axis=0, keepdims=True)
        inverse = 1.0 / total
        delta = delta * inverse
        query_grad = jnp.zeros((head_dim, wide), F32)
        for b in range(t + 1):
            weights = raw_ref[b] * inverse
            score_grad = (weights * (back_ref[b] - delta)).astype(BF16)
            value_part = nn(weights.astype(BF16), grad).reshape(ctx_size, tile, head_dim)
            key_part = nn(score_grad, query).reshape(ctx_size, tile, head_dim)
            here = slice(b * tile, (b + 1) * tile)
            if t == tiles - 1:
                acc_ref[:, here, 0:head_dim] = key_part
                acc_ref[:, here, head_dim:] = value_part
            else:
                acc_ref[:, here, 0:head_dim] += key_part
                acc_ref[:, here, head_dim:] += value_part
            query_grad = query_grad + tn(keys_of(b), score_grad)
        turned = (query_grad * scale).T
        by_head = [turned[h * tile : (h + 1) * tile, :] for h in range(heads)]
        if in_kernel:
            pairs = [
                jnp.concatenate(by_head[h : h + 2], axis=1) for h in range(0, heads, 2)
            ]
            for k in range(tile // per):
                rows_here = [p[k * per : (k + 1) * per, :] for p in pairs]
                query_acc_ref[t * (tile // per) + k] = jnp.concatenate(rows_here, axis=0)
        else:
            for h in range(heads):
                query_out_ref[t * tile : (t + 1) * tile, h * head_dim : (h + 1) * head_dim] = (
                    by_head[h].astype(BF16)
                )

    both = jnp.where(iota((1, 1, 2 * head_dim), 2) < head_dim, scale, 1.0)
    if in_kernel:
        for chip in range(ctx_size // 2):
            for out_ref, core in ((keep_ref, me % 2), (give_ref, 1 - me % 2)):
                target = 2 * chip + core
                start = pl.multiple_of(target * per, per)
                block = acc_ref[:, pl.ds(start, per), :] * both
                out_ref[chip, 0:rows, :] = block.reshape(rows, 2 * head_dim).astype(BF16)
                out_ref[chip, rows:, :] = query_acc_ref[target].astype(BF16)
    else:
        pack_ref[...] = (acc_ref[...] * both).astype(BF16)


def join_kernel(me_ref, keep_ref, got_ref, *out_refs):
    mid = keep_ref.shape[1]
    rows = 2 * mid - out_refs[0].shape[0]
    chip = me_ref[0] // 2
    for k, out_ref in enumerate(out_refs):
        target = chip ^ k
        both = keep_ref[target, 0:rows, :].astype(F32) + got_ref[target, 0:rows, :].astype(F32)
        out_ref[0:rows, :] = both.astype(BF16)
        out_ref[rows:mid, :] = keep_ref[target, rows:, :]
        out_ref[mid:, :] = got_ref[target, rows:, :]


def in_token_order(ctx_size, devices, grads):
    rows = grads.shape[0]
    per = rows // ctx_size
    token, came = iota((rows, rows), 0), iota((rows, rows), 1)
    order = (token == (came % per) * ctx_size + devices(came // per)).astype(BF16)
    return nn(order, grads).astype(BF16)


def gate_kernel(
    order,
    me_ref,
    weight_ref,
    gated_ref,
    inverse_ref,
    active_ref,
    slope_ref,
    gain_ref,
    read_ref,
    grow_ref,
    sum_ref,
    *rest,
):
    *part_refs, gate_out_ref, grad_out_ref, keep_ref, give_ref, grown_ref = rest
    rows = gated_ref.shape[0]
    chips = len(part_refs)
    ctx_size = 2 * chips
    per = rows // ctx_size
    part_refs = [part_refs[order.index(k)] for k in range(chips)]
    me = me_ref[0]
    sums = part_refs[0][0:rows, :].astype(F32)
    for part_ref in part_refs[1:]:
        sums = sums + part_ref[0:rows, :].astype(F32)
    kv_grads = in_token_order(ctx_size, lambda place: place, sums.astype(BF16))
    extra = (part_refs[0].shape[0] - rows) // 2
    query_rows = [part_ref[rows:, :].astype(F32) for part_ref in part_refs]
    columns = []
    for part in range(extra // per):
        blocks = [
            block[core * extra + part * per : core * extra + (part + 1) * per, :]
            for core in range(2)
            for block in query_rows
        ]
        columns.append(jnp.concatenate(blocks, axis=0))
    query_grads = in_token_order(
        ctx_size,
        lambda place: (2 * (place % chips) + place // chips) ^ me,
        jnp.concatenate(columns, axis=1).astype(BF16),
    )
    grads = jnp.concatenate([query_grads, kv_grads], axis=1)
    mixer_grad = nt(grads, weight_ref[...]).astype(BF16).astype(F32)

    gated = gated_ref[...]
    inverse = inverse_ref[:, 0:1]
    scaled = gain_ref[...] * mixer_grad
    mean = jnp.mean(scaled * gated, axis=-1, keepdims=True)
    gated_grad = scaled * inverse - gated * (mean * inverse * inverse * inverse)
    gate_out_ref[...] = gated_grad * slope_ref[...]
    out_grad = (gated_grad * active_ref[...]).astype(BF16)
    grad_out_ref[...] = out_grad
    grown_ref[...] = (out_grad.astype(F32) * grow_ref[...]).astype(BF16)
    last = sum_ref[rows - 1 :, :]
    write_halves(me % 2, last, grown_ref, read_ref, keep_ref, give_ref)


def local_kernel(
    me_ref,
    grad_ref,
    grown_ref,
    input_ref,
    write_ref,
    read_ref,
    sum_ref,
    turned_ref,
    mine_ref,
    other_ref,
    value_ref,
    write_out_ref,
    read_out_ref,
    both_ref,
):
    rows, channels = input_ref.shape
    mheads = sum_ref.shape[1]
    mdim = channels // mheads
    cumulated, turned = sum_ref[...], turned_ref[...]
    turned_products = nt(write_ref[...], read_ref[...])
    causal = iota((rows, rows), 0) >= iota((rows, rows), 1)
    later = iota((rows, rows), 0) <= iota((rows, rows), 1)
    pair_sum = jnp.zeros((rows, rows), F32)

    def decays_of(head):
        spread = cumulated[:, head : head + 1] - turned[head : head + 1, :]
        return jnp.exp(jnp.where(causal, spread, -jnp.inf))

    def turned_weights_of(head):
        spread = turned[head : head + 1, :] - cumulated[:, head : head + 1]
        return (jnp.exp(jnp.where(later, spread, -jnp.inf)) * turned_products).astype(BF16)

    for pair in range(mheads // 2):
        lanes = slice(pair * 2 * mdim, (pair + 1) * 2 * mdim)
        grads = split_pair(grad_ref[:, lanes], mdim)
        weights = jnp.concatenate(
            [turned_weights_of(2 * pair), turned_weights_of(2 * pair + 1)], axis=1
        )
        value_ref[:, lanes] = nn(weights, grads)
        pairs = nt(grads, input_ref[:, lanes])
        pair_sum = (
            pair_sum + decays_of(2 * pair) * pairs[:rows] + decays_of(2 * pair + 1) * pairs[rows:]
        )
    pair_low = pair_sum.astype(BF16)
    incoming = whole_state(me_ref, mine_ref, other_ref, both_ref)
    read_out_ref[...] = nn(pair_low, write_ref[...]) + nn(grown_ref[...], incoming)
    write_out_ref[...] = tn(pair_low, read_ref[...])


def final_kernel(
    me_ref,
    value_ref,
    write_part_ref,
    scaled_ref,
    remain_ref,
    write_ref,
    mine_ref,
    other_ref,
    out_ref,
    write_out_ref,
    both_ref,
):
    adjoint = whole_state(me_ref, mine_ref, other_ref, both_ref)
    out_ref[...] = value_ref[...] + remain_ref[...] * nt(write_ref[...], adjoint)
    write_out_ref[...] = write_part_ref[...] + nn(scaled_ref[...], adjoint)


def crossed(array, bits):
    pairs = [(i, i ^ bits) for i in range(lax.axis_size("ctx"))]
    return lax.ppermute(array, "ctx", pairs)


def tied(arrays, after):
    return lax.optimization_barrier((arrays, after))[0]


def scan_slices(me, cumulated, keep, give, reverse):
    group = lax.axis_size("ctx") // 4
    half_rows, nstate = keep.shape
    got = crossed(give, 1)
    slices = call(
        functools.partial(chip_kernel, reverse),
        [struct((half_rows // group + EXTRA, nstate), BF16)] * group,
        [me, cumulated, keep, got],
        half_rows * nstate,
        smem=(0,),
        scratch=[pltpu.VMEM((half_rows, nstate), F32)],
    )
    return slices, got


def scan_parts(slices):
    return [slices[0]] + [crossed(slices[k], 2 * k) for k in range(len(slices) - 1, 0, -1)]


def scan_total(me, cumulated, keep, parts, reverse):
    group = len(parts)
    half_rows, nstate = keep.shape
    slice_rows = half_rows // group
    heads = cumulated.shape[1]
    (total,) = call(
        functools.partial(total_kernel, reverse, heads, 2 * half_rows // heads),
        [struct((slice_rows, nstate), BF16)],
        [me] + list(parts),
        half_rows * nstate,
        smem=(0,),
        scratch=[pltpu.VMEM((group, slice_rows + EXTRA, nstate), BF16)],
    )
    return total


def scan_carry(total, reverse):
    half = lax.axis_size("ctx") // 2
    if reverse:
        pairs = [(i + half, i) for i in range(half)]
    else:
        pairs = [(i, i + half) for i in range(half)]
    return lax.ppermute(total, "ctx", pairs)


def scan_back(me, cumulated, carry, keep, parts, reverse):
    group = len(parts)
    slice_rows, nstate = carry.shape
    heads = cumulated.shape[1]
    backs = call(
        functools.partial(scan_kernel, reverse, heads, 2 * keep.shape[0] // heads),
        [struct(carry.shape, BF16)] * group,
        [me, carry] + list(parts),
        group * slice_rows * nstate,
        smem=(0,),
        scratch=[
            pltpu.VMEM((group, slice_rows + EXTRA, nstate), BF16),
            pltpu.VMEM((group, slice_rows, nstate), BF16),
        ],
    )
    return backs


def scan_out(me, cumulated, returned, keep, got, reverse):
    mine, send = call(
        functools.partial(core_kernel, reverse),
        [struct(keep.shape, BF16)] * 2,
        [me, cumulated, keep, got] + list(returned),
        keep.size,
        smem=(0,),
        scratch=[pltpu.VMEM(keep.shape, BF16)],
    )
    return mine, crossed(send, 1)


def body(
    queries,
    keys,
    values,
    d_out,
    mixer_input,
    gate_input,
    state_write,
    state_read,
    log_decay,
    norm_gain,
    project_weight,
):
    ctx_size = lax.axis_size("ctx")
    ctx_index = lax.axis_index("ctx")
    rows, head_dim = keys.shape
    wide = queries.shape[1]
    channels = mixer_input.shape[1]
    nstate = state_write.shape[1]
    mheads = log_decay.shape[1]
    per = rows // ctx_size
    me = ctx_index.astype(jnp.int32).reshape(1)
    packed = jnp.pad(keys, ((0, 0), (0, head_dim))) + jnp.pad(values, ((0, 0), (head_dim, 0)))
    near_plane = [packed] + [crossed(packed, k) for k in range(4, ctx_size, 4)]
    (plane,) = call(
        plane_kernel,
        [struct((ctx_size // 4, rows, 2 * head_dim), BF16)],
        near_plane,
        rows * head_dim,
    )
    plane_other = crossed(plane, 1)
    half_states = [
        struct((channels // 2, nstate), BF16),
        struct((channels // 2 + EXTRA, nstate), BF16),
    ]
    tile = tile_of(rows)
    columns = tile * wide // head_dim
    stacked = struct((rows // tile, columns, head_dim), BF16)
    keep, give, scaled, remain, grow, cumulated, turned = call(
        state_kernel,
        [
            *half_states,
            struct((rows, channels), BF16),
            struct((rows, channels), F32),
            struct((rows, channels), F32),
            struct((rows, mheads), F32),
            struct((mheads, rows), F32),
        ],
        [me, mixer_input, state_write, tied(log_decay.T, packed)],
        2 * rows * channels * nstate,
        smem=(0,),
    )

    query_tiles, grad_tiles = call(
        stack_kernel, [stacked, stacked], [queries, d_out], rows * wide
    )
    slices, got = scan_slices(me, cumulated, keep, give, False)
    parts = scan_parts(slices)
    across = crossed(plane, 2)
    across_other = crossed(tied(across, (tuple(parts[1:]), query_tiles)), 1)

    total = scan_total(me, cumulated, keep, parts, False)
    carry = scan_carry(total, False)
    query_tiles = tied(query_tiles, total)

    in_kernel = per % 8 == 0
    flops = 10 * rows * wide * ctx_size * rows
    scratch = [
        pltpu.VMEM((ctx_size, rows, 2 * head_dim), BF16),
        pltpu.VMEM((ctx_size, rows, 2 * head_dim), F32),
        pltpu.VMEM((rows // tile, ctx_size * tile, columns), F32),
        pltpu.VMEM((rows // tile, ctx_size * tile, columns), F32),
    ]
    attention_args = [me, query_tiles, grad_tiles, plane, plane_other, across, across_other]
    chips = ctx_size // 2
    extra = per * wide // (2 * head_dim)
    if in_kernel:
        part = struct((chips, rows + extra, 2 * head_dim), BF16)
        kv_keep, kv_give = call(
            functools.partial(attention_kernel, True, ctx_size),
            [part, part],
            attention_args,
            flops,
            smem=(0,),
            scratch=scratch + [pltpu.VMEM((ctx_size, extra, 2 * head_dim), F32)],
        )
    else:
        query_grad, kv_grad = call(
            functools.partial(attention_kernel, False, ctx_size),
            [struct((rows, wide), BF16), struct((ctx_size, rows, 2 * head_dim), BF16)],
            attention_args,
            flops,
            smem=(0,),
            scratch=scratch,
        )
        by_target = kv_grad.reshape(ctx_size, ctx_size, per, 2 * head_dim).transpose(1, 0, 2, 3)
        by_pair = query_grad.reshape(ctx_size, per, -1, 2 * head_dim).transpose(0, 2, 1, 3)
        sent = jnp.concatenate(
            [
                by_target.reshape(ctx_size, rows, 2 * head_dim),
                by_pair.reshape(ctx_size, extra, 2 * head_dim),
            ],
            axis=1,
        ).reshape(chips, 2, rows + extra, 2 * head_dim)
        kv_keep = lax.dynamic_index_in_dim(sent, ctx_index % 2, 1, False)
        kv_give = lax.dynamic_index_in_dim(sent, 1 - ctx_index % 2, 1, False)

    carry, kv_keep, kv_give = lax.optimization_barrier((carry, kv_keep, kv_give))
    kv_got = crossed(kv_give, 1)
    sent = call(
        join_kernel,
        [struct((rows + 2 * extra, 2 * head_dim), BF16)] * chips,
        [me, kv_keep, kv_got],
        chips * rows * 2 * head_dim,
        smem=(0,),
    )
    backs = scan_back(me, cumulated, tied(carry, sent[0]), keep, parts, False)
    order = sorted(range(chips), key=lambda k: (-(k // 4), k % 2, -k))
    received = [crossed(sent[k], 2 * k) if k else sent[k] for k in order]
    returned = tied(tuple(scan_parts(backs)), tuple(received[:5]))
    incoming, incoming_other = scan_out(me, cumulated, returned, keep, got, False)

    both_states = pltpu.VMEM((2, channels // 2, nstate), BF16)
    whole = struct((rows, channels), F32)
    gated, inverse, active, slope = call(
        mixer_kernel,
        [whole, struct((rows, 128), F32), whole, whole],
        [
            me,
            mixer_input,
            state_write,
            state_read,
            cumulated,
            turned,
            grow,
            gate_input,
            incoming,
            incoming_other,
        ],
        2 * rows * channels * (nstate + rows),
        smem=(0,),
        scratch=[both_states, pltpu.VMEM((rows, channels), F32)],
    )
    gate_gradient, out_grad, adjoint_keep, adjoint_give, grown = call(
        functools.partial(gate_kernel, order),
        [
            struct((rows, channels), F32),
            struct((rows, channels), BF16),
            *half_states,
            struct((rows, channels), BF16),
        ],
        [
            me,
            project_weight,
            gated,
            inverse,
            active,
            slope,
            norm_gain.reshape(1, channels),
            state_read,
            grow,
            cumulated,
        ]
        + received,
        2 * rows * channels * (nstate + project_weight.shape[1]),
        smem=(0,),
    )
    value_part, write_part, read_gradient = call(
        local_kernel,
        [
            struct((rows, channels), F32),
            struct((rows, nstate), F32),
            struct((rows, nstate), F32),
        ],
        [
            me,
            out_grad,
            grown,
            mixer_input,
            state_write,
            state_read,
            cumulated,
            turned,
            incoming,
            incoming_other,
        ],
        2 * rows * channels * (nstate + 2 * rows),
        smem=(0,),
        scratch=[both_states],
    )
    slices, got = scan_slices(me, cumulated, adjoint_keep, adjoint_give, True)
    parts = scan_parts(slices)
    carry = scan_carry(scan_total(me, cumulated, adjoint_keep, parts, True), True)
    carry = tied(carry, write_part)
    backs = scan_back(me, cumulated, carry, adjoint_keep, parts, True)
    adjoint, adjoint_other = scan_out(
        me, cumulated, scan_parts(backs), adjoint_keep, got, True
    )
    input_gradient, write_gradient = call(
        final_kernel,
        [struct((rows, channels), F32), struct((rows, nstate), F32)],
        [
            me,
            value_part,
            write_part,
            scaled,
            remain,
            state_write,
            adjoint,
            adjoint_other,
        ],
        4 * rows * channels * nstate,
        smem=(0,),
        scratch=[both_states],
    )
    return (input_gradient, gate_gradient, write_gradient, read_gradient)


def solution(mesh):
    both = P("ctx", "groups")
    return jax.shard_map(
        body,
        mesh=mesh,
        in_specs=(both,) * 9 + (P("groups"), P(None, "groups")),
        out_specs=(both,) * 4,
        check_vma=False,
    )
```

```python
import functools
import math

import jax
import jax.numpy as jnp
from jax import lax
from jax.experimental import pallas as pl
from jax.experimental.pallas import tpu as pltpu
from jax.sharding import PartitionSpec as P

EPSILON = 1e-05
HIGHEST = lax.Precision.HIGHEST
F32 = jnp.float32
BF16 = jnp.bfloat16
EXTRA = 16
MIB = 1024 * 1024


def nn(a, b, **kw):
    return lax.dot_general(a, b, (((1,), (0,)), ((), ())), preferred_element_type=F32, **kw)


def nt(a, b, **kw):
    return lax.dot_general(a, b, (((1,), (1,)), ((), ())), preferred_element_type=F32, **kw)


def tn(a, b, **kw):
    return lax.dot_general(a, b, (((0,), (0,)), ((), ())), preferred_element_type=F32, **kw)


def iota(shape, dim):
    return lax.broadcasted_iota(jnp.int32, shape, dim)


def call(kernel, outs, args, flops, smem=(), scratch=(), spare=4 * MIB):
    specs = [
        pl.BlockSpec(memory_space=pltpu.SMEM if i in smem else pltpu.VMEM) for i in range(len(args))
    ]
    moved = sum(a.size * a.dtype.itemsize for a in args) + sum(
        math.prod(o.shape) * o.dtype.itemsize for o in outs
    )
    held = moved + sum(
        math.prod(s.shape) * jnp.dtype(s.dtype).itemsize for s in scratch
    )
    return pl.pallas_call(
        kernel,
        out_shape=tuple(outs),
        in_specs=specs,
        out_specs=tuple(pl.BlockSpec(memory_space=pltpu.VMEM) for _ in outs),
        scratch_shapes=list(scratch),
        compiler_params=pltpu.CompilerParams(vmem_limit_bytes=held + spare),
        cost_estimate=pl.CostEstimate(flops=flops, bytes_accessed=moved, transcendentals=0),
    )(*args)


def struct(shape, dtype):
    return jax.ShapeDtypeStruct(shape, dtype)


def running_sums(log_decay):
    rows = log_decay.shape[1]
    lower = (iota((rows, rows), 0) >= iota((rows, rows), 1)).astype(F32)
    upper = (iota((rows, rows), 0) <= iota((rows, rows), 1)).astype(F32)
    return nt(lower, log_decay, precision=HIGHEST), nn(log_decay, upper, precision=HIGHEST)


def spread_heads(per_head, mdim):
    rows, heads = per_head.shape
    first = iota((rows, 2 * mdim), 1) < mdim
    pairs = [
        jnp.where(first, per_head[:, h : h + 1], per_head[:, h + 1 : h + 2])
        for h in range(0, heads, 2)
    ]
    return jnp.concatenate(pairs, axis=1)


def split_pair(block, mdim):
    first = iota(block.shape, 1) < mdim
    zero = jnp.zeros_like(block)
    return jnp.concatenate([jnp.where(first, block, zero), jnp.where(first, zero, block)], axis=0)


def plane_kernel(*refs):
    *piece_refs, out_ref = refs
    for i, piece_ref in enumerate(piece_refs):
        out_ref[i] = piece_ref[...]


def tile_of(rows):
    return min(32, rows)


def stack_kernel(*refs):
    count = len(refs) // 2
    for ref, out_ref in zip(refs[:count], refs[count:]):
        tiles, wide, head_dim = out_ref.shape
        tile = ref.shape[0] // tiles
        for t in range(tiles):
            for h in range(wide // tile):
                out_ref[t, h * tile : (h + 1) * tile, :] = ref[
                    t * tile : (t + 1) * tile, h * head_dim : (h + 1) * head_dim
                ]


def put_logs(ref, logs):
    heads = logs.shape[1]
    high = logs.astype(BF16).astype(F32)
    middle = (logs - high).astype(BF16).astype(F32)
    low = (logs - high - middle).astype(BF16).astype(F32)
    place = iota((EXTRA, heads), 0)
    split = jnp.where(place == 0, high, jnp.where(place == 1, middle, low))
    wide = jnp.concatenate([split, jnp.zeros((EXTRA, ref.shape[1] - heads), F32)], axis=1)
    ref[ref.shape[0] - EXTRA :, :] = wide.astype(BF16)


def get_logs(ref, heads):
    parts = ref[ref.shape[0] - EXTRA :, 0:heads].astype(F32)
    return parts[0:1, :] + parts[1:2, :] + parts[2:3, :]


def times(logs, start, mdim, state):
    head = iota(logs.shape, 1)
    blocks = []
    for i in range(state.shape[0] // mdim):
        log = jnp.sum(jnp.where(head == start + i, logs, 0.0), axis=1, keepdims=True)
        blocks.append(jnp.exp(log) * state[i * mdim : (i + 1) * mdim, :])
    return jnp.concatenate(blocks, axis=0)


def write_halves(core, logs, scaled_ref, other_ref, keep_ref, give_ref):
    half = keep_ref.shape[0]
    for out_ref, which in ((keep_ref, core), (give_ref, 1 - core)):
        lanes = pl.ds(pl.multiple_of(which * half, half), half)
        out_ref[0:half, :] = tn(scaled_ref[:, lanes], other_ref[...]).astype(BF16)
    put_logs(give_ref, logs)


def state_kernel(
    me_ref,
    input_ref,
    write_ref,
    decay_ref,
    keep_ref,
    give_ref,
    scaled_ref,
    remain_ref,
    grow_ref,
    sum_ref,
    turned_ref,
):
    cumulated, turned = running_sums(decay_ref[...])
    sum_ref[...], turned_ref[...] = cumulated, turned
    mdim = input_ref.shape[1] // cumulated.shape[1]
    last = cumulated[-1:, :]
    remain_ref[...] = spread_heads(jnp.exp(last - cumulated), mdim)
    grow_ref[...] = spread_heads(jnp.exp(cumulated), mdim)
    scaled_ref[...] = (input_ref[...].astype(F32) * remain_ref[...]).astype(BF16)
    write_halves(me_ref[0] % 2, last, scaled_ref, write_ref, keep_ref, give_ref)


def chip_kernel(reverse, me_ref, sum_ref, keep_ref, got_ref, *rest):
    *out_refs, total_ref = rest
    heads = sum_ref.shape[1]
    half = keep_ref.shape[0]
    mdim = 2 * half // heads
    core = me_ref[0] % 2
    chip = me_ref[0] // 2 % len(out_refs)
    slice_rows = out_refs[0].shape[0] - EXTRA
    own_logs = sum_ref[sum_ref.shape[0] - 1 :, :]
    got_logs = get_logs(got_ref, heads)
    keep, got = keep_ref[...].astype(F32), got_ref[0:half, :].astype(F32)
    first = core == (1 if reverse else 0)
    decayed = times(jnp.where(first, got_logs, own_logs), core * heads // 2, mdim, jnp.where(first, keep, got))
    total_ref[...] = decayed + jnp.where(first, got, keep)
    for k, out_ref in enumerate(out_refs):
        start = pl.multiple_of((chip ^ k) * slice_rows, slice_rows)
        out_ref[0:slice_rows, :] = total_ref[pl.ds(start, slice_rows), :].astype(BF16)
        put_logs(out_ref, own_logs + got_logs)


def steps(count, reverse):
    return range(count - 1, -1, -1) if reverse else range(count)


def ordered(chip, part_refs, order_ref):
    for k, part_ref in enumerate(part_refs):
        order_ref[chip ^ k] = part_ref[...]


def advance(order_ref, source, start, heads, mdim, state):
    part_ref = order_ref.at[source]
    rows = state.shape[0]
    return times(get_logs(part_ref, heads), start, mdim, state) + part_ref[0:rows, :].astype(F32)


def total_kernel(reverse, heads, mdim, me_ref, *rest):
    *part_refs, out_ref, order_ref = rest
    count = len(part_refs)
    chip = me_ref[0] // 2 % count
    ordered(chip, part_refs, order_ref)
    start = me_ref[0] % 2 * (heads // 2) + chip * (heads // 2 // count)
    state = jnp.zeros(out_ref.shape, F32)
    for source in steps(count, reverse):
        state = advance(order_ref, source, start, heads, mdim, state)
    out_ref[...] = state.astype(BF16)


def scan_kernel(reverse, heads, mdim, me_ref, carry_ref, *rest):
    *refs, order_ref, result_ref = rest
    count = len(refs) // 2
    chip = me_ref[0] // 2 % count
    ordered(chip, refs[:count], order_ref)
    start = me_ref[0] % 2 * (heads // 2) + chip * (heads // 2 // count)
    state = carry_ref[...].astype(F32)
    for source in steps(count, reverse):
        result_ref[source] = state.astype(BF16)
        state = advance(order_ref, source, start, heads, mdim, state)
    for k, out_ref in enumerate(refs[count:]):
        out_ref[...] = result_ref[chip ^ k]


def core_kernel(reverse, me_ref, sum_ref, keep_ref, got_ref, *rest):
    *part_refs, mine_ref, send_ref, order_ref = rest
    count = len(part_refs)
    heads = sum_ref.shape[1]
    half = keep_ref.shape[0]
    core = me_ref[0] % 2
    chip = me_ref[0] // 2 % count
    slice_rows = part_refs[0].shape[0]
    for k, part_ref in enumerate(part_refs):
        start = pl.multiple_of((chip ^ k) * slice_rows, slice_rows)
        order_ref[pl.ds(start, slice_rows), :] = part_ref[...]
    first = core == (1 if reverse else 0)
    logs = jnp.where(first, sum_ref[sum_ref.shape[0] - 1 :, :], get_logs(got_ref, heads))
    own = jnp.where(first, keep_ref[...].astype(F32), got_ref[0:half, :].astype(F32))
    incoming = order_ref[...].astype(F32)
    passed = times(logs, core * heads // 2, 2 * half // heads, incoming) + own
    mine_ref[...] = jnp.where(first, incoming, passed).astype(BF16)
    send_ref[...] = jnp.where(first, passed, incoming).astype(BF16)


def whole_state(me_ref, mine_ref, other_ref, both_ref):
    core = me_ref[0] % 2
    both_ref[core] = mine_ref[...]
    both_ref[1 - core] = other_ref[...]
    _, half, nstate = both_ref.shape
    return both_ref[...].reshape(2 * half, nstate)


def mixer_kernel(
    me_ref,
    input_ref,
    write_ref,
    read_ref,
    sum_ref,
    turned_ref,
    grow_ref,
    gate_ref,
    mine_ref,
    other_ref,
    gated_ref,
    inverse_ref,
    active_ref,
    slope_ref,
    both_ref,
    out_ref,
):
    rows, channels = input_ref.shape
    mheads = sum_ref.shape[1]
    mdim = channels // mheads
    cumulated, turned = sum_ref[...], turned_ref[...]
    carried = nt(read_ref[...], whole_state(me_ref, mine_ref, other_ref, both_ref))
    out_ref[...] = grow_ref[...] * carried
    products = nt(read_ref[...], write_ref[...])
    causal = iota((rows, rows), 0) >= iota((rows, rows), 1)

    def weights_of(head):
        spread = cumulated[:, head : head + 1] - turned[head : head + 1, :]
        return (jnp.exp(jnp.where(causal, spread, -jnp.inf)) * products).astype(BF16)

    for pair in range(mheads // 2):
        lanes = slice(pair * 2 * mdim, (pair + 1) * 2 * mdim)
        weights = jnp.concatenate([weights_of(2 * pair), weights_of(2 * pair + 1)], axis=1)
        out_ref[:, lanes] += nn(weights, split_pair(input_ref[:, lanes], mdim))

    mixer_out = out_ref[...]
    gate = gate_ref[...].astype(F32)
    sigmoid = jax.nn.sigmoid(gate)
    active = gate * sigmoid
    gated = mixer_out * active
    active_ref[...] = active
    gated_ref[...] = gated
    slope_ref[...] = mixer_out * sigmoid * (1.0 + gate * (1.0 - sigmoid))
    inverse = lax.rsqrt(jnp.mean(gated * gated, axis=-1, keepdims=True) + EPSILON)
    inverse_ref[...] = jnp.broadcast_to(inverse, inverse_ref.shape)


def attention_kernel(
    in_kernel, ctx_size, me_ref, query_ref, grad_ref, *rest
):
    plane_refs, rest = rest[:4], rest[4:]
    if in_kernel:
        keep_ref, give_ref, gathered_ref, acc_ref, raw_ref, back_ref, query_acc_ref = rest
    else:
        query_out_ref, pack_ref, gathered_ref, acc_ref, raw_ref, back_ref = rest
    tiles, wide, head_dim = query_ref.shape
    rows = gathered_ref.shape[1]
    tile = rows // tiles
    heads = wide // tile
    me = me_ref[0]
    scale = 1.0 / math.sqrt(head_dim)
    base2 = scale * math.log2(math.e)
    per = rows // ctx_size
    for offset, plane_ref in enumerate(plane_refs):
        for level in range(ctx_size // 4):
            gathered_ref[me ^ (4 * level + offset)] = plane_ref[level]

    def keys_of(b):
        return gathered_ref[:, b * tile : (b + 1) * tile, 0:head_dim].reshape(
            ctx_size * tile, head_dim
        )

    def values_of(b):
        return gathered_ref[:, b * tile : (b + 1) * tile, head_dim : 2 * head_dim].reshape(
            ctx_size * tile, head_dim
        )

    key_row = iota((ctx_size * tile, wide), 0)
    key_place = (key_row % tile) * ctx_size + key_row // tile
    query_place = (iota((ctx_size * tile, wide), 1) % tile) * ctx_size + me
    visible = key_place <= query_place

    def score(t):
        slot = t % 2
        query = query_ref[t]
        highest = None
        for b in range(t, -1, -1):
            raw = nt(keys_of(b), query)
            if b == t:
                raw = jnp.where(visible, raw, -jnp.inf)
            raw_ref[slot, b] = raw
            block_high = jnp.max(raw, axis=0, keepdims=True)
            highest = block_high if highest is None else jnp.maximum(highest, block_high)
        return highest

    def weigh(t, highest):
        slot = t % 2
        grad = grad_ref[t]
        total = jnp.zeros((1, wide), F32)
        delta = jnp.zeros((1, wide), F32)
        for b in range(t + 1):
            probs = jnp.exp2((raw_ref[slot, b] - highest) * base2)
            back = nt(values_of(b), grad)
            raw_ref[slot, b] = probs
            back_ref[slot, b] = back
            total = total + jnp.sum(probs, axis=0, keepdims=True)
            delta = delta + jnp.sum(probs * back, axis=0, keepdims=True)
        inverse = 1.0 / total
        return inverse, delta * inverse

    def gather(t, inverse, delta):
        slot = t % 2
        query, grad = query_ref[t], grad_ref[t]
        query_grad = jnp.zeros((head_dim, wide), F32)
        for b in range(t + 1):
            weights = raw_ref[slot, b] * inverse
            score_grad = (weights * (back_ref[slot, b] - delta)).astype(BF16)
            value_part = nn(weights.astype(BF16), grad).reshape(ctx_size, tile, head_dim)
            key_part = nn(score_grad, query).reshape(ctx_size, tile, head_dim)
            here = slice(b * tile, (b + 1) * tile)
            if t == tiles - 1:
                acc_ref[:, here, 0:head_dim] = key_part
                acc_ref[:, here, head_dim:] = value_part
            else:
                acc_ref[:, here, 0:head_dim] += key_part
                acc_ref[:, here, head_dim:] += value_part
            query_grad = query_grad + tn(keys_of(b), score_grad)
        turned = (query_grad * scale).T
        by_head = [turned[h * tile : (h + 1) * tile, :] for h in range(heads)]
        if in_kernel:
            pairs = [
                jnp.concatenate(by_head[h : h + 2], axis=1) for h in range(0, heads, 2)
            ]
            for k in range(tile // per):
                rows_here = [p[k * per : (k + 1) * per, :] for p in pairs]
                query_acc_ref[t * (tile // per) + k] = jnp.concatenate(rows_here, axis=0)
        else:
            for h in range(heads):
                query_out_ref[t * tile : (t + 1) * tile, h * head_dim : (h + 1) * head_dim] = (
                    by_head[h].astype(BF16)
                )

    last = tiles - 1
    state = weigh(last, score(last))
    for t in range(last, -1, -1):
        if t:
            highest = score(t - 1)
        gather(t, *state)
        if t:
            state = weigh(t - 1, highest)

    both = jnp.where(iota((1, 1, 2 * head_dim), 2) < head_dim, scale, 1.0)
    if in_kernel:
        for chip in range(ctx_size // 2):
            for out_ref, core in ((keep_ref, me % 2), (give_ref, 1 - me % 2)):
                target = 2 * chip + core
                start = pl.multiple_of(target * per, per)
                block = acc_ref[:, pl.ds(start, per), :] * both
                out_ref[chip, 0:rows, :] = block.reshape(rows, 2 * head_dim).astype(BF16)
                out_ref[chip, rows:, :] = query_acc_ref[target].astype(BF16)
    else:
        pack_ref[...] = (acc_ref[...] * both).astype(BF16)


def join_kernel(me_ref, keep_ref, got_ref, *out_refs):
    mid = keep_ref.shape[1]
    rows = 2 * mid - out_refs[0].shape[0]
    chip = me_ref[0] // 2
    for k, out_ref in enumerate(out_refs):
        target = chip ^ k
        both = keep_ref[target, 0:rows, :].astype(F32) + got_ref[target, 0:rows, :].astype(F32)
        out_ref[0:rows, :] = both.astype(BF16)
        out_ref[rows:mid, :] = keep_ref[target, rows:, :]
        out_ref[mid:, :] = got_ref[target, rows:, :]


def in_token_order(ctx_size, devices, grads):
    rows = grads.shape[0]
    per = rows // ctx_size
    token, came = iota((rows, rows), 0), iota((rows, rows), 1)
    order = (token == (came % per) * ctx_size + devices(came // per)).astype(BF16)
    return nn(order, grads).astype(BF16)


def gate_kernel(
    order,
    me_ref,
    weight_ref,
    gated_ref,
    inverse_ref,
    active_ref,
    gain_ref,
    read_ref,
    grow_ref,
    sum_ref,
    *rest,
):
    *part_refs, gated_grad_ref, grad_out_ref, keep_ref, give_ref, grown_ref = rest
    rows = gated_ref.shape[0]
    chips = len(part_refs)
    ctx_size = 2 * chips
    per = rows // ctx_size
    part_refs = [part_refs[order.index(k)] for k in range(chips)]
    me = me_ref[0]
    sums = part_refs[0][0:rows, :].astype(F32)
    for part_ref in part_refs[1:]:
        sums = sums + part_ref[0:rows, :].astype(F32)
    kv_grads = in_token_order(ctx_size, lambda place: place, sums.astype(BF16))
    extra = (part_refs[0].shape[0] - rows) // 2
    query_rows = [part_ref[rows:, :].astype(F32) for part_ref in part_refs]
    columns = []
    for part in range(extra // per):
        blocks = [
            block[core * extra + part * per : core * extra + (part + 1) * per, :]
            for core in range(2)
            for block in query_rows
        ]
        columns.append(jnp.concatenate(blocks, axis=0))
    query_grads = in_token_order(
        ctx_size,
        lambda place: (2 * (place % chips) + place // chips) ^ me,
        jnp.concatenate(columns, axis=1).astype(BF16),
    )
    grads = jnp.concatenate([query_grads, kv_grads], axis=1)
    mixer_grad = nt(grads, weight_ref[...]).astype(BF16).astype(F32)

    gated = gated_ref[...]
    inverse = inverse_ref[:, 0:1]
    scaled = gain_ref[...] * mixer_grad
    mean = jnp.mean(scaled * gated, axis=-1, keepdims=True)
    gated_grad = scaled * inverse - gated * (mean * inverse * inverse * inverse)
    gated_grad_ref[...] = gated_grad
    out_grad = (gated_grad * active_ref[...]).astype(BF16)
    grad_out_ref[...] = out_grad
    grown_ref[...] = (out_grad.astype(F32) * grow_ref[...]).astype(BF16)
    last = sum_ref[rows - 1 :, :]
    write_halves(me % 2, last, grown_ref, read_ref, keep_ref, give_ref)


def local_kernel(
    me_ref,
    grad_ref,
    grown_ref,
    input_ref,
    write_ref,
    read_ref,
    sum_ref,
    turned_ref,
    mine_ref,
    other_ref,
    gated_grad_ref,
    slope_ref,
    value_ref,
    write_out_ref,
    read_out_ref,
    gate_out_ref,
    both_ref,
):
    rows, channels = input_ref.shape
    mheads = sum_ref.shape[1]
    mdim = channels // mheads
    gate_out_ref[...] = gated_grad_ref[...] * slope_ref[...]
    cumulated, turned = sum_ref[...], turned_ref[...]
    turned_products = nt(write_ref[...], read_ref[...])
    causal = iota((rows, rows), 0) >= iota((rows, rows), 1)
    later = iota((rows, rows), 0) <= iota((rows, rows), 1)
    pair_sum = jnp.zeros((rows, rows), F32)

    def decays_of(head):
        spread = cumulated[:, head : head + 1] - turned[head : head + 1, :]
        return jnp.exp(jnp.where(causal, spread, -jnp.inf))

    def turned_weights_of(head):
        spread = turned[head : head + 1, :] - cumulated[:, head : head + 1]
        return (jnp.exp(jnp.where(later, spread, -jnp.inf)) * turned_products).astype(BF16)

    for pair in range(mheads // 2):
        lanes = slice(pair * 2 * mdim, (pair + 1) * 2 * mdim)
        grads = split_pair(grad_ref[:, lanes], mdim)
        weights = jnp.concatenate(
            [turned_weights_of(2 * pair), turned_weights_of(2 * pair + 1)], axis=1
        )
        value_ref[:, lanes] = nn(weights, grads)
        pairs = nt(grads, input_ref[:, lanes])
        pair_sum = (
            pair_sum + decays_of(2 * pair) * pairs[:rows] + decays_of(2 * pair + 1) * pairs[rows:]
        )
    pair_low = pair_sum.astype(BF16)
    incoming = whole_state(me_ref, mine_ref, other_ref, both_ref)
    read_out_ref[...] = nn(pair_low, write_ref[...]) + nn(grown_ref[...], incoming)
    write_out_ref[...] = tn(pair_low, read_ref[...])


def half_of(which, half):
    return pl.ds(pl.multiple_of(which * half, half), half)


def half_kernel(me_ref, scaled_ref, remain_ref, write_ref, mine_ref, half_ref, write_half_ref):
    lanes = half_of(me_ref[0] % 2, mine_ref.shape[0])
    half_ref[...] = remain_ref[:, lanes] * nt(write_ref[...], mine_ref[...])
    write_half_ref[...] = nn(scaled_ref[:, lanes], mine_ref[...])


def final_kernel(
    me_ref,
    value_ref,
    write_part_ref,
    half_ref,
    write_half_ref,
    scaled_ref,
    remain_ref,
    write_ref,
    other_ref,
    out_ref,
    write_out_ref,
):
    core = me_ref[0] % 2
    half = other_ref.shape[0]
    lanes = half_of(core, half)
    out_ref[:, lanes] = value_ref[:, lanes] + half_ref[...]
    lanes = half_of(1 - core, half)
    out_ref[:, lanes] = value_ref[:, lanes] + remain_ref[:, lanes] * nt(write_ref[...], other_ref[...])
    write_out_ref[...] = (
        write_part_ref[...] + write_half_ref[...] + nn(scaled_ref[:, lanes], other_ref[...])
    )


def crossed(array, bits):
    pairs = [(i, i ^ bits) for i in range(lax.axis_size("ctx"))]
    return lax.ppermute(array, "ctx", pairs)


def tied(arrays, after):
    return lax.optimization_barrier((arrays, after))[0]


def scan_slices(me, cumulated, keep, give, reverse):
    group = lax.axis_size("ctx") // 4
    half_rows, nstate = keep.shape
    got = crossed(give, 1)
    slices = call(
        functools.partial(chip_kernel, reverse),
        [struct((half_rows // group + EXTRA, nstate), BF16)] * group,
        [me, cumulated, keep, got],
        half_rows * nstate,
        smem=(0,),
        scratch=[pltpu.VMEM((half_rows, nstate), F32)],
    )
    return slices, got


def scan_parts(slices):
    return [slices[0]] + [crossed(slices[k], 2 * k) for k in range(1, len(slices))]


def scan_total(me, cumulated, keep, parts, reverse):
    group = len(parts)
    half_rows, nstate = keep.shape
    slice_rows = half_rows // group
    heads = cumulated.shape[1]
    (total,) = call(
        functools.partial(total_kernel, reverse, heads, 2 * half_rows // heads),
        [struct((slice_rows, nstate), BF16)],
        [me] + list(parts),
        half_rows * nstate,
        smem=(0,),
        scratch=[pltpu.VMEM((group, slice_rows + EXTRA, nstate), BF16)],
    )
    return total


def scan_carry(total, reverse):
    half = lax.axis_size("ctx") // 2
    if reverse:
        pairs = [(i + half, i) for i in range(half)]
    else:
        pairs = [(i, i + half) for i in range(half)]
    return lax.ppermute(total, "ctx", pairs)


def scan_back(me, cumulated, carry, keep, parts, reverse):
    group = len(parts)
    slice_rows, nstate = carry.shape
    heads = cumulated.shape[1]
    backs = call(
        functools.partial(scan_kernel, reverse, heads, 2 * keep.shape[0] // heads),
        [struct(carry.shape, BF16)] * group,
        [me, carry] + list(parts),
        group * slice_rows * nstate,
        smem=(0,),
        scratch=[
            pltpu.VMEM((group, slice_rows + EXTRA, nstate), BF16),
            pltpu.VMEM((group, slice_rows, nstate), BF16),
        ],
    )
    return backs


def scan_out(me, cumulated, returned, keep, got, reverse):
    mine, send = call(
        functools.partial(core_kernel, reverse),
        [struct(keep.shape, BF16)] * 2,
        [me, cumulated, keep, got] + list(returned),
        keep.size,
        smem=(0,),
        scratch=[pltpu.VMEM(keep.shape, BF16)],
    )
    return mine, crossed(send, 1)


def body(
    queries,
    keys,
    values,
    d_out,
    mixer_input,
    gate_input,
    state_write,
    state_read,
    log_decay,
    norm_gain,
    project_weight,
):
    ctx_size = lax.axis_size("ctx")
    ctx_index = lax.axis_index("ctx")
    rows, head_dim = keys.shape
    wide = queries.shape[1]
    channels = mixer_input.shape[1]
    nstate = state_write.shape[1]
    mheads = log_decay.shape[1]
    per = rows // ctx_size
    me = ctx_index.astype(jnp.int32).reshape(1)
    packed = jnp.pad(keys, ((0, 0), (0, head_dim))) + jnp.pad(values, ((0, 0), (head_dim, 0)))
    near_plane = [packed] + [crossed(packed, k) for k in range(4, ctx_size, 4)]
    (plane,) = call(
        plane_kernel,
        [struct((ctx_size // 4, rows, 2 * head_dim), BF16)],
        near_plane,
        rows * head_dim,
    )
    plane_other = crossed(plane, 1)
    half_states = [
        struct((channels // 2, nstate), BF16),
        struct((channels // 2 + EXTRA, nstate), BF16),
    ]
    tile = tile_of(rows)
    columns = tile * wide // head_dim
    stacked = struct((rows // tile, columns, head_dim), BF16)
    keep, give, scaled, remain, grow, cumulated, turned = call(
        state_kernel,
        [
            *half_states,
            struct((rows, channels), BF16),
            struct((rows, channels), F32),
            struct((rows, channels), F32),
            struct((rows, mheads), F32),
            struct((mheads, rows), F32),
        ],
        [me, mixer_input, state_write, tied(log_decay.T, packed)],
        2 * rows * channels * nstate,
        smem=(0,),
    )

    query_tiles, grad_tiles = call(
        stack_kernel, [stacked, stacked], [queries, d_out], rows * wide
    )
    slices, got = scan_slices(me, cumulated, keep, give, False)
    parts = scan_parts(slices)
    across = crossed(plane, 2)
    across_other = crossed(tied(across, (tuple(parts[1:]), query_tiles)), 1)

    total = scan_total(me, cumulated, keep, parts, False)
    carry = scan_carry(total, False)
    query_tiles = tied(query_tiles, total)

    in_kernel = per % 8 == 0
    flops = 10 * rows * wide * ctx_size * rows
    scratch = [
        pltpu.VMEM((ctx_size, rows, 2 * head_dim), BF16),
        pltpu.VMEM((ctx_size, rows, 2 * head_dim), F32),
        pltpu.VMEM((2, rows // tile, ctx_size * tile, columns), F32),
        pltpu.VMEM((2, rows // tile, ctx_size * tile, columns), F32),
    ]
    attention_args = [me, query_tiles, grad_tiles, plane, plane_other, across, across_other]
    chips = ctx_size // 2
    extra = per * wide // (2 * head_dim)
    if in_kernel:
        part = struct((chips, rows + extra, 2 * head_dim), BF16)
        kv_keep, kv_give = call(
            functools.partial(attention_kernel, True, ctx_size),
            [part, part],
            attention_args,
            flops,
            smem=(0,),
            scratch=scratch + [pltpu.VMEM((ctx_size, extra, 2 * head_dim), F32)],
        )
    else:
        query_grad, kv_grad = call(
            functools.partial(attention_kernel, False, ctx_size),
            [struct((rows, wide), BF16), struct((ctx_size, rows, 2 * head_dim), BF16)],
            attention_args,
            flops,
            smem=(0,),
            scratch=scratch,
        )
        by_target = kv_grad.reshape(ctx_size, ctx_size, per, 2 * head_dim).transpose(1, 0, 2, 3)
        by_pair = query_grad.reshape(ctx_size, per, -1, 2 * head_dim).transpose(0, 2, 1, 3)
        sent = jnp.concatenate(
            [
                by_target.reshape(ctx_size, rows, 2 * head_dim),
                by_pair.reshape(ctx_size, extra, 2 * head_dim),
            ],
            axis=1,
        ).reshape(chips, 2, rows + extra, 2 * head_dim)
        kv_keep = lax.dynamic_index_in_dim(sent, ctx_index % 2, 1, False)
        kv_give = lax.dynamic_index_in_dim(sent, 1 - ctx_index % 2, 1, False)

    carry, kv_keep, kv_give = lax.optimization_barrier((carry, kv_keep, kv_give))
    kv_got = crossed(kv_give, 1)
    backs = scan_back(me, cumulated, carry, keep, parts, False)
    sent = call(
        join_kernel,
        [struct((rows + 2 * extra, 2 * head_dim), BF16)] * chips,
        [me, kv_keep, tied(kv_got, backs[0])],
        chips * rows * 2 * head_dim,
        smem=(0,),
    )
    order = sorted(range(chips), key=lambda k: (-(k // 4), k % 2, -k))
    received = [crossed(sent[k], 2 * k) if k else sent[k] for k in order]
    returned = tied(tuple(scan_parts(backs)), tuple(received[:3]))
    incoming, incoming_other = scan_out(me, cumulated, returned, keep, got, False)

    both_states = pltpu.VMEM((2, channels // 2, nstate), BF16)
    whole = struct((rows, channels), F32)
    gated, inverse, active, slope = call(
        mixer_kernel,
        [whole, struct((rows, 128), F32), whole, whole],
        [
            me,
            mixer_input,
            state_write,
            state_read,
            cumulated,
            turned,
            grow,
            gate_input,
            incoming,
            incoming_other,
        ],
        2 * rows * channels * (nstate + rows),
        smem=(0,),
        scratch=[both_states, pltpu.VMEM((rows, channels), F32)],
    )
    gated_grad, out_grad, adjoint_keep, adjoint_give, grown = call(
        functools.partial(gate_kernel, order),
        [
            struct((rows, channels), F32),
            struct((rows, channels), BF16),
            *half_states,
            struct((rows, channels), BF16),
        ],
        [
            me,
            project_weight,
            gated,
            inverse,
            active,
            norm_gain.reshape(1, channels),
            state_read,
            grow,
            cumulated,
        ]
        + received,
        2 * rows * channels * (nstate + project_weight.shape[1]),
        smem=(0,),
    )
    value_part, write_part, read_gradient, gate_gradient = call(
        local_kernel,
        [
            struct((rows, channels), F32),
            struct((rows, nstate), F32),
            struct((rows, nstate), F32),
            whole,
        ],
        [
            me,
            out_grad,
            grown,
            mixer_input,
            state_write,
            state_read,
            cumulated,
            turned,
            incoming,
            incoming_other,
            gated_grad,
            slope,
        ],
        2 * rows * channels * (nstate + 2 * rows),
        smem=(0,),
        scratch=[both_states],
    )
    slices, got = scan_slices(me, cumulated, adjoint_keep, adjoint_give, True)
    parts = scan_parts(slices)
    carry = scan_carry(scan_total(me, cumulated, adjoint_keep, parts, True), True)
    carry = tied(carry, write_part)
    backs = scan_back(me, cumulated, carry, adjoint_keep, parts, True)
    adjoint, adjoint_other = scan_out(
        me, cumulated, scan_parts(backs), adjoint_keep, got, True
    )
    half_out, write_half = call(
        half_kernel,
        [struct((rows, channels // 2), F32), struct((rows, nstate), F32)],
        [me, scaled, remain, state_write, adjoint],
        2 * rows * channels * nstate,
        smem=(0,),
    )
    input_gradient, write_gradient = call(
        final_kernel,
        [whole, struct((rows, nstate), F32)],
        [
            me,
            value_part,
            write_part,
            half_out,
            write_half,
            scaled,
            remain,
            state_write,
            adjoint_other,
        ],
        2 * rows * channels * nstate,
        smem=(0,),
    )
    return (input_gradient, gate_gradient, write_gradient, read_gradient)


def solution(mesh):
    both = P("ctx", "groups")
    return jax.shard_map(
        body,
        mesh=mesh,
        in_specs=(both,) * 9 + (P("groups"), P(None, "groups")),
        out_specs=(both,) * 4,
        check_vma=False,
    )
```

```python
import functools
import math

import jax
import jax.numpy as jnp
from jax import lax
from jax.experimental import pallas as pl
from jax.experimental.pallas import tpu as pltpu
from jax.sharding import PartitionSpec as P

EPSILON = 1e-05
HIGHEST = lax.Precision.HIGHEST
F32 = jnp.float32
BF16 = jnp.bfloat16
EXTRA = 16
MIB = 1024 * 1024


def nn(a, b, **kw):
    return lax.dot_general(a, b, (((1,), (0,)), ((), ())), preferred_element_type=F32, **kw)


def nt(a, b, **kw):
    return lax.dot_general(a, b, (((1,), (1,)), ((), ())), preferred_element_type=F32, **kw)


def tn(a, b, **kw):
    return lax.dot_general(a, b, (((0,), (0,)), ((), ())), preferred_element_type=F32, **kw)


def iota(shape, dim):
    return lax.broadcasted_iota(jnp.int32, shape, dim)


def call(kernel, outs, args, flops, smem=(), scratch=(), spare=4 * MIB):
    specs = [
        pl.BlockSpec(memory_space=pltpu.SMEM if i in smem else pltpu.VMEM) for i in range(len(args))
    ]
    moved = sum(a.size * a.dtype.itemsize for a in args) + sum(
        math.prod(o.shape) * o.dtype.itemsize for o in outs
    )
    held = moved + sum(
        math.prod(s.shape) * jnp.dtype(s.dtype).itemsize for s in scratch
    )
    return pl.pallas_call(
        kernel,
        out_shape=tuple(outs),
        in_specs=specs,
        out_specs=tuple(pl.BlockSpec(memory_space=pltpu.VMEM) for _ in outs),
        scratch_shapes=list(scratch),
        compiler_params=pltpu.CompilerParams(vmem_limit_bytes=held + spare),
        cost_estimate=pl.CostEstimate(flops=flops, bytes_accessed=moved, transcendentals=0),
    )(*args)


def struct(shape, dtype):
    return jax.ShapeDtypeStruct(shape, dtype)


def running_sums(log_decay):
    rows = log_decay.shape[1]
    lower = (iota((rows, rows), 0) >= iota((rows, rows), 1)).astype(F32)
    upper = (iota((rows, rows), 0) <= iota((rows, rows), 1)).astype(F32)
    return nt(lower, log_decay, precision=HIGHEST), nn(log_decay, upper, precision=HIGHEST)


def spread_heads(per_head, mdim):
    rows, heads = per_head.shape
    first = iota((rows, 2 * mdim), 1) < mdim
    pairs = [
        jnp.where(first, per_head[:, h : h + 1], per_head[:, h + 1 : h + 2])
        for h in range(0, heads, 2)
    ]
    return jnp.concatenate(pairs, axis=1)


def split_pair(block, mdim):
    first = iota(block.shape, 1) < mdim
    zero = jnp.zeros_like(block)
    return jnp.concatenate([jnp.where(first, block, zero), jnp.where(first, zero, block)], axis=0)


def plane_kernel(*refs):
    *piece_refs, out_ref = refs
    for i, piece_ref in enumerate(piece_refs):
        out_ref[i] = piece_ref[...]


def tile_of(rows):
    return min(32, rows)


def stack_kernel(*refs):
    count = len(refs) // 2
    for ref, out_ref in zip(refs[:count], refs[count:]):
        tiles, wide, head_dim = out_ref.shape
        tile = ref.shape[0] // tiles
        for t in range(tiles):
            for h in range(wide // tile):
                out_ref[t, h * tile : (h + 1) * tile, :] = ref[
                    t * tile : (t + 1) * tile, h * head_dim : (h + 1) * head_dim
                ]


def put_logs(ref, logs):
    heads = logs.shape[1]
    high = logs.astype(BF16).astype(F32)
    middle = (logs - high).astype(BF16).astype(F32)
    low = (logs - high - middle).astype(BF16).astype(F32)
    place = iota((EXTRA, heads), 0)
    split = jnp.where(place == 0, high, jnp.where(place == 1, middle, low))
    wide = jnp.concatenate([split, jnp.zeros((EXTRA, ref.shape[1] - heads), F32)], axis=1)
    ref[ref.shape[0] - EXTRA :, :] = wide.astype(BF16)


def get_logs(ref, heads):
    parts = ref[ref.shape[0] - EXTRA :, 0:heads].astype(F32)
    return parts[0:1, :] + parts[1:2, :] + parts[2:3, :]


def times(logs, start, mdim, state):
    head = iota(logs.shape, 1)
    blocks = []
    for i in range(state.shape[0] // mdim):
        log = jnp.sum(jnp.where(head == start + i, logs, 0.0), axis=1, keepdims=True)
        blocks.append(jnp.exp(log) * state[i * mdim : (i + 1) * mdim, :])
    return jnp.concatenate(blocks, axis=0)


def write_halves(core, logs, scaled_ref, other_ref, keep_ref, give_ref):
    half = keep_ref.shape[0]
    for out_ref, which in ((keep_ref, core), (give_ref, 1 - core)):
        lanes = pl.ds(pl.multiple_of(which * half, half), half)
        out_ref[0:half, :] = tn(scaled_ref[:, lanes], other_ref[...]).astype(BF16)
    put_logs(give_ref, logs)


def state_kernel(
    me_ref,
    input_ref,
    write_ref,
    decay_ref,
    keep_ref,
    give_ref,
    scaled_ref,
    remain_ref,
    grow_ref,
    sum_ref,
    turned_ref,
):
    cumulated, turned = running_sums(decay_ref[...])
    sum_ref[...], turned_ref[...] = cumulated, turned
    mdim = input_ref.shape[1] // cumulated.shape[1]
    last = cumulated[-1:, :]
    remain_ref[...] = spread_heads(jnp.exp(last - cumulated), mdim)
    grow_ref[...] = spread_heads(jnp.exp(cumulated), mdim)
    scaled_ref[...] = (input_ref[...].astype(F32) * remain_ref[...]).astype(BF16)
    write_halves(me_ref[0] % 2, last, scaled_ref, write_ref, keep_ref, give_ref)


def chip_kernel(reverse, me_ref, sum_ref, keep_ref, got_ref, *rest):
    *out_refs, total_ref = rest
    heads = sum_ref.shape[1]
    half = keep_ref.shape[0]
    mdim = 2 * half // heads
    core = me_ref[0] % 2
    chip = me_ref[0] // 2 % len(out_refs)
    slice_rows = out_refs[0].shape[0] - EXTRA
    own_logs = sum_ref[sum_ref.shape[0] - 1 :, :]
    got_logs = get_logs(got_ref, heads)
    keep, got = keep_ref[...].astype(F32), got_ref[0:half, :].astype(F32)
    first = core == (1 if reverse else 0)
    decayed = times(jnp.where(first, got_logs, own_logs), core * heads // 2, mdim, jnp.where(first, keep, got))
    total_ref[...] = decayed + jnp.where(first, got, keep)
    for k, out_ref in enumerate(out_refs):
        start = pl.multiple_of((chip ^ k) * slice_rows, slice_rows)
        out_ref[0:slice_rows, :] = total_ref[pl.ds(start, slice_rows), :].astype(BF16)
        put_logs(out_ref, own_logs + got_logs)


def steps(count, reverse):
    return range(count - 1, -1, -1) if reverse else range(count)


def ordered(chip, part_refs, order_ref):
    for k, part_ref in enumerate(part_refs):
        order_ref[chip ^ k] = part_ref[...]


def advance(order_ref, source, start, heads, mdim, state):
    part_ref = order_ref.at[source]
    rows = state.shape[0]
    return times(get_logs(part_ref, heads), start, mdim, state) + part_ref[0:rows, :].astype(F32)


def total_kernel(reverse, heads, mdim, me_ref, *rest):
    *part_refs, out_ref, order_ref = rest
    count = len(part_refs)
    chip = me_ref[0] // 2 % count
    ordered(chip, part_refs, order_ref)
    start = me_ref[0] % 2 * (heads // 2) + chip * (heads // 2 // count)
    state = jnp.zeros(out_ref.shape, F32)
    for source in steps(count, reverse):
        state = advance(order_ref, source, start, heads, mdim, state)
    out_ref[...] = state.astype(BF16)


def scan_kernel(reverse, heads, mdim, me_ref, carry_ref, *rest):
    *refs, order_ref, result_ref = rest
    count = len(refs) // 2
    chip = me_ref[0] // 2 % count
    ordered(chip, refs[:count], order_ref)
    start = me_ref[0] % 2 * (heads // 2) + chip * (heads // 2 // count)
    state = carry_ref[...].astype(F32)
    for source in steps(count, reverse):
        result_ref[source] = state.astype(BF16)
        state = advance(order_ref, source, start, heads, mdim, state)
    for k, out_ref in enumerate(refs[count:]):
        out_ref[...] = result_ref[chip ^ k]


def core_kernel(reverse, me_ref, sum_ref, keep_ref, got_ref, *rest):
    *part_refs, mine_ref, send_ref, order_ref = rest
    count = len(part_refs)
    heads = sum_ref.shape[1]
    half = keep_ref.shape[0]
    core = me_ref[0] % 2
    chip = me_ref[0] // 2 % count
    slice_rows = part_refs[0].shape[0]
    for k, part_ref in enumerate(part_refs):
        start = pl.multiple_of((chip ^ k) * slice_rows, slice_rows)
        order_ref[pl.ds(start, slice_rows), :] = part_ref[...]
    first = core == (1 if reverse else 0)
    logs = jnp.where(first, sum_ref[sum_ref.shape[0] - 1 :, :], get_logs(got_ref, heads))
    own = jnp.where(first, keep_ref[...].astype(F32), got_ref[0:half, :].astype(F32))
    incoming = order_ref[...].astype(F32)
    passed = times(logs, core * heads // 2, 2 * half // heads, incoming) + own
    mine_ref[...] = jnp.where(first, incoming, passed).astype(BF16)
    send_ref[...] = jnp.where(first, passed, incoming).astype(BF16)


def whole_state(me_ref, mine_ref, other_ref, both_ref):
    core = me_ref[0] % 2
    both_ref[core] = mine_ref[...]
    both_ref[1 - core] = other_ref[...]
    _, half, nstate = both_ref.shape
    return both_ref[...].reshape(2 * half, nstate)


def mixer_kernel(
    me_ref,
    input_ref,
    write_ref,
    read_ref,
    sum_ref,
    turned_ref,
    grow_ref,
    gate_ref,
    mine_ref,
    other_ref,
    gated_ref,
    inverse_ref,
    active_ref,
    slope_ref,
    both_ref,
    out_ref,
):
    rows, channels = input_ref.shape
    mheads = sum_ref.shape[1]
    mdim = channels // mheads
    cumulated, turned = sum_ref[...], turned_ref[...]
    carried = nt(read_ref[...], whole_state(me_ref, mine_ref, other_ref, both_ref))
    out_ref[...] = grow_ref[...] * carried
    products = nt(read_ref[...], write_ref[...])
    causal = iota((rows, rows), 0) >= iota((rows, rows), 1)

    def weights_of(head):
        spread = cumulated[:, head : head + 1] - turned[head : head + 1, :]
        return (jnp.exp(jnp.where(causal, spread, -jnp.inf)) * products).astype(BF16)

    for pair in range(mheads // 2):
        lanes = slice(pair * 2 * mdim, (pair + 1) * 2 * mdim)
        weights = jnp.concatenate([weights_of(2 * pair), weights_of(2 * pair + 1)], axis=1)
        out_ref[:, lanes] += nn(weights, split_pair(input_ref[:, lanes], mdim))

    mixer_out = out_ref[...]
    gate = gate_ref[...].astype(F32)
    sigmoid = jax.nn.sigmoid(gate)
    active = gate * sigmoid
    gated = mixer_out * active
    active_ref[...] = active
    gated_ref[...] = gated
    slope_ref[...] = mixer_out * sigmoid * (1.0 + gate * (1.0 - sigmoid))
    inverse = lax.rsqrt(jnp.mean(gated * gated, axis=-1, keepdims=True) + EPSILON)
    inverse_ref[...] = jnp.broadcast_to(inverse, inverse_ref.shape)


def attention_kernel(
    in_kernel, ctx_size, me_ref, query_ref, grad_ref, *rest
):
    plane_refs, rest = rest[:4], rest[4:]
    if in_kernel:
        keep_ref, give_ref, gathered_ref, acc_ref, raw_ref, back_ref, query_acc_ref = rest
    else:
        query_out_ref, pack_ref, gathered_ref, acc_ref, raw_ref, back_ref = rest
    tiles, wide, head_dim = query_ref.shape
    rows = gathered_ref.shape[1]
    tile = rows // tiles
    heads = wide // tile
    me = me_ref[0]
    scale = 1.0 / math.sqrt(head_dim)
    base2 = scale * math.log2(math.e)
    per = rows // ctx_size
    for offset, plane_ref in enumerate(plane_refs):
        for level in range(ctx_size // 4):
            gathered_ref[me ^ (4 * level + offset)] = plane_ref[level]

    def keys_of(b):
        return gathered_ref[:, b * tile : (b + 1) * tile, 0:head_dim].reshape(
            ctx_size * tile, head_dim
        )

    def values_of(b):
        return gathered_ref[:, b * tile : (b + 1) * tile, head_dim : 2 * head_dim].reshape(
            ctx_size * tile, head_dim
        )

    key_row = iota((ctx_size * tile, wide), 0)
    key_place = (key_row % tile) * ctx_size + key_row // tile
    query_place = (iota((ctx_size * tile, wide), 1) % tile) * ctx_size + me
    visible = key_place <= query_place

    def score(t):
        slot = t % 2
        query = query_ref[t]
        highest = None
        for b in range(t, -1, -1):
            raw = nt(keys_of(b), query)
            if b == t:
                raw = jnp.where(visible, raw, -jnp.inf)
            raw_ref[slot, b] = raw
            block_high = jnp.max(raw, axis=0, keepdims=True)
            highest = block_high if highest is None else jnp.maximum(highest, block_high)
        return highest

    def weigh(t, highest):
        slot = t % 2
        grad = grad_ref[t]
        total = jnp.zeros((1, wide), F32)
        delta = jnp.zeros((1, wide), F32)
        for b in range(t + 1):
            probs = jnp.exp2((raw_ref[slot, b] - highest) * base2)
            back = nt(values_of(b), grad)
            raw_ref[slot, b] = probs
            back_ref[slot, b] = back
            total = total + jnp.sum(probs, axis=0, keepdims=True)
            delta = delta + jnp.sum(probs * back, axis=0, keepdims=True)
        inverse = 1.0 / total
        return inverse, delta * inverse

    def gather(t, inverse, delta):
        slot = t % 2
        query, grad = query_ref[t], grad_ref[t]
        query_grad = jnp.zeros((head_dim, wide), F32)
        for b in range(t + 1):
            weights = raw_ref[slot, b] * inverse
            score_grad = (weights * (back_ref[slot, b] - delta)).astype(BF16)
            value_part = nn(weights.astype(BF16), grad).reshape(ctx_size, tile, head_dim)
            key_part = nn(score_grad, query).reshape(ctx_size, tile, head_dim)
            here = slice(b * tile, (b + 1) * tile)
            if t == tiles - 1:
                acc_ref[:, here, 0:head_dim] = key_part
                acc_ref[:, here, head_dim:] = value_part
            else:
                acc_ref[:, here, 0:head_dim] += key_part
                acc_ref[:, here, head_dim:] += value_part
            query_grad = query_grad + tn(keys_of(b), score_grad)
        turned = (query_grad * scale).T
        by_head = [turned[h * tile : (h + 1) * tile, :] for h in range(heads)]
        if in_kernel:
            pairs = [
                jnp.concatenate(by_head[h : h + 2], axis=1) for h in range(0, heads, 2)
            ]
            for k in range(tile // per):
                rows_here = [p[k * per : (k + 1) * per, :] for p in pairs]
                query_acc_ref[t * (tile // per) + k] = jnp.concatenate(rows_here, axis=0)
        else:
            for h in range(heads):
                query_out_ref[t * tile : (t + 1) * tile, h * head_dim : (h + 1) * head_dim] = (
                    by_head[h].astype(BF16)
                )

    last = tiles - 1
    state = weigh(last, score(last))
    for t in range(last, -1, -1):
        if t:
            highest = score(t - 1)
        gather(t, *state)
        if t:
            state = weigh(t - 1, highest)

    both = jnp.where(iota((1, 1, 2 * head_dim), 2) < head_dim, scale, 1.0)
    if in_kernel:
        for chip in range(ctx_size // 2):
            for out_ref, core in ((keep_ref, me % 2), (give_ref, 1 - me % 2)):
                target = 2 * chip + core
                start = pl.multiple_of(target * per, per)
                block = acc_ref[:, pl.ds(start, per), :] * both
                out_ref[chip, 0:rows, :] = block.reshape(rows, 2 * head_dim).astype(BF16)
                out_ref[chip, rows:, :] = query_acc_ref[target].astype(BF16)
    else:
        pack_ref[...] = (acc_ref[...] * both).astype(BF16)


def join_kernel(me_ref, keep_ref, got_ref, *out_refs):
    mid = keep_ref.shape[1]
    rows = 2 * mid - out_refs[0].shape[0]
    chip = me_ref[0] // 2
    for k, out_ref in enumerate(out_refs):
        target = chip ^ k
        both = keep_ref[target, 0:rows, :].astype(F32) + got_ref[target, 0:rows, :].astype(F32)
        out_ref[0:rows, :] = both.astype(BF16)
        out_ref[rows:mid, :] = keep_ref[target, rows:, :]
        out_ref[mid:, :] = got_ref[target, rows:, :]


def in_token_order(ctx_size, devices, grads):
    rows = grads.shape[0]
    per = rows // ctx_size
    token, came = iota((rows, rows), 0), iota((rows, rows), 1)
    order = (token == (came % per) * ctx_size + devices(came // per)).astype(BF16)
    return nn(order, grads).astype(BF16)


def gate_kernel(
    order,
    me_ref,
    weight_ref,
    gated_ref,
    inverse_ref,
    active_ref,
    gain_ref,
    read_ref,
    grow_ref,
    sum_ref,
    *rest,
):
    *part_refs, gated_grad_ref, grad_out_ref, keep_ref, give_ref, grown_ref = rest
    rows = gated_ref.shape[0]
    chips = len(part_refs)
    ctx_size = 2 * chips
    per = rows // ctx_size
    part_refs = [part_refs[order.index(k)] for k in range(chips)]
    me = me_ref[0]
    sums = part_refs[0][0:rows, :].astype(F32)
    for part_ref in part_refs[1:]:
        sums = sums + part_ref[0:rows, :].astype(F32)
    kv_grads = in_token_order(ctx_size, lambda place: place, sums.astype(BF16))
    extra = (part_refs[0].shape[0] - rows) // 2
    query_rows = [part_ref[rows:, :].astype(F32) for part_ref in part_refs]
    columns = []
    for part in range(extra // per):
        blocks = [
            block[core * extra + part * per : core * extra + (part + 1) * per, :]
            for core in range(2)
            for block in query_rows
        ]
        columns.append(jnp.concatenate(blocks, axis=0))
    query_grads = in_token_order(
        ctx_size,
        lambda place: (2 * (place % chips) + place // chips) ^ me,
        jnp.concatenate(columns, axis=1).astype(BF16),
    )
    grads = jnp.concatenate([query_grads, kv_grads], axis=1)
    mixer_grad = nt(grads, weight_ref[...]).astype(BF16).astype(F32)

    gated = gated_ref[...]
    inverse = inverse_ref[:, 0:1]
    scaled = gain_ref[...] * mixer_grad
    mean = jnp.mean(scaled * gated, axis=-1, keepdims=True)
    gated_grad = scaled * inverse - gated * (mean * inverse * inverse * inverse)
    gated_grad_ref[...] = gated_grad
    out_grad = (gated_grad * active_ref[...]).astype(BF16)
    grad_out_ref[...] = out_grad
    grown_ref[...] = (out_grad.astype(F32) * grow_ref[...]).astype(BF16)
    last = sum_ref[rows - 1 :, :]
    write_halves(me % 2, last, grown_ref, read_ref, keep_ref, give_ref)


def local_kernel(
    me_ref,
    grad_ref,
    grown_ref,
    input_ref,
    write_ref,
    read_ref,
    sum_ref,
    turned_ref,
    mine_ref,
    other_ref,
    gated_grad_ref,
    slope_ref,
    value_ref,
    write_out_ref,
    read_out_ref,
    gate_out_ref,
    both_ref,
):
    rows, channels = input_ref.shape
    mheads = sum_ref.shape[1]
    mdim = channels // mheads
    gate_out_ref[...] = gated_grad_ref[...] * slope_ref[...]
    cumulated, turned = sum_ref[...], turned_ref[...]
    turned_products = nt(write_ref[...], read_ref[...])
    causal = iota((rows, rows), 0) >= iota((rows, rows), 1)
    later = iota((rows, rows), 0) <= iota((rows, rows), 1)
    pair_sum = jnp.zeros((rows, rows), F32)

    def decays_of(head):
        spread = cumulated[:, head : head + 1] - turned[head : head + 1, :]
        return jnp.exp(jnp.where(causal, spread, -jnp.inf))

    def turned_weights_of(head):
        spread = turned[head : head + 1, :] - cumulated[:, head : head + 1]
        return (jnp.exp(jnp.where(later, spread, -jnp.inf)) * turned_products).astype(BF16)

    for pair in range(mheads // 2):
        lanes = slice(pair * 2 * mdim, (pair + 1) * 2 * mdim)
        grads = split_pair(grad_ref[:, lanes], mdim)
        weights = jnp.concatenate(
            [turned_weights_of(2 * pair), turned_weights_of(2 * pair + 1)], axis=1
        )
        value_ref[:, lanes] = nn(weights, grads)
        pairs = nt(grads, input_ref[:, lanes])
        pair_sum = (
            pair_sum + decays_of(2 * pair) * pairs[:rows] + decays_of(2 * pair + 1) * pairs[rows:]
        )
    pair_low = pair_sum.astype(BF16)
    incoming = whole_state(me_ref, mine_ref, other_ref, both_ref)
    read_out_ref[...] = nn(pair_low, write_ref[...]) + nn(grown_ref[...], incoming)
    write_out_ref[...] = tn(pair_low, read_ref[...])


def half_of(which, half):
    return pl.ds(pl.multiple_of(which * half, half), half)


def half_kernel(me_ref, scaled_ref, remain_ref, write_ref, mine_ref, half_ref, write_half_ref):
    lanes = half_of(me_ref[0] % 2, mine_ref.shape[0])
    half_ref[...] = remain_ref[:, lanes] * nt(write_ref[...], mine_ref[...])
    write_half_ref[...] = nn(scaled_ref[:, lanes], mine_ref[...])


def final_kernel(
    me_ref,
    value_ref,
    write_part_ref,
    half_ref,
    write_half_ref,
    scaled_ref,
    remain_ref,
    write_ref,
    other_ref,
    out_ref,
    write_out_ref,
):
    core = me_ref[0] % 2
    half = other_ref.shape[0]
    lanes = half_of(core, half)
    out_ref[:, lanes] = value_ref[:, lanes] + half_ref[...]
    lanes = half_of(1 - core, half)
    out_ref[:, lanes] = value_ref[:, lanes] + remain_ref[:, lanes] * nt(write_ref[...], other_ref[...])
    write_out_ref[...] = (
        write_part_ref[...] + write_half_ref[...] + nn(scaled_ref[:, lanes], other_ref[...])
    )


def crossed(array, bits):
    pairs = [(i, i ^ bits) for i in range(lax.axis_size("ctx"))]
    return lax.ppermute(array, "ctx", pairs)


def tied(arrays, after):
    return lax.optimization_barrier((arrays, after))[0]


def scan_slices(me, cumulated, keep, give, reverse):
    group = lax.axis_size("ctx") // 4
    half_rows, nstate = keep.shape
    got = crossed(give, 1)
    slices = call(
        functools.partial(chip_kernel, reverse),
        [struct((half_rows // group + EXTRA, nstate), BF16)] * group,
        [me, cumulated, keep, got],
        half_rows * nstate,
        smem=(0,),
        scratch=[pltpu.VMEM((half_rows, nstate), F32)],
    )
    return slices, got


def scan_parts(slices):
    return [slices[0]] + [crossed(slices[k], 2 * k) for k in range(1, len(slices))]


def scan_total(me, cumulated, keep, parts, reverse):
    group = len(parts)
    half_rows, nstate = keep.shape
    slice_rows = half_rows // group
    heads = cumulated.shape[1]
    (total,) = call(
        functools.partial(total_kernel, reverse, heads, 2 * half_rows // heads),
        [struct((slice_rows, nstate), BF16)],
        [me] + list(parts),
        half_rows * nstate,
        smem=(0,),
        scratch=[pltpu.VMEM((group, slice_rows + EXTRA, nstate), BF16)],
    )
    return total


def scan_carry(total, reverse):
    half = lax.axis_size("ctx") // 2
    if reverse:
        pairs = [(i + half, i) for i in range(half)]
    else:
        pairs = [(i, i + half) for i in range(half)]
    return lax.ppermute(total, "ctx", pairs)


def scan_back(me, cumulated, carry, keep, parts, reverse):
    group = len(parts)
    slice_rows, nstate = carry.shape
    heads = cumulated.shape[1]
    backs = call(
        functools.partial(scan_kernel, reverse, heads, 2 * keep.shape[0] // heads),
        [struct(carry.shape, BF16)] * group,
        [me, carry] + list(parts),
        group * slice_rows * nstate,
        smem=(0,),
        scratch=[
            pltpu.VMEM((group, slice_rows + EXTRA, nstate), BF16),
            pltpu.VMEM((group, slice_rows, nstate), BF16),
        ],
    )
    return backs


def scan_out(me, cumulated, returned, keep, got, reverse):
    mine, send = call(
        functools.partial(core_kernel, reverse),
        [struct(keep.shape, BF16)] * 2,
        [me, cumulated, keep, got] + list(returned),
        keep.size,
        smem=(0,),
        scratch=[pltpu.VMEM(keep.shape, BF16)],
    )
    return mine, crossed(send, 1)


def body(
    queries,
    keys,
    values,
    d_out,
    mixer_input,
    gate_input,
    state_write,
    state_read,
    log_decay,
    norm_gain,
    project_weight,
):
    ctx_size = lax.axis_size("ctx")
    ctx_index = lax.axis_index("ctx")
    rows, head_dim = keys.shape
    wide = queries.shape[1]
    channels = mixer_input.shape[1]
    nstate = state_write.shape[1]
    mheads = log_decay.shape[1]
    per = rows // ctx_size
    me = ctx_index.astype(jnp.int32).reshape(1)
    packed = jnp.pad(keys, ((0, 0), (0, head_dim))) + jnp.pad(values, ((0, 0), (head_dim, 0)))
    near_plane = [packed] + [crossed(packed, k) for k in range(4, ctx_size, 4)]
    (plane,) = call(
        plane_kernel,
        [struct((ctx_size // 4, rows, 2 * head_dim), BF16)],
        near_plane,
        rows * head_dim,
    )
    plane_other = crossed(plane, 1)
    half_states = [
        struct((channels // 2, nstate), BF16),
        struct((channels // 2 + EXTRA, nstate), BF16),
    ]
    tile = tile_of(rows)
    columns = tile * wide // head_dim
    stacked = struct((rows // tile, columns, head_dim), BF16)
    keep, give, scaled, remain, grow, cumulated, turned = call(
        state_kernel,
        [
            *half_states,
            struct((rows, channels), BF16),
            struct((rows, channels), F32),
            struct((rows, channels), F32),
            struct((rows, mheads), F32),
            struct((mheads, rows), F32),
        ],
        [me, mixer_input, state_write, tied(log_decay.T, packed)],
        2 * rows * channels * nstate,
        smem=(0,),
    )

    query_tiles, grad_tiles = call(
        stack_kernel, [stacked, stacked], [queries, d_out], rows * wide
    )
    slices, got = scan_slices(me, cumulated, keep, tied(give, plane), False)
    parts = scan_parts(slices)
    across = crossed(plane, 2)
    across_other = crossed(tied(across, (tuple(parts[1:]), query_tiles)), 1)

    total = scan_total(me, cumulated, keep, parts, False)
    carry = scan_carry(total, False)
    query_tiles = tied(query_tiles, total)

    in_kernel = per % 8 == 0
    flops = 10 * rows * wide * ctx_size * rows
    scratch = [
        pltpu.VMEM((ctx_size, rows, 2 * head_dim), BF16),
        pltpu.VMEM((ctx_size, rows, 2 * head_dim), F32),
        pltpu.VMEM((2, rows // tile, ctx_size * tile, columns), F32),
        pltpu.VMEM((2, rows // tile, ctx_size * tile, columns), F32),
    ]
    attention_args = [me, query_tiles, grad_tiles, plane, plane_other, across, across_other]
    chips = ctx_size // 2
    extra = per * wide // (2 * head_dim)
    if in_kernel:
        part = struct((chips, rows + extra, 2 * head_dim), BF16)
        kv_keep, kv_give = call(
            functools.partial(attention_kernel, True, ctx_size),
            [part, part],
            attention_args,
            flops,
            smem=(0,),
            scratch=scratch + [pltpu.VMEM((ctx_size, extra, 2 * head_dim), F32)],
        )
    else:
        query_grad, kv_grad = call(
            functools.partial(attention_kernel, False, ctx_size),
            [struct((rows, wide), BF16), struct((ctx_size, rows, 2 * head_dim), BF16)],
            attention_args,
            flops,
            smem=(0,),
            scratch=scratch,
        )
        by_target = kv_grad.reshape(ctx_size, ctx_size, per, 2 * head_dim).transpose(1, 0, 2, 3)
        by_pair = query_grad.reshape(ctx_size, per, -1, 2 * head_dim).transpose(0, 2, 1, 3)
        sent = jnp.concatenate(
            [
                by_target.reshape(ctx_size, rows, 2 * head_dim),
                by_pair.reshape(ctx_size, extra, 2 * head_dim),
            ],
            axis=1,
        ).reshape(chips, 2, rows + extra, 2 * head_dim)
        kv_keep = lax.dynamic_index_in_dim(sent, ctx_index % 2, 1, False)
        kv_give = lax.dynamic_index_in_dim(sent, 1 - ctx_index % 2, 1, False)

    carry, kv_keep, kv_give = lax.optimization_barrier((carry, kv_keep, kv_give))
    kv_got = crossed(kv_give, 1)
    backs = scan_back(me, cumulated, carry, keep, parts, False)
    sent = call(
        join_kernel,
        [struct((rows + 2 * extra, 2 * head_dim), BF16)] * chips,
        [me, kv_keep, tied(kv_got, backs[0])],
        chips * rows * 2 * head_dim,
        smem=(0,),
    )
    order = sorted(range(chips), key=lambda k: (-(k // 4), k % 2, -k))
    received = [crossed(sent[k], 2 * k) if k else sent[k] for k in order]
    returned = tied(tuple(scan_parts(backs)), tuple(received[:3]))
    incoming, incoming_other = scan_out(me, cumulated, returned, keep, got, False)

    both_states = pltpu.VMEM((2, channels // 2, nstate), BF16)
    whole = struct((rows, channels), F32)
    gated, inverse, active, slope = call(
        mixer_kernel,
        [whole, struct((rows, 128), F32), whole, whole],
        [
            me,
            mixer_input,
            state_write,
            state_read,
            cumulated,
            turned,
            grow,
            gate_input,
            incoming,
            incoming_other,
        ],
        2 * rows * channels * (nstate + rows),
        smem=(0,),
        scratch=[both_states, pltpu.VMEM((rows, channels), F32)],
    )
    gated_grad, out_grad, adjoint_keep, adjoint_give, grown = call(
        functools.partial(gate_kernel, order),
        [
            struct((rows, channels), F32),
            struct((rows, channels), BF16),
            *half_states,
            struct((rows, channels), BF16),
        ],
        [
            me,
            project_weight,
            gated,
            inverse,
            active,
            norm_gain.reshape(1, channels),
            state_read,
            grow,
            cumulated,
        ]
        + received,
        2 * rows * channels * (nstate + project_weight.shape[1]),
        smem=(0,),
    )
    value_part, write_part, read_gradient, gate_gradient = call(
        local_kernel,
        [
            struct((rows, channels), F32),
            struct((rows, nstate), F32),
            struct((rows, nstate), F32),
            whole,
        ],
        [
            me,
            out_grad,
            grown,
            mixer_input,
            state_write,
            state_read,
            cumulated,
            turned,
            incoming,
            incoming_other,
            gated_grad,
            slope,
        ],
        2 * rows * channels * (nstate + 2 * rows),
        smem=(0,),
        scratch=[both_states],
    )
    slices, got = scan_slices(me, cumulated, adjoint_keep, adjoint_give, True)
    parts = scan_parts(slices)
    carry = scan_carry(scan_total(me, cumulated, adjoint_keep, parts, True), True)
    carry = tied(carry, write_part)
    backs = scan_back(me, cumulated, carry, adjoint_keep, parts, True)
    adjoint, adjoint_other = scan_out(
        me, cumulated, scan_parts(backs), adjoint_keep, got, True
    )
    half_out, write_half = call(
        half_kernel,
        [struct((rows, channels // 2), F32), struct((rows, nstate), F32)],
        [me, scaled, remain, state_write, adjoint],
        2 * rows * channels * nstate,
        smem=(0,),
    )
    input_gradient, write_gradient = call(
        final_kernel,
        [whole, struct((rows, nstate), F32)],
        [
            me,
            value_part,
            write_part,
            half_out,
            write_half,
            scaled,
            remain,
            state_write,
            adjoint_other,
        ],
        2 * rows * channels * nstate,
        smem=(0,),
    )
    return (input_gradient, gate_gradient, write_gradient, read_gradient)


def solution(mesh):
    both = P("ctx", "groups")
    return jax.shard_map(
        body,
        mesh=mesh,
        in_specs=(both,) * 9 + (P("groups"), P(None, "groups")),
        out_specs=(both,) * 4,
        check_vma=False,
    )
```

```python
import functools
import math

import jax
import jax.numpy as jnp
from jax import lax
from jax.experimental import pallas as pl
from jax.experimental.pallas import tpu as pltpu
from jax.sharding import PartitionSpec as P

EPSILON = 1e-05
HIGHEST = lax.Precision.HIGHEST
F32 = jnp.float32
BF16 = jnp.bfloat16
EXTRA = 16
MIB = 1024 * 1024


def nn(a, b, **kw):
    return lax.dot_general(a, b, (((1,), (0,)), ((), ())), preferred_element_type=F32, **kw)


def nt(a, b, **kw):
    return lax.dot_general(a, b, (((1,), (1,)), ((), ())), preferred_element_type=F32, **kw)


def tn(a, b, **kw):
    return lax.dot_general(a, b, (((0,), (0,)), ((), ())), preferred_element_type=F32, **kw)


def iota(shape, dim):
    return lax.broadcasted_iota(jnp.int32, shape, dim)


def call(kernel, outs, args, flops, smem=(), scratch=(), spare=4 * MIB):
    specs = [
        pl.BlockSpec(memory_space=pltpu.SMEM if i in smem else pltpu.VMEM) for i in range(len(args))
    ]
    moved = sum(a.size * a.dtype.itemsize for a in args) + sum(
        math.prod(o.shape) * o.dtype.itemsize for o in outs
    )
    held = moved + sum(
        math.prod(s.shape) * jnp.dtype(s.dtype).itemsize for s in scratch
    )
    return pl.pallas_call(
        kernel,
        out_shape=tuple(outs),
        in_specs=specs,
        out_specs=tuple(pl.BlockSpec(memory_space=pltpu.VMEM) for _ in outs),
        scratch_shapes=list(scratch),
        compiler_params=pltpu.CompilerParams(vmem_limit_bytes=held + spare),
        cost_estimate=pl.CostEstimate(flops=flops, bytes_accessed=moved, transcendentals=0),
    )(*args)


def struct(shape, dtype):
    return jax.ShapeDtypeStruct(shape, dtype)


def running_sums(log_decay):
    rows = log_decay.shape[1]
    lower = (iota((rows, rows), 0) >= iota((rows, rows), 1)).astype(F32)
    upper = (iota((rows, rows), 0) <= iota((rows, rows), 1)).astype(F32)
    return nt(lower, log_decay, precision=HIGHEST), nn(log_decay, upper, precision=HIGHEST)


def spread_heads(per_head, mdim):
    rows, heads = per_head.shape
    first = iota((rows, 2 * mdim), 1) < mdim
    pairs = [
        jnp.where(first, per_head[:, h : h + 1], per_head[:, h + 1 : h + 2])
        for h in range(0, heads, 2)
    ]
    return jnp.concatenate(pairs, axis=1)


def split_pair(block, mdim):
    first = iota(block.shape, 1) < mdim
    zero = jnp.zeros_like(block)
    return jnp.concatenate([jnp.where(first, block, zero), jnp.where(first, zero, block)], axis=0)


def plane_kernel(*refs):
    *piece_refs, out_ref = refs
    for i, piece_ref in enumerate(piece_refs):
        out_ref[i] = piece_ref[...]


def tile_of(rows):
    return min(32, rows)


def stack_kernel(*refs):
    count = len(refs) // 2
    for ref, out_ref in zip(refs[:count], refs[count:]):
        tiles, wide, head_dim = out_ref.shape
        tile = ref.shape[0] // tiles
        for t in range(tiles):
            for h in range(wide // tile):
                out_ref[t, h * tile : (h + 1) * tile, :] = ref[
                    t * tile : (t + 1) * tile, h * head_dim : (h + 1) * head_dim
                ]


def put_logs(ref, logs):
    heads = logs.shape[1]
    high = logs.astype(BF16).astype(F32)
    middle = (logs - high).astype(BF16).astype(F32)
    low = (logs - high - middle).astype(BF16).astype(F32)
    place = iota((EXTRA, heads), 0)
    split = jnp.where(place == 0, high, jnp.where(place == 1, middle, low))
    wide = jnp.concatenate([split, jnp.zeros((EXTRA, ref.shape[1] - heads), F32)], axis=1)
    ref[ref.shape[0] - EXTRA :, :] = wide.astype(BF16)


def get_logs(ref, heads):
    parts = ref[ref.shape[0] - EXTRA :, 0:heads].astype(F32)
    return parts[0:1, :] + parts[1:2, :] + parts[2:3, :]


def times(logs, start, mdim, state):
    head = iota(logs.shape, 1)
    blocks = []
    for i in range(state.shape[0] // mdim):
        log = jnp.sum(jnp.where(head == start + i, logs, 0.0), axis=1, keepdims=True)
        blocks.append(jnp.exp(log) * state[i * mdim : (i + 1) * mdim, :])
    return jnp.concatenate(blocks, axis=0)


def write_halves(core, logs, scaled_ref, other_ref, keep_ref, give_ref):
    half = keep_ref.shape[0]
    for out_ref, which in ((keep_ref, core), (give_ref, 1 - core)):
        lanes = pl.ds(pl.multiple_of(which * half, half), half)
        out_ref[0:half, :] = tn(scaled_ref[:, lanes], other_ref[...]).astype(BF16)
    put_logs(give_ref, logs)


def state_kernel(
    me_ref,
    input_ref,
    write_ref,
    decay_ref,
    keep_ref,
    give_ref,
    scaled_ref,
    remain_ref,
    grow_ref,
    sum_ref,
    turned_ref,
):
    cumulated, turned = running_sums(decay_ref[...])
    sum_ref[...], turned_ref[...] = cumulated, turned
    mdim = input_ref.shape[1] // cumulated.shape[1]
    last = cumulated[-1:, :]
    remain_ref[...] = spread_heads(jnp.exp(last - cumulated), mdim)
    grow_ref[...] = spread_heads(jnp.exp(cumulated), mdim)
    scaled_ref[...] = (input_ref[...].astype(F32) * remain_ref[...]).astype(BF16)
    write_halves(me_ref[0] % 2, last, scaled_ref, write_ref, keep_ref, give_ref)


def chip_kernel(reverse, me_ref, sum_ref, keep_ref, got_ref, *rest):
    *out_refs, total_ref = rest
    heads = sum_ref.shape[1]
    half = keep_ref.shape[0]
    mdim = 2 * half // heads
    core = me_ref[0] % 2
    chip = me_ref[0] // 2 % len(out_refs)
    slice_rows = out_refs[0].shape[0] - EXTRA
    own_logs = sum_ref[sum_ref.shape[0] - 1 :, :]
    got_logs = get_logs(got_ref, heads)
    keep, got = keep_ref[...].astype(F32), got_ref[0:half, :].astype(F32)
    first = core == (1 if reverse else 0)
    decayed = times(jnp.where(first, got_logs, own_logs), core * heads // 2, mdim, jnp.where(first, keep, got))
    total_ref[...] = decayed + jnp.where(first, got, keep)
    for k, out_ref in enumerate(out_refs):
        start = pl.multiple_of((chip ^ k) * slice_rows, slice_rows)
        out_ref[0:slice_rows, :] = total_ref[pl.ds(start, slice_rows), :].astype(BF16)
        put_logs(out_ref, own_logs + got_logs)


def steps(count, reverse):
    return range(count - 1, -1, -1) if reverse else range(count)


def ordered(chip, part_refs, order_ref):
    for k, part_ref in enumerate(part_refs):
        order_ref[chip ^ k] = part_ref[...]


def advance(order_ref, source, start, heads, mdim, state):
    part_ref = order_ref.at[source]
    rows = state.shape[0]
    return times(get_logs(part_ref, heads), start, mdim, state) + part_ref[0:rows, :].astype(F32)


def total_kernel(reverse, heads, mdim, me_ref, *rest):
    *part_refs, out_ref, order_ref = rest
    count = len(part_refs)
    chip = me_ref[0] // 2 % count
    ordered(chip, part_refs, order_ref)
    start = me_ref[0] % 2 * (heads // 2) + chip * (heads // 2 // count)
    state = jnp.zeros(out_ref.shape, F32)
    for source in steps(count, reverse):
        state = advance(order_ref, source, start, heads, mdim, state)
    out_ref[...] = state.astype(BF16)


def scan_kernel(reverse, heads, mdim, me_ref, carry_ref, *rest):
    *refs, order_ref, result_ref = rest
    count = len(refs) // 2
    chip = me_ref[0] // 2 % count
    ordered(chip, refs[:count], order_ref)
    start = me_ref[0] % 2 * (heads // 2) + chip * (heads // 2 // count)
    state = carry_ref[...].astype(F32)
    for source in steps(count, reverse):
        result_ref[source] = state.astype(BF16)
        state = advance(order_ref, source, start, heads, mdim, state)
    for k, out_ref in enumerate(refs[count:]):
        out_ref[...] = result_ref[chip ^ k]


def core_kernel(reverse, me_ref, sum_ref, keep_ref, got_ref, *rest):
    *part_refs, mine_ref, send_ref, order_ref = rest
    count = len(part_refs)
    heads = sum_ref.shape[1]
    half = keep_ref.shape[0]
    core = me_ref[0] % 2
    chip = me_ref[0] // 2 % count
    slice_rows = part_refs[0].shape[0]
    for k, part_ref in enumerate(part_refs):
        start = pl.multiple_of((chip ^ k) * slice_rows, slice_rows)
        order_ref[pl.ds(start, slice_rows), :] = part_ref[...]
    first = core == (1 if reverse else 0)
    logs = jnp.where(first, sum_ref[sum_ref.shape[0] - 1 :, :], get_logs(got_ref, heads))
    own = jnp.where(first, keep_ref[...].astype(F32), got_ref[0:half, :].astype(F32))
    incoming = order_ref[...].astype(F32)
    passed = times(logs, core * heads // 2, 2 * half // heads, incoming) + own
    mine_ref[...] = jnp.where(first, incoming, passed).astype(BF16)
    send_ref[...] = jnp.where(first, passed, incoming).astype(BF16)


def whole_state(me_ref, mine_ref, other_ref, both_ref):
    core = me_ref[0] % 2
    both_ref[core] = mine_ref[...]
    both_ref[1 - core] = other_ref[...]
    _, half, nstate = both_ref.shape
    return both_ref[...].reshape(2 * half, nstate)


def mixer_kernel(
    me_ref,
    input_ref,
    write_ref,
    read_ref,
    sum_ref,
    turned_ref,
    grow_ref,
    gate_ref,
    mine_ref,
    other_ref,
    gated_ref,
    inverse_ref,
    active_ref,
    slope_ref,
    both_ref,
    out_ref,
):
    rows, channels = input_ref.shape
    mheads = sum_ref.shape[1]
    mdim = channels // mheads
    cumulated, turned = sum_ref[...], turned_ref[...]
    carried = nt(read_ref[...], whole_state(me_ref, mine_ref, other_ref, both_ref))
    out_ref[...] = grow_ref[...] * carried
    products = nt(read_ref[...], write_ref[...])
    causal = iota((rows, rows), 0) >= iota((rows, rows), 1)

    def weights_of(head):
        spread = cumulated[:, head : head + 1] - turned[head : head + 1, :]
        return (jnp.exp(jnp.where(causal, spread, -jnp.inf)) * products).astype(BF16)

    for pair in range(mheads // 2):
        lanes = slice(pair * 2 * mdim, (pair + 1) * 2 * mdim)
        weights = jnp.concatenate([weights_of(2 * pair), weights_of(2 * pair + 1)], axis=1)
        out_ref[:, lanes] += nn(weights, split_pair(input_ref[:, lanes], mdim))

    mixer_out = out_ref[...]
    gate = gate_ref[...].astype(F32)
    sigmoid = jax.nn.sigmoid(gate)
    active = gate * sigmoid
    gated = mixer_out * active
    active_ref[...] = active
    gated_ref[...] = gated
    slope_ref[...] = mixer_out * sigmoid * (1.0 + gate * (1.0 - sigmoid))
    inverse = lax.rsqrt(jnp.mean(gated * gated, axis=-1, keepdims=True) + EPSILON)
    inverse_ref[...] = jnp.broadcast_to(inverse, inverse_ref.shape)


def attention_kernel(
    in_kernel, ctx_size, me_ref, query_ref, grad_ref, *rest
):
    plane_refs, rest = rest[:4], rest[4:]
    if in_kernel:
        keep_ref, give_ref, gathered_ref, acc_ref, raw_ref, back_ref, query_acc_ref = rest
    else:
        query_out_ref, pack_ref, gathered_ref, acc_ref, raw_ref, back_ref = rest
    tiles, wide, head_dim = query_ref.shape
    rows = gathered_ref.shape[1]
    tile = rows // tiles
    heads = wide // tile
    me = me_ref[0]
    scale = 1.0 / math.sqrt(head_dim)
    base2 = scale * math.log2(math.e)
    per = rows // ctx_size
    for offset, plane_ref in enumerate(plane_refs):
        for level in range(ctx_size // 4):
            gathered_ref[me ^ (4 * level + offset)] = plane_ref[level]

    def keys_of(b):
        return gathered_ref[:, b * tile : (b + 1) * tile, 0:head_dim].reshape(
            ctx_size * tile, head_dim
        )

    def values_of(b):
        return gathered_ref[:, b * tile : (b + 1) * tile, head_dim : 2 * head_dim].reshape(
            ctx_size * tile, head_dim
        )

    key_row = iota((ctx_size * tile, wide), 0)
    key_place = (key_row % tile) * ctx_size + key_row // tile
    query_place = (iota((ctx_size * tile, wide), 1) % tile) * ctx_size + me
    visible = key_place <= query_place

    def score(t):
        slot = t % 2
        query = query_ref[t]
        highest = None
        for b in range(t, -1, -1):
            raw = nt(keys_of(b), query)
            if b == t:
                raw = jnp.where(visible, raw, -jnp.inf)
            raw_ref[slot, b] = raw
            block_high = jnp.max(raw, axis=0, keepdims=True)
            highest = block_high if highest is None else jnp.maximum(highest, block_high)
        return highest

    def weigh(t, highest):
        slot = t % 2
        grad = grad_ref[t]
        total = jnp.zeros((1, wide), F32)
        delta = jnp.zeros((1, wide), F32)
        for b in range(t + 1):
            probs = jnp.exp2((raw_ref[slot, b] - highest) * base2)
            back = nt(values_of(b), grad)
            raw_ref[slot, b] = probs
            back_ref[slot, b] = back
            total = total + jnp.sum(probs, axis=0, keepdims=True)
            delta = delta + jnp.sum(probs * back, axis=0, keepdims=True)
        inverse = 1.0 / total
        return inverse, delta * inverse

    def gather(t, inverse, delta):
        slot = t % 2
        query, grad = query_ref[t], grad_ref[t]
        query_grad = jnp.zeros((head_dim, wide), F32)
        for b in range(t + 1):
            weights = raw_ref[slot, b] * inverse
            score_grad = (weights * (back_ref[slot, b] - delta)).astype(BF16)
            value_part = nn(weights.astype(BF16), grad).reshape(ctx_size, tile, head_dim)
            key_part = nn(score_grad, query).reshape(ctx_size, tile, head_dim)
            here = slice(b * tile, (b + 1) * tile)
            if t == tiles - 1:
                acc_ref[:, here, 0:head_dim] = key_part
                acc_ref[:, here, head_dim:] = value_part
            else:
                acc_ref[:, here, 0:head_dim] += key_part
                acc_ref[:, here, head_dim:] += value_part
            query_grad = query_grad + tn(keys_of(b), score_grad)
        turned = (query_grad * scale).T
        by_head = [turned[h * tile : (h + 1) * tile, :] for h in range(heads)]
        if in_kernel:
            pairs = [
                jnp.concatenate(by_head[h : h + 2], axis=1) for h in range(0, heads, 2)
            ]
            for k in range(tile // per):
                rows_here = [p[k * per : (k + 1) * per, :] for p in pairs]
                query_acc_ref[t * (tile // per) + k] = jnp.concatenate(rows_here, axis=0)
        else:
            for h in range(heads):
                query_out_ref[t * tile : (t + 1) * tile, h * head_dim : (h + 1) * head_dim] = (
                    by_head[h].astype(BF16)
                )

    last = tiles - 1
    state = weigh(last, score(last))
    for t in range(last, -1, -1):
        if t:
            highest = score(t - 1)
        gather(t, *state)
        if t:
            state = weigh(t - 1, highest)

    both = jnp.where(iota((1, 1, 2 * head_dim), 2) < head_dim, scale, 1.0)
    if in_kernel:
        for chip in range(ctx_size // 2):
            for out_ref, core in ((keep_ref, me % 2), (give_ref, 1 - me % 2)):
                target = 2 * chip + core
                start = pl.multiple_of(target * per, per)
                block = acc_ref[:, pl.ds(start, per), :] * both
                out_ref[chip, 0:rows, :] = block.reshape(rows, 2 * head_dim).astype(BF16)
                out_ref[chip, rows:, :] = query_acc_ref[target].astype(BF16)
    else:
        pack_ref[...] = (acc_ref[...] * both).astype(BF16)


def join_kernel(me_ref, keep_ref, got_ref, *out_refs):
    mid = keep_ref.shape[1]
    rows = 2 * mid - out_refs[0].shape[0]
    chip = me_ref[0] // 2
    for k, out_ref in enumerate(out_refs):
        target = chip ^ k
        both = keep_ref[target, 0:rows, :].astype(F32) + got_ref[target, 0:rows, :].astype(F32)
        out_ref[0:rows, :] = both.astype(BF16)
        out_ref[rows:mid, :] = keep_ref[target, rows:, :]
        out_ref[mid:, :] = got_ref[target, rows:, :]


def in_token_order(ctx_size, devices, grads):
    rows = grads.shape[0]
    per = rows // ctx_size
    token, came = iota((rows, rows), 0), iota((rows, rows), 1)
    order = (token == (came % per) * ctx_size + devices(came // per)).astype(BF16)
    return nn(order, grads).astype(BF16)


def gate_kernel(
    order,
    me_ref,
    weight_ref,
    gated_ref,
    inverse_ref,
    active_ref,
    gain_ref,
    read_ref,
    grow_ref,
    sum_ref,
    *rest,
):
    *part_refs, gated_grad_ref, grad_out_ref, keep_ref, give_ref, grown_ref = rest
    rows = gated_ref.shape[0]
    chips = len(part_refs)
    ctx_size = 2 * chips
    per = rows // ctx_size
    part_refs = [part_refs[order.index(k)] for k in range(chips)]
    me = me_ref[0]
    sums = part_refs[0][0:rows, :].astype(F32)
    for part_ref in part_refs[1:]:
        sums = sums + part_ref[0:rows, :].astype(F32)
    kv_grads = in_token_order(ctx_size, lambda place: place, sums.astype(BF16))
    extra = (part_refs[0].shape[0] - rows) // 2
    query_rows = [part_ref[rows:, :].astype(F32) for part_ref in part_refs]
    columns = []
    for part in range(extra // per):
        blocks = [
            block[core * extra + part * per : core * extra + (part + 1) * per, :]
            for core in range(2)
            for block in query_rows
        ]
        columns.append(jnp.concatenate(blocks, axis=0))
    query_grads = in_token_order(
        ctx_size,
        lambda place: (2 * (place % chips) + place // chips) ^ me,
        jnp.concatenate(columns, axis=1).astype(BF16),
    )
    grads = jnp.concatenate([query_grads, kv_grads], axis=1)
    mixer_grad = nt(grads, weight_ref[...]).astype(BF16).astype(F32)

    gated = gated_ref[...]
    inverse = inverse_ref[:, 0:1]
    scaled = gain_ref[...] * mixer_grad
    mean = jnp.mean(scaled * gated, axis=-1, keepdims=True)
    gated_grad = scaled * inverse - gated * (mean * inverse * inverse * inverse)
    gated_grad_ref[...] = gated_grad
    out_grad = (gated_grad * active_ref[...]).astype(BF16)
    grad_out_ref[...] = out_grad
    grown_ref[...] = (out_grad.astype(F32) * grow_ref[...]).astype(BF16)
    last = sum_ref[rows - 1 :, :]
    write_halves(me % 2, last, grown_ref, read_ref, keep_ref, give_ref)


def local_kernel(
    me_ref,
    grad_ref,
    grown_ref,
    input_ref,
    write_ref,
    read_ref,
    sum_ref,
    turned_ref,
    mine_ref,
    other_ref,
    gated_grad_ref,
    slope_ref,
    value_ref,
    write_out_ref,
    read_out_ref,
    gate_out_ref,
    both_ref,
):
    rows, channels = input_ref.shape
    mheads = sum_ref.shape[1]
    mdim = channels // mheads
    gate_out_ref[...] = gated_grad_ref[...] * slope_ref[...]
    cumulated, turned = sum_ref[...], turned_ref[...]
    turned_products = nt(write_ref[...], read_ref[...])
    causal = iota((rows, rows), 0) >= iota((rows, rows), 1)
    later = iota((rows, rows), 0) <= iota((rows, rows), 1)
    pair_sum = jnp.zeros((rows, rows), F32)

    def decays_of(head):
        spread = cumulated[:, head : head + 1] - turned[head : head + 1, :]
        return jnp.exp(jnp.where(causal, spread, -jnp.inf))

    def turned_weights_of(head):
        spread = turned[head : head + 1, :] - cumulated[:, head : head + 1]
        return (jnp.exp(jnp.where(later, spread, -jnp.inf)) * turned_products).astype(BF16)

    for pair in range(mheads // 2):
        lanes = slice(pair * 2 * mdim, (pair + 1) * 2 * mdim)
        grads = split_pair(grad_ref[:, lanes], mdim)
        weights = jnp.concatenate(
            [turned_weights_of(2 * pair), turned_weights_of(2 * pair + 1)], axis=1
        )
        value_ref[:, lanes] = nn(weights, grads)
        pairs = nt(grads, input_ref[:, lanes])
        pair_sum = (
            pair_sum + decays_of(2 * pair) * pairs[:rows] + decays_of(2 * pair + 1) * pairs[rows:]
        )
    pair_low = pair_sum.astype(BF16)
    incoming = whole_state(me_ref, mine_ref, other_ref, both_ref)
    read_out_ref[...] = nn(pair_low, write_ref[...]) + nn(grown_ref[...], incoming)
    write_out_ref[...] = tn(pair_low, read_ref[...])


def half_of(which, half):
    return pl.ds(pl.multiple_of(which * half, half), half)


def half_kernel(me_ref, scaled_ref, remain_ref, write_ref, mine_ref, half_ref, write_half_ref):
    lanes = half_of(me_ref[0] % 2, mine_ref.shape[0])
    half_ref[...] = remain_ref[:, lanes] * nt(write_ref[...], mine_ref[...])
    write_half_ref[...] = nn(scaled_ref[:, lanes], mine_ref[...])


def final_kernel(
    me_ref,
    value_ref,
    write_part_ref,
    half_ref,
    write_half_ref,
    scaled_ref,
    remain_ref,
    write_ref,
    other_ref,
    out_ref,
    write_out_ref,
):
    core = me_ref[0] % 2
    half = other_ref.shape[0]
    lanes = half_of(core, half)
    out_ref[:, lanes] = value_ref[:, lanes] + half_ref[...]
    lanes = half_of(1 - core, half)
    out_ref[:, lanes] = value_ref[:, lanes] + remain_ref[:, lanes] * nt(write_ref[...], other_ref[...])
    write_out_ref[...] = (
        write_part_ref[...] + write_half_ref[...] + nn(scaled_ref[:, lanes], other_ref[...])
    )


def crossed(array, bits):
    pairs = [(i, i ^ bits) for i in range(lax.axis_size("ctx"))]
    return lax.ppermute(array, "ctx", pairs)


def tied(arrays, after):
    return lax.optimization_barrier((arrays, after))[0]


def scan_slices(me, cumulated, keep, give, reverse):
    group = lax.axis_size("ctx") // 4
    half_rows, nstate = keep.shape
    got = crossed(give, 1)
    slices = call(
        functools.partial(chip_kernel, reverse),
        [struct((half_rows // group + EXTRA, nstate), BF16)] * group,
        [me, cumulated, keep, got],
        half_rows * nstate,
        smem=(0,),
        scratch=[pltpu.VMEM((half_rows, nstate), F32)],
    )
    return slices, got


def scan_parts(slices):
    return [slices[0]] + [crossed(slices[k], 2 * k) for k in range(1, len(slices))]


def scan_total(me, cumulated, keep, parts, reverse):
    group = len(parts)
    half_rows, nstate = keep.shape
    slice_rows = half_rows // group
    heads = cumulated.shape[1]
    (total,) = call(
        functools.partial(total_kernel, reverse, heads, 2 * half_rows // heads),
        [struct((slice_rows, nstate), BF16)],
        [me] + list(parts),
        half_rows * nstate,
        smem=(0,),
        scratch=[pltpu.VMEM((group, slice_rows + EXTRA, nstate), BF16)],
    )
    return total


def scan_carry(total, reverse):
    half = lax.axis_size("ctx") // 2
    if reverse:
        pairs = [(i + half, i) for i in range(half)]
    else:
        pairs = [(i, i + half) for i in range(half)]
    return lax.ppermute(total, "ctx", pairs)


def scan_back(me, cumulated, carry, keep, parts, reverse):
    group = len(parts)
    slice_rows, nstate = carry.shape
    heads = cumulated.shape[1]
    backs = call(
        functools.partial(scan_kernel, reverse, heads, 2 * keep.shape[0] // heads),
        [struct(carry.shape, BF16)] * group,
        [me, carry] + list(parts),
        group * slice_rows * nstate,
        smem=(0,),
        scratch=[
            pltpu.VMEM((group, slice_rows + EXTRA, nstate), BF16),
            pltpu.VMEM((group, slice_rows, nstate), BF16),
        ],
    )
    return backs


def scan_out(me, cumulated, returned, keep, got, reverse):
    mine, send = call(
        functools.partial(core_kernel, reverse),
        [struct(keep.shape, BF16)] * 2,
        [me, cumulated, keep, got] + list(returned),
        keep.size,
        smem=(0,),
        scratch=[pltpu.VMEM(keep.shape, BF16)],
    )
    return mine, crossed(send, 1)


def body(
    queries,
    keys,
    values,
    d_out,
    mixer_input,
    gate_input,
    state_write,
    state_read,
    log_decay,
    norm_gain,
    project_weight,
):
    ctx_size = lax.axis_size("ctx")
    ctx_index = lax.axis_index("ctx")
    rows, head_dim = keys.shape
    wide = queries.shape[1]
    channels = mixer_input.shape[1]
    nstate = state_write.shape[1]
    mheads = log_decay.shape[1]
    per = rows // ctx_size
    me = ctx_index.astype(jnp.int32).reshape(1)
    packed = jnp.pad(keys, ((0, 0), (0, head_dim))) + jnp.pad(values, ((0, 0), (head_dim, 0)))
    near_plane = [packed] + [crossed(packed, k) for k in range(4, ctx_size, 4)]
    (plane,) = call(
        plane_kernel,
        [struct((ctx_size // 4, rows, 2 * head_dim), BF16)],
        near_plane,
        rows * head_dim,
    )
    plane_other = crossed(plane, 1)
    half_states = [
        struct((channels // 2, nstate), BF16),
        struct((channels // 2 + EXTRA, nstate), BF16),
    ]
    tile = tile_of(rows)
    columns = tile * wide // head_dim
    stacked = struct((rows // tile, columns, head_dim), BF16)
    keep, give, scaled, remain, grow, cumulated, turned = call(
        state_kernel,
        [
            *half_states,
            struct((rows, channels), BF16),
            struct((rows, channels), F32),
            struct((rows, channels), F32),
            struct((rows, mheads), F32),
            struct((mheads, rows), F32),
        ],
        [me, mixer_input, state_write, tied(log_decay.T, packed)],
        2 * rows * channels * nstate,
        smem=(0,),
    )

    query_tiles, grad_tiles = call(
        stack_kernel, [stacked, stacked], [queries, d_out], rows * wide
    )
    slices, got = scan_slices(me, cumulated, keep, tied(give, plane), False)
    parts = scan_parts(slices)
    across = crossed(plane, 2)
    across_other = crossed(tied(across, (tuple(parts[1:]), query_tiles)), 1)

    total = scan_total(me, cumulated, keep, parts, False)
    carry = scan_carry(total, False)
    query_tiles = tied(query_tiles, total)

    in_kernel = per % 8 == 0
    flops = 10 * rows * wide * ctx_size * rows
    scratch = [
        pltpu.VMEM((ctx_size, rows, 2 * head_dim), BF16),
        pltpu.VMEM((ctx_size, rows, 2 * head_dim), F32),
        pltpu.VMEM((2, rows // tile, ctx_size * tile, columns), F32),
        pltpu.VMEM((2, rows // tile, ctx_size * tile, columns), F32),
    ]
    attention_args = [me, query_tiles, grad_tiles, plane, plane_other, across, across_other]
    chips = ctx_size // 2
    extra = per * wide // (2 * head_dim)
    if in_kernel:
        part = struct((chips, rows + extra, 2 * head_dim), BF16)
        kv_keep, kv_give = call(
            functools.partial(attention_kernel, True, ctx_size),
            [part, part],
            attention_args,
            flops,
            smem=(0,),
            scratch=scratch + [pltpu.VMEM((ctx_size, extra, 2 * head_dim), F32)],
        )
    else:
        query_grad, kv_grad = call(
            functools.partial(attention_kernel, False, ctx_size),
            [struct((rows, wide), BF16), struct((ctx_size, rows, 2 * head_dim), BF16)],
            attention_args,
            flops,
            smem=(0,),
            scratch=scratch,
        )
        by_target = kv_grad.reshape(ctx_size, ctx_size, per, 2 * head_dim).transpose(1, 0, 2, 3)
        by_pair = query_grad.reshape(ctx_size, per, -1, 2 * head_dim).transpose(0, 2, 1, 3)
        sent = jnp.concatenate(
            [
                by_target.reshape(ctx_size, rows, 2 * head_dim),
                by_pair.reshape(ctx_size, extra, 2 * head_dim),
            ],
            axis=1,
        ).reshape(chips, 2, rows + extra, 2 * head_dim)
        kv_keep = lax.dynamic_index_in_dim(sent, ctx_index % 2, 1, False)
        kv_give = lax.dynamic_index_in_dim(sent, 1 - ctx_index % 2, 1, False)

    carry, kv_keep, kv_give = lax.optimization_barrier((carry, kv_keep, kv_give))
    kv_got = crossed(kv_give, 1)
    backs = scan_back(me, cumulated, carry, keep, parts, False)
    sent = call(
        join_kernel,
        [struct((rows + 2 * extra, 2 * head_dim), BF16)] * chips,
        [me, kv_keep, tied(kv_got, backs[0])],
        chips * rows * 2 * head_dim,
        smem=(0,),
    )
    order = sorted(range(chips), key=lambda k: (-(k // 4), k % 2, -k))
    received = [crossed(sent[k], 2 * k) if k else sent[k] for k in order]
    returned = tied(tuple(scan_parts(backs)), tuple(received[:2]))
    incoming, incoming_other = scan_out(me, cumulated, returned, keep, got, False)

    both_states = pltpu.VMEM((2, channels // 2, nstate), BF16)
    whole = struct((rows, channels), F32)
    gated, inverse, active, slope = call(
        mixer_kernel,
        [whole, struct((rows, 128), F32), whole, whole],
        [
            me,
            mixer_input,
            state_write,
            state_read,
            cumulated,
            turned,
            grow,
            gate_input,
            incoming,
            incoming_other,
        ],
        2 * rows * channels * (nstate + rows),
        smem=(0,),
        scratch=[both_states, pltpu.VMEM((rows, channels), F32)],
    )
    gated_grad, out_grad, adjoint_keep, adjoint_give, grown = call(
        functools.partial(gate_kernel, order),
        [
            struct((rows, channels), F32),
            struct((rows, channels), BF16),
            *half_states,
            struct((rows, channels), BF16),
        ],
        [
            me,
            project_weight,
            gated,
            inverse,
            active,
            norm_gain.reshape(1, channels),
            state_read,
            grow,
            cumulated,
        ]
        + received,
        2 * rows * channels * (nstate + project_weight.shape[1]),
        smem=(0,),
    )
    value_part, write_part, read_gradient, gate_gradient = call(
        local_kernel,
        [
            struct((rows, channels), F32),
            struct((rows, nstate), F32),
            struct((rows, nstate), F32),
            whole,
        ],
        [
            me,
            out_grad,
            grown,
            mixer_input,
            state_write,
            state_read,
            cumulated,
            turned,
            incoming,
            incoming_other,
            gated_grad,
            slope,
        ],
        2 * rows * channels * (nstate + 2 * rows),
        smem=(0,),
        scratch=[both_states],
    )
    slices, got = scan_slices(me, cumulated, adjoint_keep, adjoint_give, True)
    parts = scan_parts(slices)
    carry = scan_carry(scan_total(me, cumulated, adjoint_keep, parts, True), True)
    carry = tied(carry, write_part)
    backs = scan_back(me, cumulated, carry, adjoint_keep, parts, True)
    adjoint, adjoint_other = scan_out(
        me, cumulated, scan_parts(backs), adjoint_keep, got, True
    )
    half_out, write_half = call(
        half_kernel,
        [struct((rows, channels // 2), F32), struct((rows, nstate), F32)],
        [me, scaled, remain, state_write, adjoint],
        2 * rows * channels * nstate,
        smem=(0,),
    )
    input_gradient, write_gradient = call(
        final_kernel,
        [whole, struct((rows, nstate), F32)],
        [
            me,
            value_part,
            write_part,
            half_out,
            write_half,
            scaled,
            remain,
            state_write,
            adjoint_other,
        ],
        2 * rows * channels * nstate,
        smem=(0,),
    )
    return (input_gradient, gate_gradient, write_gradient, read_gradient)


def solution(mesh):
    both = P("ctx", "groups")
    return jax.shard_map(
        body,
        mesh=mesh,
        in_specs=(both,) * 9 + (P("groups"), P(None, "groups")),
        out_specs=(both,) * 4,
        check_vma=False,
    )
```

```python
import functools
import math

import jax
import jax.numpy as jnp
from jax import lax
from jax.experimental import pallas as pl
from jax.experimental.pallas import tpu as pltpu
from jax.sharding import PartitionSpec as P

EPSILON = 1e-05
HIGHEST = lax.Precision.HIGHEST
F32 = jnp.float32
BF16 = jnp.bfloat16
EXTRA = 16
MIB = 1024 * 1024


def nn(a, b, **kw):
    return lax.dot_general(a, b, (((1,), (0,)), ((), ())), preferred_element_type=F32, **kw)


def nt(a, b, **kw):
    return lax.dot_general(a, b, (((1,), (1,)), ((), ())), preferred_element_type=F32, **kw)


def tn(a, b, **kw):
    return lax.dot_general(a, b, (((0,), (0,)), ((), ())), preferred_element_type=F32, **kw)


def iota(shape, dim):
    return lax.broadcasted_iota(jnp.int32, shape, dim)


def call(kernel, outs, args, flops, smem=(), scratch=(), spare=4 * MIB):
    specs = [
        pl.BlockSpec(memory_space=pltpu.SMEM if i in smem else pltpu.VMEM) for i in range(len(args))
    ]
    moved = sum(a.size * a.dtype.itemsize for a in args) + sum(
        math.prod(o.shape) * o.dtype.itemsize for o in outs
    )
    held = moved + sum(
        math.prod(s.shape) * jnp.dtype(s.dtype).itemsize for s in scratch
    )
    return pl.pallas_call(
        kernel,
        out_shape=tuple(outs),
        in_specs=specs,
        out_specs=tuple(pl.BlockSpec(memory_space=pltpu.VMEM) for _ in outs),
        scratch_shapes=list(scratch),
        compiler_params=pltpu.CompilerParams(vmem_limit_bytes=held + spare),
        cost_estimate=pl.CostEstimate(flops=flops, bytes_accessed=moved, transcendentals=0),
    )(*args)


def struct(shape, dtype):
    return jax.ShapeDtypeStruct(shape, dtype)


def running_sums(log_decay):
    rows = log_decay.shape[1]
    lower = (iota((rows, rows), 0) >= iota((rows, rows), 1)).astype(F32)
    upper = (iota((rows, rows), 0) <= iota((rows, rows), 1)).astype(F32)
    return nt(lower, log_decay, precision=HIGHEST), nn(log_decay, upper, precision=HIGHEST)


def spread_heads(per_head, mdim):
    rows, heads = per_head.shape
    first = iota((rows, 2 * mdim), 1) < mdim
    pairs = [
        jnp.where(first, per_head[:, h : h + 1], per_head[:, h + 1 : h + 2])
        for h in range(0, heads, 2)
    ]
    return jnp.concatenate(pairs, axis=1)


def split_pair(block, mdim):
    first = iota(block.shape, 1) < mdim
    zero = jnp.zeros_like(block)
    return jnp.concatenate([jnp.where(first, block, zero), jnp.where(first, zero, block)], axis=0)


def plane_kernel(*refs):
    *piece_refs, out_ref = refs
    for i, piece_ref in enumerate(piece_refs):
        out_ref[i] = piece_ref[...]


def tile_of(rows):
    return min(32, rows)


def stack_kernel(*refs):
    count = len(refs) // 2
    for ref, out_ref in zip(refs[:count], refs[count:]):
        tiles, wide, head_dim = out_ref.shape
        tile = ref.shape[0] // tiles
        for t in range(tiles):
            for h in range(wide // tile):
                out_ref[t, h * tile : (h + 1) * tile, :] = ref[
                    t * tile : (t + 1) * tile, h * head_dim : (h + 1) * head_dim
                ]


def put_logs(ref, logs):
    heads = logs.shape[1]
    high = logs.astype(BF16).astype(F32)
    middle = (logs - high).astype(BF16).astype(F32)
    low = (logs - high - middle).astype(BF16).astype(F32)
    place = iota((EXTRA, heads), 0)
    split = jnp.where(place == 0, high, jnp.where(place == 1, middle, low))
    wide = jnp.concatenate([split, jnp.zeros((EXTRA, ref.shape[1] - heads), F32)], axis=1)
    ref[ref.shape[0] - EXTRA :, :] = wide.astype(BF16)


def get_logs(ref, heads):
    parts = ref[ref.shape[0] - EXTRA :, 0:heads].astype(F32)
    return parts[0:1, :] + parts[1:2, :] + parts[2:3, :]


def times(logs, start, mdim, state):
    head = iota(logs.shape, 1)
    blocks = []
    for i in range(state.shape[0] // mdim):
        log = jnp.sum(jnp.where(head == start + i, logs, 0.0), axis=1, keepdims=True)
        blocks.append(jnp.exp(log) * state[i * mdim : (i + 1) * mdim, :])
    return jnp.concatenate(blocks, axis=0)


def write_halves(core, logs, scaled_ref, other_ref, keep_ref, give_ref):
    half = keep_ref.shape[0]
    for out_ref, which in ((keep_ref, core), (give_ref, 1 - core)):
        lanes = pl.ds(pl.multiple_of(which * half, half), half)
        out_ref[0:half, :] = tn(scaled_ref[:, lanes], other_ref[...]).astype(BF16)
    put_logs(give_ref, logs)


def state_kernel(
    me_ref,
    input_ref,
    write_ref,
    decay_ref,
    keep_ref,
    give_ref,
    scaled_ref,
    remain_ref,
    grow_ref,
    sum_ref,
    turned_ref,
):
    cumulated, turned = running_sums(decay_ref[...])
    sum_ref[...], turned_ref[...] = cumulated, turned
    mdim = input_ref.shape[1] // cumulated.shape[1]
    last = cumulated[-1:, :]
    remain_ref[...] = spread_heads(jnp.exp(last - cumulated), mdim)
    grow_ref[...] = spread_heads(jnp.exp(cumulated), mdim)
    scaled_ref[...] = (input_ref[...].astype(F32) * remain_ref[...]).astype(BF16)
    write_halves(me_ref[0] % 2, last, scaled_ref, write_ref, keep_ref, give_ref)


def chip_kernel(reverse, me_ref, sum_ref, keep_ref, got_ref, *rest):
    *out_refs, total_ref = rest
    heads = sum_ref.shape[1]
    half = keep_ref.shape[0]
    mdim = 2 * half // heads
    core = me_ref[0] % 2
    chip = me_ref[0] // 2 % len(out_refs)
    slice_rows = out_refs[0].shape[0] - EXTRA
    own_logs = sum_ref[sum_ref.shape[0] - 1 :, :]
    got_logs = get_logs(got_ref, heads)
    keep, got = keep_ref[...].astype(F32), got_ref[0:half, :].astype(F32)
    first = core == (1 if reverse else 0)
    decayed = times(jnp.where(first, got_logs, own_logs), core * heads // 2, mdim, jnp.where(first, keep, got))
    total_ref[...] = decayed + jnp.where(first, got, keep)
    for k, out_ref in enumerate(out_refs):
        start = pl.multiple_of((chip ^ k) * slice_rows, slice_rows)
        out_ref[0:slice_rows, :] = total_ref[pl.ds(start, slice_rows), :].astype(BF16)
        put_logs(out_ref, own_logs + got_logs)


def steps(count, reverse):
    return range(count - 1, -1, -1) if reverse else range(count)


def ordered(chip, part_refs, order_ref):
    for k, part_ref in enumerate(part_refs):
        order_ref[chip ^ k] = part_ref[...]


def advance(order_ref, source, start, heads, mdim, state):
    part_ref = order_ref.at[source]
    rows = state.shape[0]
    return times(get_logs(part_ref, heads), start, mdim, state) + part_ref[0:rows, :].astype(F32)


def total_kernel(reverse, heads, mdim, me_ref, *rest):
    *part_refs, out_ref, order_ref = rest
    count = len(part_refs)
    chip = me_ref[0] // 2 % count
    ordered(chip, part_refs, order_ref)
    start = me_ref[0] % 2 * (heads // 2) + chip * (heads // 2 // count)
    state = jnp.zeros(out_ref.shape, F32)
    for source in steps(count, reverse):
        state = advance(order_ref, source, start, heads, mdim, state)
    out_ref[...] = state.astype(BF16)


def scan_kernel(reverse, heads, mdim, me_ref, carry_ref, *rest):
    *refs, order_ref, result_ref = rest
    count = len(refs) // 2
    chip = me_ref[0] // 2 % count
    ordered(chip, refs[:count], order_ref)
    start = me_ref[0] % 2 * (heads // 2) + chip * (heads // 2 // count)
    state = carry_ref[...].astype(F32)
    for source in steps(count, reverse):
        result_ref[source] = state.astype(BF16)
        state = advance(order_ref, source, start, heads, mdim, state)
    for k, out_ref in enumerate(refs[count:]):
        out_ref[...] = result_ref[chip ^ k]


def core_kernel(reverse, me_ref, sum_ref, keep_ref, got_ref, *rest):
    *part_refs, mine_ref, send_ref, order_ref = rest
    count = len(part_refs)
    heads = sum_ref.shape[1]
    half = keep_ref.shape[0]
    core = me_ref[0] % 2
    chip = me_ref[0] // 2 % count
    slice_rows = part_refs[0].shape[0]
    for k, part_ref in enumerate(part_refs):
        start = pl.multiple_of((chip ^ k) * slice_rows, slice_rows)
        order_ref[pl.ds(start, slice_rows), :] = part_ref[...]
    first = core == (1 if reverse else 0)
    logs = jnp.where(first, sum_ref[sum_ref.shape[0] - 1 :, :], get_logs(got_ref, heads))
    own = jnp.where(first, keep_ref[...].astype(F32), got_ref[0:half, :].astype(F32))
    incoming = order_ref[...].astype(F32)
    passed = times(logs, core * heads // 2, 2 * half // heads, incoming) + own
    mine_ref[...] = jnp.where(first, incoming, passed).astype(BF16)
    send_ref[...] = jnp.where(first, passed, incoming).astype(BF16)


def whole_state(me_ref, mine_ref, other_ref, both_ref):
    core = me_ref[0] % 2
    both_ref[core] = mine_ref[...]
    both_ref[1 - core] = other_ref[...]
    _, half, nstate = both_ref.shape
    return both_ref[...].reshape(2 * half, nstate)


def mixer_kernel(
    me_ref,
    input_ref,
    write_ref,
    read_ref,
    sum_ref,
    turned_ref,
    grow_ref,
    gate_ref,
    mine_ref,
    other_ref,
    gated_ref,
    inverse_ref,
    active_ref,
    slope_ref,
    both_ref,
    out_ref,
):
    rows, channels = input_ref.shape
    mheads = sum_ref.shape[1]
    mdim = channels // mheads
    cumulated, turned = sum_ref[...], turned_ref[...]
    carried = nt(read_ref[...], whole_state(me_ref, mine_ref, other_ref, both_ref))
    out_ref[...] = grow_ref[...] * carried
    products = nt(read_ref[...], write_ref[...])
    causal = iota((rows, rows), 0) >= iota((rows, rows), 1)

    def weights_of(head):
        spread = cumulated[:, head : head + 1] - turned[head : head + 1, :]
        return (jnp.exp(jnp.where(causal, spread, -jnp.inf)) * products).astype(BF16)

    for pair in range(mheads // 2):
        lanes = slice(pair * 2 * mdim, (pair + 1) * 2 * mdim)
        weights = jnp.concatenate([weights_of(2 * pair), weights_of(2 * pair + 1)], axis=1)
        out_ref[:, lanes] += nn(weights, split_pair(input_ref[:, lanes], mdim))

    mixer_out = out_ref[...]
    gate = gate_ref[...].astype(F32)
    sigmoid = jax.nn.sigmoid(gate)
    active = gate * sigmoid
    gated = mixer_out * active
    active_ref[...] = active
    gated_ref[...] = gated
    slope_ref[...] = mixer_out * sigmoid * (1.0 + gate * (1.0 - sigmoid))
    inverse = lax.rsqrt(jnp.mean(gated * gated, axis=-1, keepdims=True) + EPSILON)
    inverse_ref[...] = jnp.broadcast_to(inverse, inverse_ref.shape)


def attention_kernel(
    in_kernel, ctx_size, me_ref, query_ref, grad_ref, *rest
):
    plane_refs, rest = rest[:4], rest[4:]
    if in_kernel:
        keep_ref, give_ref, gathered_ref, acc_ref, raw_ref, back_ref, query_acc_ref = rest
    else:
        query_out_ref, pack_ref, gathered_ref, acc_ref, raw_ref, back_ref = rest
    tiles, wide, head_dim = query_ref.shape
    rows = gathered_ref.shape[1]
    tile = rows // tiles
    heads = wide // tile
    me = me_ref[0]
    scale = 1.0 / math.sqrt(head_dim)
    base2 = scale * math.log2(math.e)
    per = rows // ctx_size
    for offset, plane_ref in enumerate(plane_refs):
        for level in range(ctx_size // 4):
            gathered_ref[me ^ (4 * level + offset)] = plane_ref[level]

    def keys_of(b):
        return gathered_ref[:, b * tile : (b + 1) * tile, 0:head_dim].reshape(
            ctx_size * tile, head_dim
        )

    def values_of(b):
        return gathered_ref[:, b * tile : (b + 1) * tile, head_dim : 2 * head_dim].reshape(
            ctx_size * tile, head_dim
        )

    key_row = iota((ctx_size * tile, wide), 0)
    key_place = (key_row % tile) * ctx_size + key_row // tile
    query_place = (iota((ctx_size * tile, wide), 1) % tile) * ctx_size + me
    visible = key_place <= query_place

    def score(t):
        slot = t % 2
        query = query_ref[t]
        highest = None
        for b in range(t, -1, -1):
            raw = nt(keys_of(b), query)
            if b == t:
                raw = jnp.where(visible, raw, -jnp.inf)
            raw_ref[slot, b] = raw
            block_high = jnp.max(raw, axis=0, keepdims=True)
            highest = block_high if highest is None else jnp.maximum(highest, block_high)
        return highest

    def weigh(t, highest):
        slot = t % 2
        grad = grad_ref[t]
        total = jnp.zeros((1, wide), F32)
        delta = jnp.zeros((1, wide), F32)
        for b in range(t + 1):
            probs = jnp.exp2((raw_ref[slot, b] - highest) * base2)
            back = nt(values_of(b), grad)
            raw_ref[slot, b] = probs
            back_ref[slot, b] = back
            total = total + jnp.sum(probs, axis=0, keepdims=True)
            delta = delta + jnp.sum(probs * back, axis=0, keepdims=True)
        inverse = 1.0 / total
        return inverse, delta * inverse

    def gather(t, inverse, delta):
        slot = t % 2
        query, grad = query_ref[t], grad_ref[t]
        query_grad = jnp.zeros((head_dim, wide), F32)
        for b in range(t + 1):
            weights = raw_ref[slot, b] * inverse
            score_grad = (weights * (back_ref[slot, b] - delta)).astype(BF16)
            value_part = nn(weights.astype(BF16), grad).reshape(ctx_size, tile, head_dim)
            key_part = nn(score_grad, query).reshape(ctx_size, tile, head_dim)
            here = slice(b * tile, (b + 1) * tile)
            if t == tiles - 1:
                acc_ref[:, here, 0:head_dim] = key_part
                acc_ref[:, here, head_dim:] = value_part
            else:
                acc_ref[:, here, 0:head_dim] += key_part
                acc_ref[:, here, head_dim:] += value_part
            query_grad = query_grad + tn(keys_of(b), score_grad)
        turned = (query_grad * scale).T
        by_head = [turned[h * tile : (h + 1) * tile, :] for h in range(heads)]
        if in_kernel:
            pairs = [
                jnp.concatenate(by_head[h : h + 2], axis=1) for h in range(0, heads, 2)
            ]
            for k in range(tile // per):
                rows_here = [p[k * per : (k + 1) * per, :] for p in pairs]
                query_acc_ref[t * (tile // per) + k] = jnp.concatenate(rows_here, axis=0)
        else:
            for h in range(heads):
                query_out_ref[t * tile : (t + 1) * tile, h * head_dim : (h + 1) * head_dim] = (
                    by_head[h].astype(BF16)
                )

    last = tiles - 1
    state = weigh(last, score(last))
    for t in range(last, -1, -1):
        if t:
            highest = score(t - 1)
        gather(t, *state)
        if t:
            state = weigh(t - 1, highest)

    both = jnp.where(iota((1, 1, 2 * head_dim), 2) < head_dim, scale, 1.0)
    if in_kernel:
        for chip in range(ctx_size // 2):
            for out_ref, core in ((keep_ref, me % 2), (give_ref, 1 - me % 2)):
                target = 2 * chip + core
                start = pl.multiple_of(target * per, per)
                block = acc_ref[:, pl.ds(start, per), :] * both
                out_ref[chip, 0:rows, :] = block.reshape(rows, 2 * head_dim).astype(BF16)
                out_ref[chip, rows:, :] = query_acc_ref[target].astype(BF16)
    else:
        pack_ref[...] = (acc_ref[...] * both).astype(BF16)


def join_kernel(me_ref, keep_ref, got_ref, *out_refs):
    mid = keep_ref.shape[1]
    rows = 2 * mid - out_refs[0].shape[0]
    chip = me_ref[0] // 2
    for k, out_ref in enumerate(out_refs):
        target = chip ^ k
        both = keep_ref[target, 0:rows, :].astype(F32) + got_ref[target, 0:rows, :].astype(F32)
        out_ref[0:rows, :] = both.astype(BF16)
        out_ref[rows:mid, :] = keep_ref[target, rows:, :]
        out_ref[mid:, :] = got_ref[target, rows:, :]


def in_token_order(ctx_size, devices, grads):
    rows = grads.shape[0]
    per = rows // ctx_size
    token, came = iota((rows, rows), 0), iota((rows, rows), 1)
    order = (token == (came % per) * ctx_size + devices(came // per)).astype(BF16)
    return nn(order, grads).astype(BF16)


def gate_kernel(
    order,
    me_ref,
    weight_ref,
    gated_ref,
    inverse_ref,
    active_ref,
    gain_ref,
    read_ref,
    grow_ref,
    sum_ref,
    *rest,
):
    *part_refs, gated_grad_ref, grad_out_ref, keep_ref, give_ref, grown_ref = rest
    rows = gated_ref.shape[0]
    chips = len(part_refs)
    ctx_size = 2 * chips
    per = rows // ctx_size
    part_refs = [part_refs[order.index(k)] for k in range(chips)]
    me = me_ref[0]
    sums = part_refs[0][0:rows, :].astype(F32)
    for part_ref in part_refs[1:]:
        sums = sums + part_ref[0:rows, :].astype(F32)
    kv_grads = in_token_order(ctx_size, lambda place: place, sums.astype(BF16))
    extra = (part_refs[0].shape[0] - rows) // 2
    query_rows = [part_ref[rows:, :].astype(F32) for part_ref in part_refs]
    columns = []
    for part in range(extra // per):
        blocks = [
            block[core * extra + part * per : core * extra + (part + 1) * per, :]
            for core in range(2)
            for block in query_rows
        ]
        columns.append(jnp.concatenate(blocks, axis=0))
    query_grads = in_token_order(
        ctx_size,
        lambda place: (2 * (place % chips) + place // chips) ^ me,
        jnp.concatenate(columns, axis=1).astype(BF16),
    )
    grads = jnp.concatenate([query_grads, kv_grads], axis=1)
    mixer_grad = nt(grads, weight_ref[...]).astype(BF16).astype(F32)

    gated = gated_ref[...]
    inverse = inverse_ref[:, 0:1]
    scaled = gain_ref[...] * mixer_grad
    mean = jnp.mean(scaled * gated, axis=-1, keepdims=True)
    gated_grad = scaled * inverse - gated * (mean * inverse * inverse * inverse)
    gated_grad_ref[...] = gated_grad
    out_grad = (gated_grad * active_ref[...]).astype(BF16)
    grad_out_ref[...] = out_grad
    grown_ref[...] = (out_grad.astype(F32) * grow_ref[...]).astype(BF16)
    last = sum_ref[rows - 1 :, :]
    write_halves(me % 2, last, grown_ref, read_ref, keep_ref, give_ref)


def local_kernel(
    me_ref,
    grad_ref,
    grown_ref,
    input_ref,
    write_ref,
    read_ref,
    sum_ref,
    turned_ref,
    mine_ref,
    other_ref,
    gated_grad_ref,
    slope_ref,
    value_ref,
    write_out_ref,
    read_out_ref,
    gate_out_ref,
    both_ref,
):
    rows, channels = input_ref.shape
    mheads = sum_ref.shape[1]
    mdim = channels // mheads
    gate_out_ref[...] = gated_grad_ref[...] * slope_ref[...]
    cumulated, turned = sum_ref[...], turned_ref[...]
    turned_products = nt(write_ref[...], read_ref[...])
    causal = iota((rows, rows), 0) >= iota((rows, rows), 1)
    later = iota((rows, rows), 0) <= iota((rows, rows), 1)
    pair_sum = jnp.zeros((rows, rows), F32)

    def decays_of(head):
        spread = cumulated[:, head : head + 1] - turned[head : head + 1, :]
        return jnp.exp(jnp.where(causal, spread, -jnp.inf))

    def turned_weights_of(head):
        spread = turned[head : head + 1, :] - cumulated[:, head : head + 1]
        return (jnp.exp(jnp.where(later, spread, -jnp.inf)) * turned_products).astype(BF16)

    for pair in range(mheads // 2):
        lanes = slice(pair * 2 * mdim, (pair + 1) * 2 * mdim)
        grads = split_pair(grad_ref[:, lanes], mdim)
        weights = jnp.concatenate(
            [turned_weights_of(2 * pair), turned_weights_of(2 * pair + 1)], axis=1
        )
        value_ref[:, lanes] = nn(weights, grads)
        pairs = nt(grads, input_ref[:, lanes])
        pair_sum = (
            pair_sum + decays_of(2 * pair) * pairs[:rows] + decays_of(2 * pair + 1) * pairs[rows:]
        )
    pair_low = pair_sum.astype(BF16)
    incoming = whole_state(me_ref, mine_ref, other_ref, both_ref)
    read_out_ref[...] = nn(pair_low, write_ref[...]) + nn(grown_ref[...], incoming)
    write_out_ref[...] = tn(pair_low, read_ref[...])


def half_of(which, half):
    return pl.ds(pl.multiple_of(which * half, half), half)


def half_kernel(me_ref, scaled_ref, remain_ref, write_ref, mine_ref, half_ref, write_half_ref):
    lanes = half_of(me_ref[0] % 2, mine_ref.shape[0])
    half_ref[...] = remain_ref[:, lanes] * nt(write_ref[...], mine_ref[...])
    write_half_ref[...] = nn(scaled_ref[:, lanes], mine_ref[...])


def final_kernel(
    me_ref,
    value_ref,
    write_part_ref,
    half_ref,
    write_half_ref,
    scaled_ref,
    remain_ref,
    write_ref,
    other_ref,
    out_ref,
    write_out_ref,
):
    core = me_ref[0] % 2
    half = other_ref.shape[0]
    lanes = half_of(core, half)
    out_ref[:, lanes] = value_ref[:, lanes] + half_ref[...]
    lanes = half_of(1 - core, half)
    out_ref[:, lanes] = value_ref[:, lanes] + remain_ref[:, lanes] * nt(write_ref[...], other_ref[...])
    write_out_ref[...] = (
        write_part_ref[...] + write_half_ref[...] + nn(scaled_ref[:, lanes], other_ref[...])
    )


def crossed(array, bits):
    pairs = [(i, i ^ bits) for i in range(lax.axis_size("ctx"))]
    return lax.ppermute(array, "ctx", pairs)


def tied(arrays, after):
    return lax.optimization_barrier((arrays, after))[0]


def scan_slices(me, cumulated, keep, give, reverse):
    group = lax.axis_size("ctx") // 4
    half_rows, nstate = keep.shape
    got = crossed(give, 1)
    slices = call(
        functools.partial(chip_kernel, reverse),
        [struct((half_rows // group + EXTRA, nstate), BF16)] * group,
        [me, cumulated, keep, got],
        half_rows * nstate,
        smem=(0,),
        scratch=[pltpu.VMEM((half_rows, nstate), F32)],
    )
    return slices, got


def scan_parts(slices):
    return [slices[0]] + [crossed(slices[k], 2 * k) for k in range(1, len(slices))]


def scan_total(me, cumulated, keep, parts, reverse):
    group = len(parts)
    half_rows, nstate = keep.shape
    slice_rows = half_rows // group
    heads = cumulated.shape[1]
    (total,) = call(
        functools.partial(total_kernel, reverse, heads, 2 * half_rows // heads),
        [struct((slice_rows, nstate), BF16)],
        [me] + list(parts),
        half_rows * nstate,
        smem=(0,),
        scratch=[pltpu.VMEM((group, slice_rows + EXTRA, nstate), BF16)],
    )
    return total


def scan_carry(total, reverse):
    half = lax.axis_size("ctx") // 2
    if reverse:
        pairs = [(i + half, i) for i in range(half)]
    else:
        pairs = [(i, i + half) for i in range(half)]
    return lax.ppermute(total, "ctx", pairs)


def scan_back(me, cumulated, carry, keep, parts, reverse):
    group = len(parts)
    slice_rows, nstate = carry.shape
    heads = cumulated.shape[1]
    backs = call(
        functools.partial(scan_kernel, reverse, heads, 2 * keep.shape[0] // heads),
        [struct(carry.shape, BF16)] * group,
        [me, carry] + list(parts),
        group * slice_rows * nstate,
        smem=(0,),
        scratch=[
            pltpu.VMEM((group, slice_rows + EXTRA, nstate), BF16),
            pltpu.VMEM((group, slice_rows, nstate), BF16),
        ],
    )
    return backs


def scan_out(me, cumulated, returned, keep, got, reverse):
    mine, send = call(
        functools.partial(core_kernel, reverse),
        [struct(keep.shape, BF16)] * 2,
        [me, cumulated, keep, got] + list(returned),
        keep.size,
        smem=(0,),
        scratch=[pltpu.VMEM(keep.shape, BF16)],
    )
    return mine, crossed(send, 1)


def body(
    queries,
    keys,
    values,
    d_out,
    mixer_input,
    gate_input,
    state_write,
    state_read,
    log_decay,
    norm_gain,
    project_weight,
):
    ctx_size = lax.axis_size("ctx")
    ctx_index = lax.axis_index("ctx")
    rows, head_dim = keys.shape
    wide = queries.shape[1]
    channels = mixer_input.shape[1]
    nstate = state_write.shape[1]
    mheads = log_decay.shape[1]
    per = rows // ctx_size
    me = ctx_index.astype(jnp.int32).reshape(1)
    packed = jnp.pad(keys, ((0, 0), (0, head_dim))) + jnp.pad(values, ((0, 0), (head_dim, 0)))
    near_plane = [packed] + [crossed(packed, k) for k in range(4, ctx_size, 4)]
    (plane,) = call(
        plane_kernel,
        [struct((ctx_size // 4, rows, 2 * head_dim), BF16)],
        near_plane,
        rows * head_dim,
    )
    plane_other = crossed(plane, 1)
    half_states = [
        struct((channels // 2, nstate), BF16),
        struct((channels // 2 + EXTRA, nstate), BF16),
    ]
    tile = tile_of(rows)
    columns = tile * wide // head_dim
    stacked = struct((rows // tile, columns, head_dim), BF16)
    keep, give, scaled, remain, grow, cumulated, turned = call(
        state_kernel,
        [
            *half_states,
            struct((rows, channels), BF16),
            struct((rows, channels), F32),
            struct((rows, channels), F32),
            struct((rows, mheads), F32),
            struct((mheads, rows), F32),
        ],
        [me, mixer_input, state_write, tied(log_decay.T, packed)],
        2 * rows * channels * nstate,
        smem=(0,),
    )

    query_tiles, grad_tiles = call(
        stack_kernel, [stacked, stacked], [queries, d_out], rows * wide
    )
    slices, got = scan_slices(me, cumulated, keep, tied(give, plane), False)
    parts = scan_parts(slices)
    across = crossed(plane, 2)
    across_other = crossed(tied(across, (tuple(parts[1:]), query_tiles)), 1)

    query_tiles = tied(query_tiles, tuple(parts))

    in_kernel = per % 8 == 0
    flops = 10 * rows * wide * ctx_size * rows
    scratch = [
        pltpu.VMEM((ctx_size, rows, 2 * head_dim), BF16),
        pltpu.VMEM((ctx_size, rows, 2 * head_dim), F32),
        pltpu.VMEM((2, rows // tile, ctx_size * tile, columns), F32),
        pltpu.VMEM((2, rows // tile, ctx_size * tile, columns), F32),
    ]
    attention_args = [me, query_tiles, grad_tiles, plane, plane_other, across, across_other]
    chips = ctx_size // 2
    extra = per * wide // (2 * head_dim)
    if in_kernel:
        part = struct((chips, rows + extra, 2 * head_dim), BF16)
        kv_keep, kv_give = call(
            functools.partial(attention_kernel, True, ctx_size),
            [part, part],
            attention_args,
            flops,
            smem=(0,),
            scratch=scratch + [pltpu.VMEM((ctx_size, extra, 2 * head_dim), F32)],
        )
    else:
        query_grad, kv_grad = call(
            functools.partial(attention_kernel, False, ctx_size),
            [struct((rows, wide), BF16), struct((ctx_size, rows, 2 * head_dim), BF16)],
            attention_args,
            flops,
            smem=(0,),
            scratch=scratch,
        )
        by_target = kv_grad.reshape(ctx_size, ctx_size, per, 2 * head_dim).transpose(1, 0, 2, 3)
        by_pair = query_grad.reshape(ctx_size, per, -1, 2 * head_dim).transpose(0, 2, 1, 3)
        sent = jnp.concatenate(
            [
                by_target.reshape(ctx_size, rows, 2 * head_dim),
                by_pair.reshape(ctx_size, extra, 2 * head_dim),
            ],
            axis=1,
        ).reshape(chips, 2, rows + extra, 2 * head_dim)
        kv_keep = lax.dynamic_index_in_dim(sent, ctx_index % 2, 1, False)
        kv_give = lax.dynamic_index_in_dim(sent, 1 - ctx_index % 2, 1, False)

    carry = scan_carry(scan_total(me, cumulated, keep, tied(tuple(parts), kv_keep), False), False)
    kv_got = crossed(kv_give, 1)
    sent = call(
        join_kernel,
        [struct((rows + 2 * extra, 2 * head_dim), BF16)] * chips,
        [me, kv_keep, kv_got],
        chips * rows * 2 * head_dim,
        smem=(0,),
    )
    backs = scan_back(me, cumulated, tied(carry, sent[0]), keep, parts, False)
    order = sorted(range(chips), key=lambda k: (-(k // 4), k % 2, -k))
    received = [crossed(sent[k], 2 * k) if k else sent[k] for k in order]
    returned = tied(tuple(scan_parts(backs)), tuple(received[:3]))
    incoming, incoming_other = scan_out(me, cumulated, returned, keep, got, False)

    both_states = pltpu.VMEM((2, channels // 2, nstate), BF16)
    whole = struct((rows, channels), F32)
    gated, inverse, active, slope = call(
        mixer_kernel,
        [whole, struct((rows, 128), F32), whole, whole],
        [
            me,
            mixer_input,
            state_write,
            state_read,
            cumulated,
            turned,
            grow,
            gate_input,
            incoming,
            incoming_other,
        ],
        2 * rows * channels * (nstate + rows),
        smem=(0,),
        scratch=[both_states, pltpu.VMEM((rows, channels), F32)],
    )
    gated_grad, out_grad, adjoint_keep, adjoint_give, grown = call(
        functools.partial(gate_kernel, order),
        [
            struct((rows, channels), F32),
            struct((rows, channels), BF16),
            *half_states,
            struct((rows, channels), BF16),
        ],
        [
            me,
            project_weight,
            gated,
            inverse,
            active,
            norm_gain.reshape(1, channels),
            state_read,
            grow,
            cumulated,
        ]
        + received,
        2 * rows * channels * (nstate + project_weight.shape[1]),
        smem=(0,),
    )
    value_part, write_part, read_gradient, gate_gradient = call(
        local_kernel,
        [
            struct((rows, channels), F32),
            struct((rows, nstate), F32),
            struct((rows, nstate), F32),
            whole,
        ],
        [
            me,
            out_grad,
            grown,
            mixer_input,
            state_write,
            state_read,
            cumulated,
            turned,
            incoming,
            incoming_other,
            gated_grad,
            slope,
        ],
        2 * rows * channels * (nstate + 2 * rows),
        smem=(0,),
        scratch=[both_states],
    )
    slices, got = scan_slices(me, cumulated, adjoint_keep, adjoint_give, True)
    parts = scan_parts(slices)
    carry = scan_carry(scan_total(me, cumulated, adjoint_keep, parts, True), True)
    carry = tied(carry, write_part)
    backs = scan_back(me, cumulated, carry, adjoint_keep, parts, True)
    adjoint, adjoint_other = scan_out(
        me, cumulated, scan_parts(backs), adjoint_keep, got, True
    )
    half_out, write_half = call(
        half_kernel,
        [struct((rows, channels // 2), F32), struct((rows, nstate), F32)],
        [me, scaled, remain, state_write, adjoint],
        2 * rows * channels * nstate,
        smem=(0,),
    )
    input_gradient, write_gradient = call(
        final_kernel,
        [whole, struct((rows, nstate), F32)],
        [
            me,
            value_part,
            write_part,
            half_out,
            write_half,
            scaled,
            remain,
            state_write,
            adjoint_other,
        ],
        2 * rows * channels * nstate,
        smem=(0,),
    )
    return (input_gradient, gate_gradient, write_gradient, read_gradient)


def solution(mesh):
    both = P("ctx", "groups")
    return jax.shard_map(
        body,
        mesh=mesh,
        in_specs=(both,) * 9 + (P("groups"), P(None, "groups")),
        out_specs=(both,) * 4,
        check_vma=False,
    )
```
